32 devices in a mesh: dp: 8 (over z, x), section: 4 (over y, core).
Axes of the slice: x: 2, y: 2, z: 4, core: 2. Of those that a mesh axis runs over, the one named last changes fastest.
Arguments:
- tokens: bfloat16 [24576, 768], P(('dp', 'section')), may hold values from -6 to 6
- counts: int32 [16, 3], P('dp'), may hold values from 1 to 8, 12 in all within a row
- attn_weight: bfloat16 [2, 768, 3072], replicated
- attn_bias: bfloat16 [2, 3, 768], replicated, may hold values from -3 to 3
- attn_norm: bfloat16 [2, 2, 768], replicated
- mlp_weight: bfloat16 [2, 2, 768, 3072], replicated
- mlp_bias: bfloat16 [2, 3072], replicated, may hold values from -3 to 3
- mlp_small: bfloat16 [2, 3, 768], replicated
- seg_embed: bfloat16 [8, 768], replicated, may hold values from -3 to 3
- cotangent: bfloat16 [24576, 768], P(('dp', 'section')), may hold values from -6 to 6
Outputs:
- encoded: bfloat16 [24576, 768], P(('dp', 'section'))
- input_grad: bfloat16 [24576, 768], P(('dp', 'section'))
- grad_attn_weight: float32 [2, 768, 3072], P(None, None, ('dp', 'section'))
- grad_attn_bias: float32 [2, 3, 768], replicated
- grad_attn_norm: float32 [2, 2, 768], replicated
- grad_mlp_weight: float32 [2, 2, 768, 3072], P(None, None, None, ('dp', 'section'))
- grad_mlp_bias: float32 [2, 3072], replicated
- grad_mlp_small: float32 [2, 3, 768], replicated
- grad_seg_embed: float32 [8, 768], replicated
The draws below stay inside these ranges and needn't reach their ends.
Inputs may be any that keep to these rules, and one draw needn't show every extreme that they name: Each row holds the segment counts of the 3 documents of one micro-batch in order; they sum to 12 and one is exactly 8.
All inputs are finite; a program needn't handle non-finite values.
Results may differ from the reference program's by a relative error of at most 0.018.
Values may be sent and summed in bfloat16 or wider, within the bound.
A program may use at most 256 MiB of HBM per device.

```python
import math
import jax
import jax.numpy as jnp
import numpy as np
from jax import lax

D = 768
HEAD = 64
FF = 3072
SEG = 128
MICRO = 2
SEGS = 12
MOSTSEG = 8
DOCS = 3
TOKENS = 24576
N_DP = 8


def draw_attn_weight(key, part):
    key = jax.random.fold_in(key, 11)
    column = jnp.arange(4 * D)
    factor = jnp.where(column < 3 * D, D ** (-0.5), (D / 8.0) ** (-0.5))
    raw_values = jnp.clip(jax.random.normal(key, (2, D, 4 * D), jnp.float32), -6.0, 6.0)
    return (raw_values * factor).astype(jnp.bfloat16)


def draw_attn_norm(key, part):
    key = jax.random.fold_in(key, 12)
    gain_key, shift_key = jax.random.split(key)
    gain_row = jax.random.uniform(gain_key, (2, 1, D), jnp.float32, 0.6, 1.4)
    shift_row = 0.3 * jnp.clip(jax.random.normal(shift_key, (2, 1, D), jnp.float32), -3.0, 3.0)
    return jnp.concatenate([gain_row, shift_row], axis=1).astype(jnp.bfloat16)


def draw_mlp_weight(key, part):
    key = jax.random.fold_in(key, 13)
    factor = jnp.array([D ** (-0.5), FF ** (-0.5)], jnp.float32).reshape(1, 2, 1, 1)
    raw_values = jnp.clip(jax.random.normal(key, (2, 2, D, FF), jnp.float32), -6.0, 6.0)
    return (raw_values * factor).astype(jnp.bfloat16)


def draw_mlp_small(key, part):
    key = jax.random.fold_in(key, 14)
    bias_key, gain_key, shift_key = jax.random.split(key, 3)
    bias_row = 0.3 * jnp.clip(jax.random.normal(bias_key, (2, 1, D), jnp.float32), -3.0, 3.0)
    gain_row = jax.random.uniform(gain_key, (2, 1, D), jnp.float32, 0.6, 1.4)
    shift_row = 0.3 * jnp.clip(jax.random.normal(shift_key, (2, 1, D), jnp.float32), -3.0, 3.0)
    return jnp.concatenate([bias_row, gain_row, shift_row], axis=1).astype(jnp.bfloat16)


def strengthened(drawn, own_key, source, target, parts, factor):
    def block_of(dim):
        return (jnp.arange(drawn.shape[dim]) // (drawn.shape[dim] // parts)).reshape((-1,) + (1,) * (drawn.ndim - 1 - dim))

    one_side = jax.random.permutation(own_key, parts)[block_of(target)]
    second = (block_of(target) + parts // 2) % parts
    return jnp.where((block_of(source) == one_side) | (block_of(source) == second), factor * drawn, drawn)


def shard_levels(rng, dims, shards, low, largest):
    def one(position, shards_of):
        draws = jax.random.uniform(jax.random.fold_in(jax.random.fold_in(rng, 6), position), (shards_of,), jnp.float32, low / len(shards), largest / len(shards))
        return jnp.repeat(jnp.exp(draws), dims[position] // shards_of).reshape((-1,) + (1,) * (len(dims) - position - 1))

    loudness = one(*shards[0])
    for cut in shards[1:]:
        loudness = loudness * one(*cut)
    return loudness


def split_up(number_of, total, limit, slope):
    portions = [(1 << 20) // math.isqrt(rank ** slope) + 1 for rank in range(2, number_of + 1)]
    rest, given = total - limit - (number_of - 1), [1] * (number_of - 1)
    while rest > 0:
        movable = [i for i in range(number_of - 1) if given[i] < limit]
        pool, remaining = sum([portions[i] for i in movable]), rest
        for i in movable:
            extra = min(limit - given[i], max(1, remaining * portions[i] // pool), rest)
            given[i] = given[i] + extra
            rest = rest - extra
    return np.array([limit] + given)


def uneven_parts(stream_key, amount, total, limit, skew):
    if amount == 2:
        one = jax.random.randint(stream_key, (), max(1, total - limit), min(limit, total - 1) + 1)
        return jnp.stack([one, total - one])
    lengths = jnp.asarray(split_up(amount, total, limit, skew), jnp.int32)
    pairs = (amount - 1) // 2
    source_of, sink = lengths[1:1 + 2 * pairs:2], lengths[2:2 + 2 * pairs:2]
    room = jnp.minimum(source_of - 1, limit - sink)
    moved = jax.random.randint(jax.random.fold_in(stream_key, 1), (pairs,), 0, 1 << 20) % (room + 1)
    lengths = lengths.at[1:1 + 2 * pairs:2].set(source_of - moved).at[2:2 + 2 * pairs:2].set(sink + moved)
    return lengths[jax.random.permutation(jax.random.fold_in(stream_key, 2), amount)]


def noise(rng, shape, scale, reach, cuts=(), held_as=jnp.bfloat16):
    result = jax.random.normal(rng, shape, jnp.float32) * scale
    if len(cuts) > 0:
        result = shard_levels(rng, shape, cuts, -0.22, 0.18) * result
    return jnp.clip(result, min=-reach, max=reach).astype(held_as)


def gaussian_with(own_key, extent, scale, reach, pieces, heavy, held_as=jnp.bfloat16):
    entries = scale * jax.random.normal(own_key, extent, jnp.float32)
    if pieces:
        entries = entries * shard_levels(own_key, extent, pieces, -0.22, 0.18)
    return jnp.clip(strengthened(entries, jax.random.fold_in(own_key, 3), *heavy), -reach, reach).astype(held_as)


def setup_inputs(seed: int = 0) -> dict:
    arg_keys = jax.random.split(jax.random.key(seed), 11)
    tokens = noise(arg_keys[0], (TOKENS, D), 1.0, 6.0, ((0, 32),))
    counts = jax.vmap(lambda own: uneven_parts(own, DOCS, SEGS, MOSTSEG, 2))(jax.random.split(arg_keys[1], (N_DP * MICRO))).reshape((N_DP * MICRO, DOCS)).astype(jnp.int32)
    attn_weight = draw_attn_weight(jax.random.fold_in(arg_keys[10], 71), 0)
    attn_bias = noise(arg_keys[3], (2, 3, D), 0.5, 3.0)
    attn_norm = draw_attn_norm(jax.random.fold_in(arg_keys[10], 71), 0)
    mlp_weight = draw_mlp_weight(jax.random.fold_in(arg_keys[10], 71), 0)
    mlp_bias = noise(arg_keys[6], (2, FF), 0.5, 3.0)
    mlp_small = draw_mlp_small(jax.random.fold_in(arg_keys[10], 71), 0)
    seg_embed = noise(arg_keys[8], (MOSTSEG, D), 0.5, 3.0)
    cotangent = gaussian_with(arg_keys[9], (TOKENS, D), 1.0, 6.0, ((0, 32),), (0, 1, 32, 2.75))
    return dict(tokens=tokens, counts=counts, attn_weight=attn_weight, attn_bias=attn_bias, attn_norm=attn_norm, mlp_weight=mlp_weight, mlp_bias=mlp_bias, mlp_small=mlp_small, seg_embed=seg_embed, cotangent=cotangent)


@jax.custom_vjp
def low(v):
    return lax.optimization_barrier(v.astype(jnp.bfloat16)).astype(jnp.float32)

@jax.custom_vjp
def low_back(v):
    return v

def low_keep(v):
    return (low(v), None)

def low_pass(kept, grad):
    return (grad,)

def back_keep(v):
    return (v, None)

def back_low(kept, grad):
    return (low(grad),)
low.defvjp(low_keep, low_pass)
low_back.defvjp(back_keep, back_low)
HIGHEST = lax.Precision.HIGHEST
masked_score = -1e+30

def layer_norm(residual, gain_vec, shift_vec):
    center = residual - lax.optimization_barrier(jnp.mean(residual, axis=-1, keepdims=True))
    spread = lax.optimization_barrier(jnp.mean(center * center, axis=-1, keepdims=True))
    return center * lax.rsqrt(spread + 1e-05) * gain_vec + shift_vec

def doc_layout(seg_counts):
    doc_ends = jnp.cumsum(seg_counts).astype(jnp.int32)
    doc_starts = (doc_ends - seg_counts).astype(jnp.int32)
    seg_index = jnp.arange(SEGS, dtype=jnp.int32)
    doc_ids = lax.optimization_barrier(jnp.sum((seg_index[:, None] >= doc_ends[None, :]).astype(jnp.int32), axis=1)).astype(jnp.int32)
    doc_index = jnp.arange(DOCS, dtype=jnp.int32)
    own_start = lax.optimization_barrier(jnp.sum(jnp.where(doc_ids[:, None] == doc_index[None, :], doc_starts[None, :], 0), axis=1)).astype(jnp.int32)
    return (doc_ids, (seg_index - own_start).astype(jnp.int32))

def attend(inputs, weight, offset, norm_pair, length, allowed):
    row_count, model_width = inputs.shape
    head_count = model_width // HEAD
    factor = HEAD ** (-0.5)
    rounded = low(inputs)
    zeros_k = jnp.zeros_like(offset[0])
    project = jnp.dot(rounded, weight[:, :3 * model_width], precision=HIGHEST)
    project = project + jnp.concatenate([offset[0], zeros_k, offset[1]])
    qkv_all = low(low_back(project)).reshape(row_count // length, length, 3, head_count, HEAD)
    scores = jnp.einsum('gqhd,gkhd->ghqk', qkv_all[:, :, 0], qkv_all[:, :, 1], precision=HIGHEST) * factor
    scores = low_back(jnp.where(allowed, scores, masked_score))
    probs_low = low(jax.nn.softmax(scores, axis=-1))
    context = jnp.einsum('ghqk,gkhd->gqhd', probs_low, qkv_all[:, :, 2], precision=HIGHEST)
    context = low(low_back(context.reshape(row_count, model_width)))
    branch = low_back(jnp.dot(context, weight[:, 3 * model_width:], precision=HIGHEST) + offset[2])
    return layer_norm(inputs + branch, norm_pair[0], norm_pair[1])

def feed_forward(inputs, weight_in, weight_out, offset_in, small_vecs):
    hidden = low_back(jnp.dot(inputs, weight_in, precision=HIGHEST) + offset_in)
    active = low(jax.nn.gelu(hidden, approximate=False))
    branch = low_back(jnp.dot(active, weight_out.T, precision=HIGHEST) + small_vecs[0])
    return layer_norm(inputs + branch, small_vecs[1], small_vecs[2])

def micro_batch(params, inputs, seg_counts):
    attn_w, attn_b, attn_n, mlp_w, mlp_b, mlp_s, embed = params
    first_out = low(low_back(attend(inputs, attn_w[0], attn_b[0], attn_n[0], SEG, True)))
    second = low(low_back(feed_forward(first_out, mlp_w[0, 0], mlp_w[0, 1], mlp_b[0], mlp_s[0])))
    grouped = second.reshape(SEGS, SEG, -1)
    doc_ids, seg_pos = doc_layout(seg_counts)
    leaders = grouped[:, 0] + embed[seg_pos]
    allowed = doc_ids[:, None] == doc_ids[None, :]
    third_out = low(low_back(attend(leaders, attn_w[1], attn_b[1], attn_n[1], SEGS, allowed)))
    fourth = feed_forward(third_out, mlp_w[1, 0], mlp_w[1, 1], mlp_b[1], mlp_s[1])
    return grouped.at[:, 0].set(fourth).reshape(SEGS * SEG, -1)

def reference(tokens, counts, attn_weight, attn_bias, attn_norm, mlp_weight, mlp_bias, mlp_small, seg_embed, cotangent):
    params = tuple((weight.astype(jnp.float32) for weight in (attn_weight, attn_bias, attn_norm, mlp_weight, mlp_bias, mlp_small, seg_embed)))
    groups = tokens.astype(jnp.float32).reshape(-1, SEGS * SEG, tokens.shape[1])

    def forward(groups_in, *weights):

        def scan_step(carry_in, block_in):
            return (carry_in, micro_batch(weights, block_in[0], block_in[1]))
        _, outputs = lax.scan(jax.checkpoint(scan_step), None, (groups_in, counts))
        return outputs
    outputs, pull_back = jax.vjp(forward, groups, *params)
    gradients = pull_back(cotangent.astype(jnp.float32).reshape(groups.shape))
    encoded = outputs.reshape(-1, tokens.shape[1]).astype(jnp.bfloat16)
    input_grad = gradients[0].reshape(-1, tokens.shape[1]).astype(jnp.bfloat16)
    return (encoded, input_grad, gradients[1], gradients[2], gradients[3], gradients[4], gradients[5], gradients[6], gradients[7])
```

```python
import functools

import jax
import jax.numpy as jnp
from jax import lax
from jax.experimental import pallas as pl
from jax.experimental.pallas import tpu as pltpu
from jax.sharding import PartitionSpec as P

F32 = jnp.float32
BF = jnp.bfloat16
D = 768
FF = 3072
SEG = 128
HEAD = 64
HEADS = 12
PAIRS = 6
MICRO = 2
SEGS = 12
OWN = 6
ROWS = OWN * SEG
BOTH = ("dp", "section")
MASKED = -1e30
VM = pl.BlockSpec(memory_space=pltpu.VMEM)
SM = pl.BlockSpec(memory_space=pltpu.SMEM)
ANY = pl.BlockSpec(memory_space=pl.ANY)


def dot(a, b):
    return jnp.dot(a, b, preferred_element_type=F32)


def dot_nt(a, b):
    return lax.dot_general(a, b, (((1,), (1,)), ((), ())), preferred_element_type=F32)


def dot_tn(a, b):
    return lax.dot_general(a, b, (((0,), (0,)), ((), ())), preferred_element_type=F32)


def gelu_parts(h):
    e = jnp.exp(-0.5 * h * h)
    t = 1.0 / (1.0 + (0.3275911 * 0.7071067811865476) * jnp.abs(h))
    poly = t * (
        0.127414796
        + t * (-0.142248368 + t * (0.7107068705 + t * (-0.7265760135 + t * 0.5307027145)))
    )
    tail = poly * e
    phi = jnp.where(h >= 0.0, 1.0 - tail, tail)
    return h * phi, phi + h * (0.3989422804014327 * e)


def norm_rows(r):
    center = r - jnp.mean(r, axis=-1, keepdims=True)
    rstd = lax.rsqrt(jnp.mean(center * center, axis=-1, keepdims=True) + 1e-5)
    return center * rstd, rstd


def norm_back(dy, n, rstd, gain):
    dyg = dy * gain
    return (
        dyg
        - jnp.mean(dyg, axis=-1, keepdims=True)
        - n * jnp.mean(dyg * n, axis=-1, keepdims=True)
    ) * rstd


def halves(v):
    lane = lax.broadcasted_iota(jnp.int32, v.shape, 1)
    zero = jnp.zeros_like(v)
    return jnp.concatenate([jnp.where(lane < HEAD, v, zero), jnp.where(lane < HEAD, zero, v)], 0)


def unhalve(v):
    top, bottom = v[:SEG], v[SEG:]
    lane = lax.broadcasted_iota(jnp.int32, top.shape, 1)
    return jnp.where(lane < HEAD, top, bottom)


def fold8(v):
    return jnp.sum(v.reshape(v.shape[0] // 8, 8, v.shape[1]), axis=0)


def row(ref, *idx):
    i = idx[-1]
    return ref[idx[:-1] + (slice(i, i + 1), slice(None))].astype(F32)


class Copies:
    def __init__(self, sems):
        self.sems, self.all = sems, []

    def start(self, src, dst):
        copy = pltpu.make_async_copy(src, dst, self.sems.at[len(self.all)])
        copy.start()
        self.all.append(copy)
        return copy


def fwd_kernel(
    x_ref, aw, ab, an, mw, mb, ms,
    second_o, first_o, n1_o, rs1_o, n2_o, rs2_o, qkv_o, p_o, ctx_o, act_o, gp_o, cls_o,
    wq, w1, w2, second, first, n1, rs1, n2, rs2, qkv, p, ctx, act, gp, r, wsem, osem,
):
    outs, loads = Copies(osem), Copies(wsem)
    for j in range(4):
        s = slice(j * D, (j + 1) * D)
        loads.start(aw.at[0, :, s], wq.at[:, s])
    loads.start(mw.at[0, 0], w1)
    loads.start(mw.at[0, 1], w2)
    loads = loads.all
    x = x_ref[...]
    for j in range(3):
        loads[j].wait()
        s = slice(j * D, (j + 1) * D)
        v = dot(x, wq[:, s])
        if j != 1:
            v = v + row(ab, 0, j // 2)
        qkv[:, s] = v.astype(BF)
    outs.start(qkv, qkv_o)

    @pl.loop(0, OWN)
    def _(g):
        rows = pl.ds(pl.multiple_of(g * SEG, SEG), SEG)
        for h in range(PAIRS):
            c = slice(h * 128, (h + 1) * 128)
            q = qkv[rows, c] * jnp.asarray(0.125, BF)
            kc = halves(qkv[rows, D + h * 128 : D + (h + 1) * 128])
            vc = halves(qkv[rows, 2 * D + h * 128 : 2 * D + (h + 1) * 128])
            s = dot_nt(q, kc)
            ps = []
            for i in range(2):
                si = s[:, i * 128 : (i + 1) * 128]
                e = jnp.exp(si - jnp.max(si, axis=-1, keepdims=True))
                ps.append((e / jnp.sum(e, axis=-1, keepdims=True)).astype(BF))
            pp = jnp.concatenate(ps, axis=1)
            p[pl.ds(pl.multiple_of(g * ROWS + h * SEG, SEG), SEG), :] = pp
            ctx[rows, c] = dot(pp, vc).astype(BF)

    outs.start(p, p_o)
    outs.start(ctx, ctx_o)
    loads[3].wait()
    r[...] = x.astype(F32) + dot(ctx[...], wq[:, 3 * D :]) + row(ab, 0, 2)

    @pl.loop(0, ROWS // 64)
    def _(i):
        rows = pl.ds(pl.multiple_of(i * 64, 64), 64)
        n, rs = norm_rows(r[rows, :])
        n1[rows, :] = n.astype(BF)
        rs1[rows, :] = rs
        first[rows, :] = (n * row(an, 0, 0) + row(an, 0, 1)).astype(BF)

    outs.start(n1, n1_o)
    outs.start(rs1, rs1_o)
    outs.start(first, first_o)
    loads[4].wait()
    for j in range(4):
        s = slice(j * D, (j + 1) * D)
        r[...] = dot(first[...], w1[:, s]) + mb[0:1, s].astype(F32)

        @pl.loop(0, ROWS // 32)
        def _(i):
            rows = pl.ds(pl.multiple_of(i * 32, 32), 32)
            a, g = gelu_parts(r[rows, :])
            act[rows, s] = a.astype(BF)
            gp[rows, s] = g.astype(BF)

    outs.start(act, act_o)
    outs.start(gp, gp_o)
    loads[5].wait()
    r[...] = first[...].astype(F32) + dot_nt(act[...], w2[...]) + row(ms, 0, 0)
    cls_o[...] = jnp.zeros_like(cls_o)

    @pl.loop(0, OWN)
    def _(g):
        for part in range(2):
            rows = pl.ds(pl.multiple_of(g * SEG + part * 64, 64), 64)
            n, rs = norm_rows(r[rows, :])
            n2[rows, :] = n.astype(BF)
            rs2[rows, :] = rs
            value = (n * row(ms, 0, 1) + row(ms, 0, 2)).astype(BF)
            second[rows, :] = value
            if part == 0:
                cls_o[pl.ds(g, 1), :] = value[0:1].astype(F32)

    outs.start(n2, n2_o)
    outs.start(rs2, rs2_o)
    outs.start(second, second_o)
    for copy in outs.all:
        copy.wait()


def forward(x, aw, ab, an, mw, mb, ms):
    def big(width, dt=BF):
        return ((ROWS, width), dt)

    specs = [big(D), big(D), big(D), big(1, F32), big(D), big(1, F32), big(3 * D)]
    specs += [((OWN * ROWS, 256), BF), big(D), big(FF), big(FF)]
    shapes = [jax.ShapeDtypeStruct(*s) for s in specs] + [jax.ShapeDtypeStruct((8, D), F32)]
    return pl.pallas_call(
        fwd_kernel,
        out_shape=shapes,
        in_specs=[VM, ANY, VM, VM, ANY, VM, VM],
        out_specs=[ANY] * len(specs) + [VM],
        scratch_shapes=[pltpu.VMEM((D, FF), BF)] * 3
        + [pltpu.VMEM(*s) for s in specs]
        + [
            pltpu.VMEM((ROWS, D), F32),
            pltpu.SemaphoreType.DMA((6,)),
            pltpu.SemaphoreType.DMA((len(specs),)),
        ],
        compiler_params=pltpu.CompilerParams(vmem_limit_bytes=56 * 2**20),
    )(x, aw, ab, an, mw, mb, ms)


def cls_kernel(
    own_ref, other_ref, cown_ref, cother_ref, counts, aw, ab, an, mw, mb, ms, embed,
    fourth_o, dlead_o, cols_o, wide_o, small_o,
    wq, w1, w2, wsem,
):
    loads = Copies(wsem)
    loads.start(aw.at[1], wq)
    loads.start(mw.at[1, 0], w1)
    loads.start(mw.at[1, 1], w2)
    loads = loads.all
    section = lax.axis_index("section")
    per_micro = lax.axis_size("section") // MICRO
    half = lax.rem(section, per_micro)
    micro = section // per_micro
    ends = [counts[micro, 0], counts[micro, 0] + counts[micro, 1]]

    def layout(shape, axis):
        r = lax.broadcasted_iota(jnp.int32, shape, axis)
        seg = jnp.where(r < 8, r, r - 2)
        valid = (r < 6) | ((r >= 8) & (r < 14))
        doc = jnp.where(seg >= ends[0], 1, 0) + jnp.where(seg >= ends[1], 1, 0)
        start = jnp.where(doc == 0, 0, jnp.where(doc == 1, ends[0], ends[1]))
        pos = jnp.where(valid, seg - start, -1)
        return jnp.where(valid, doc, jnp.where(r < 16, 100 + r, -1)), pos, valid

    def order(a_ref, b_ref):
        a, b = a_ref[...], b_ref[...]
        first = half == 0
        return jnp.concatenate([jnp.where(first, a, b), jnp.where(first, b, a)], axis=0)

    def mine(v):
        return jnp.where(half == 0, v[:8], v[8:])

    doc_q, pos, valid = layout((16, 128), 0)
    doc_k, _, _ = layout((16, 128), 1)
    allowed = jnp.concatenate([doc_q == doc_k] * HEADS, axis=0)
    lanes8 = lax.broadcasted_iota(jnp.int32, (16, 8), 1)
    onehot = (pos[:, :8] == lanes8).astype(BF)
    leaders = order(own_ref, other_ref) + dot(onehot, embed[...])
    low = leaders.astype(BF)
    lane = lax.broadcasted_iota(jnp.int32, (16, D), 1) // HEAD

    def stack(v):
        return jnp.concatenate([jnp.where(lane == h, v, jnp.zeros_like(v)) for h in range(HEADS)], 0)

    def unstack(v):
        total = jnp.where(lane == 0, v[:16], 0.0)
        for h in range(1, HEADS):
            total = total + jnp.where(lane == h, v[h * 16 : (h + 1) * 16], 0.0)
        return total

    def deep(v):
        return jnp.concatenate([v, jnp.zeros((112, D), BF)], axis=0)

    loads[0].wait()
    q = (dot(low, wq[:, :D]) + row(ab, 1, 0)).astype(BF)
    k = dot(low, wq[:, D : 2 * D]).astype(BF)
    v = (dot(low, wq[:, 2 * D : 3 * D]) + row(ab, 1, 1)).astype(BF)
    qs, kd, vd = stack(q), deep(k), deep(v)
    scores = jnp.where(allowed, dot_nt(qs, kd) * 0.125, MASKED)
    e = jnp.exp(scores - jnp.max(scores, axis=-1, keepdims=True))
    probs = e / jnp.sum(e, axis=-1, keepdims=True)
    probs_low = probs.astype(BF)
    ctx = unstack(dot(probs_low, vd)).astype(BF)
    n1, rs1 = norm_rows(leaders + dot(ctx, wq[:, 3 * D :]) + row(ab, 1, 2))
    third = (n1 * row(an, 1, 0) + row(an, 1, 1)).astype(BF)
    loads[1].wait()
    act, gp = gelu_parts(dot(third, w1[...]) + mb[1:2, :].astype(F32))
    act = act.astype(BF)
    loads[2].wait()
    n2, rs2 = norm_rows(third.astype(F32) + dot_nt(act, w2[...]) + row(ms, 1, 0))
    fourth_o[...] = mine(n2 * row(ms, 1, 1) + row(ms, 1, 2))

    dy = order(cown_ref, cother_ref)
    small_o[10:11, :] = jnp.sum(mine(dy * n2), axis=0, keepdims=True)
    small_o[11:12, :] = jnp.sum(mine(dy), axis=0, keepdims=True)
    dr = norm_back(dy, n2, rs2, row(ms, 1, 1))
    dbf = dr.astype(BF)
    small_o[9:10, :] = jnp.sum(mine(dbf.astype(F32)), axis=0, keepdims=True)
    dh = (dot(dbf, w2[...]) * gp).astype(BF)
    dh_mine = mine(dh.astype(F32))
    dh_sum = jnp.sum(dh_mine, axis=0, keepdims=True)
    for j in range(4):
        small_o[5 + j : 6 + j, :] = dh_sum[:, j * D : (j + 1) * D]
    dthird = (dr + dot_nt(dh, w1[...])).astype(BF).astype(F32)
    small_o[3:4, :] = jnp.sum(mine(dthird * n1), axis=0, keepdims=True)
    small_o[4:5, :] = jnp.sum(mine(dthird), axis=0, keepdims=True)
    dr = norm_back(dthird, n1, rs1, row(an, 1, 0))
    dba = dr.astype(BF)
    small_o[2:3, :] = jnp.sum(mine(dba.astype(F32)), axis=0, keepdims=True)
    dctx = stack(dot_nt(dba, wq[:, 3 * D :]).astype(BF))
    dp = dot_nt(dctx, vd)
    dv = dot_tn(probs_low, dctx)[:16].astype(BF)
    ds = (probs * (dp - jnp.sum(dp * probs, axis=-1, keepdims=True))).astype(BF)
    dq = (unstack(dot(ds, kd)) * 0.125).astype(BF)
    dk = (dot_tn(ds, qs)[:16] * 0.125).astype(BF)
    small_o[0:1, :] = jnp.sum(mine(dq.astype(F32)), axis=0, keepdims=True)
    small_o[1:2, :] = jnp.sum(mine(dv.astype(F32)), axis=0, keepdims=True)
    dlead = dr + dot_nt(dq, wq[:, :D]) + dot_nt(dk, wq[:, D : 2 * D])
    dlead = dlead + dot_nt(dv, wq[:, 2 * D : 3 * D])
    dlead_mine = mine(dlead)
    dlead_o[...] = dlead_mine
    pos_mine = jnp.where(half == 0, pos[:8], pos[8:])
    for i in range(8):
        hit = jnp.where(pos_mine[:, 0:1] == i, dlead_mine, 0.0)
        small_o[12 + i : 13 + i, :] = jnp.sum(hit, axis=0, keepdims=True)
    for j, piece in enumerate((dq, dk, dv, dba)):
        cols_o[0, :, j * D : (j + 1) * D] = mine(piece.astype(F32)).astype(BF)
    cols_o[1] = dh_mine.astype(BF)
    cols_o[2] = mine(act.astype(F32)).astype(BF)
    for j, piece in enumerate((low, ctx, third, dbf)):
        wide_o[j] = mine(piece.astype(F32)).astype(BF)


def cls_chain(own, other, cown, cother, counts, aw, ab, an, mw, mb, ms, embed):
    shapes = [((8, D), F32), ((8, D), F32), ((3, 8, FF), BF), ((4, 8, D), BF), ((20, D), F32)]
    return pl.pallas_call(
        cls_kernel,
        out_shape=[jax.ShapeDtypeStruct(*s) for s in shapes],
        in_specs=[VM, VM, VM, VM, SM, ANY, VM, VM, ANY, VM, VM, VM],
        out_specs=[VM] * 5,
        scratch_shapes=[pltpu.VMEM((D, FF), BF)] * 3 + [pltpu.SemaphoreType.DMA((3,))],
        compiler_params=pltpu.CompilerParams(vmem_limit_bytes=56 * 2**20),
    )(own, other, cown, cother, counts, aw, ab, an, mw, mb, ms, embed)


def bwd_kernel(
    cot, dlead, x, n1_i, rs1_i, n2_i, rs2_i, first_i, qkv_i, p_i, ctx_i, act_i, gp_i,
    aw, an, mw, ms,
    dx_o, dw_o, small_o,
    wq, w1, w2, first, n1, rs1, n2, rs2, qkv, p, ctx, act, gp,
    r, db, dqkv, dctx, dw, sums, wsem, osem,
):
    loads = Copies(wsem)
    for src, dst in (
        (n2_i, n2), (rs2_i, rs2), (act_i, act), (mw.at[0, 1], w2), (gp_i, gp), (first_i, first),
        (mw.at[0, 0], w1), (n1_i, n1), (rs1_i, rs1), (ctx_i, ctx), (aw.at[0], wq), (qkv_i, qkv), (p_i, p),
    ):
        loads.start(src, dst)
    loads = loads.all
    pending = [None, None]
    count = [0]

    def put(value, which, start):
        slot = count[0] % 2
        if pending[slot] is not None:
            pending[slot].wait()
        dw[slot] = value.astype(BF)
        copy = pltpu.make_async_copy(dw.at[slot], dw_o.at[which, start : start + D, :], osem.at[slot])
        copy.start()
        pending[slot] = copy
        count[0] += 1

    sums[...] = jnp.zeros_like(sums)

    def norm_step(rows, dy, n_ref, rs_ref, gain, at):
        n = n_ref[rows, :].astype(F32)
        dr = norm_back(dy, n, rs_ref[rows, :], gain)
        r[rows, :] = dr
        low = dr.astype(BF)
        db[rows, :] = low
        sums[at] += fold8(low.astype(F32))
        sums[at + 1] += fold8(dy * n)
        sums[at + 2] += fold8(dy)

    loads[0].wait()
    loads[1].wait()

    @pl.loop(0, OWN)
    def _(g):
        for part in range(2):
            rows = pl.ds(pl.multiple_of(g * SEG + part * 64, 64), 64)
            dy = cot[rows, :].astype(F32)
            if part == 0:
                cls = lax.broadcasted_iota(jnp.int32, (64, D), 0) == 0
                lead = dlead[pl.ds(g, 1), :].astype(BF).astype(F32)
                dy = jnp.where(cls, lead, dy)
            norm_step(rows, dy, n2, rs2, row(ms, 0, 1), 0)

    loads[2].wait()
    for j in range(4):
        put(dot_tn(act[:, j * D : (j + 1) * D], db[...]), 2, j * D)
    loads[3].wait()
    loads[4].wait()
    for j in range(4):
        s = slice(j * D, (j + 1) * D)
        low = (dot(db[...], w2[:, s]) * gp[:, s].astype(F32)).astype(BF)
        gp[:, s] = low
        sums[6 + j] = fold8(low.astype(F32))
    loads[5].wait()
    for j in range(4):
        put(dot_tn(gp[:, j * D : (j + 1) * D], first[...]), 1, j * D)
    loads[6].wait()
    r[...] += dot_nt(gp[...], w1[...])
    loads[7].wait()
    loads[8].wait()

    @pl.loop(0, ROWS // 64)
    def _(i):
        rows = pl.ds(pl.multiple_of(i * 64, 64), 64)
        dy = r[rows, :].astype(BF).astype(F32)
        norm_step(rows, dy, n1, rs1, row(an, 0, 0), 3)

    loads[9].wait()
    put(dot_tn(db[...], ctx[...]), 0, 3 * D)
    loads[10].wait()
    dctx[...] = dot_nt(db[...], wq[:, 3 * D :]).astype(BF)
    loads[11].wait()
    loads[12].wait()

    @pl.loop(0, OWN)
    def _(g):
        rows = pl.ds(pl.multiple_of(g * SEG, SEG), SEG)
        for h in range(PAIRS):
            cq = slice(h * 128, (h + 1) * 128)
            ck = slice(D + h * 128, D + (h + 1) * 128)
            cv = slice(2 * D + h * 128, 2 * D + (h + 1) * 128)
            q = qkv[rows, cq]
            kc, vc = halves(qkv[rows, ck]), halves(qkv[rows, cv])
            dc = dctx[rows, cq]
            pp = p[pl.ds(pl.multiple_of(g * ROWS + h * SEG, SEG), SEG), :]
            dp = dot_nt(dc, vc)
            pf = pp.astype(F32)
            ds = []
            for i in range(2):
                c = slice(i * 128, (i + 1) * 128)
                pi, di = pf[:, c], dp[:, c]
                ds.append((pi * (di - jnp.sum(di * pi, axis=-1, keepdims=True))).astype(BF))
            ds = jnp.concatenate(ds, axis=1)
            dqkv[rows, cq] = (dot(ds, kc) * 0.125).astype(BF)
            dqkv[rows, ck] = (unhalve(dot_tn(ds, q)) * 0.125).astype(BF)
            dqkv[rows, cv] = unhalve(dot_tn(pp, dc)).astype(BF)

    for j in range(3):
        s = slice(j * D, (j + 1) * D)
        put(dot_tn(dqkv[:, s], x[...]), 0, j * D)
        if j != 1:
            sums[10 + j // 2] = fold8(dqkv[:, s].astype(F32))
    dx_o[...] = (r[...] + dot_nt(dqkv[...], wq[:, : 3 * D])).astype(BF)
    for i, at in enumerate((10, 11, 3, 4, 5, 6, 7, 8, 9, 0, 1, 2)):
        small_o[i : i + 1, :] = jnp.sum(sums[at], axis=0, keepdims=True)
    for copy in pending:
        copy.wait()


def backward(cot, dlead, x, n1, rs1, n2, rs2, first, qkv, p, ctx, act, gp, aw, an, mw, ms):
    shapes = [((ROWS, D), BF), ((3, FF, D), BF), ((12, D), F32)]
    kept = (first, n1, rs1, n2, rs2, qkv, p, ctx, act, gp)
    return pl.pallas_call(
        bwd_kernel,
        out_shape=[jax.ShapeDtypeStruct(*s) for s in shapes],
        in_specs=[VM, VM, VM] + [ANY] * 11 + [VM, ANY, VM],
        out_specs=[VM, ANY, VM],
        scratch_shapes=[pltpu.VMEM((D, FF), BF)] * 3
        + [pltpu.VMEM(a.shape, a.dtype) for a in kept]
        + [
            pltpu.VMEM((ROWS, D), F32),
            pltpu.VMEM((ROWS, D), BF),
            pltpu.VMEM((ROWS, 3 * D), BF),
            pltpu.VMEM((ROWS, D), BF),
            pltpu.VMEM((2, D, D), BF),
            pltpu.VMEM((12, 8, D), F32),
            pltpu.SemaphoreType.DMA((13,)),
            pltpu.SemaphoreType.DMA((2,)),
        ],
        compiler_params=pltpu.CompilerParams(vmem_limit_bytes=60 * 2**20),
    )(cot, dlead, x, n1, rs1, n2, rs2, first, qkv, p, ctx, act, gp, aw, an, mw, ms)


def place_kernel(red, cols, wide, ga_o, gm_o):
    width = red.shape[1]
    me = lax.axis_index("dp") * lax.axis_size("section") + lax.axis_index("section")
    right = jnp.where(me * width >= 3 * D, wide[1].astype(F32), wide[0].astype(F32)).astype(BF)
    ga_o[0] = red[0].astype(F32).T
    gm_o[0, 0] = red[1].astype(F32).T
    gm_o[0, 1] = red[2].astype(F32).T
    ga_o[1] = dot_tn(right, cols[0])
    gm_o[1, 0] = dot_tn(wide[2], cols[1])
    gm_o[1, 1] = dot_tn(wide[3], cols[2])


def place(red, cols, wide):
    width = red.shape[1]
    return pl.pallas_call(
        place_kernel,
        out_shape=[
            jax.ShapeDtypeStruct((2, D, width), F32),
            jax.ShapeDtypeStruct((2, 2, D, width), F32),
        ],
        in_specs=[VM] * 3,
        out_specs=[VM] * 2,
        compiler_params=pltpu.CompilerParams(vmem_limit_bytes=56 * 2**20),
    )(red, cols, wide)


def swap_half(v):
    size = lax.axis_size("section")
    per_micro = size // MICRO
    return lax.ppermute(v, "section", [(i, i - i % per_micro + (i + 1) % per_micro) for i in range(size)])


def on_device(tokens, counts, aw, ab, an, mw, mb, ms, embed, cot):
    cls_cot = jnp.pad(cot.reshape(OWN, SEG, D)[:, 0].astype(F32), ((0, 2), (0, 0)))
    cls_cot_other = swap_half(cls_cot)
    second, first, n1, rs1, n2, rs2, qkv, p, ctx, act, gp, cls = forward(tokens, aw, ab, an, mw, mb, ms)
    fourth, dlead, cols, wide, small1 = cls_chain(
        cls, swap_half(cls), cls_cot, cls_cot_other, counts, aw, ab, an, mw, mb, ms, embed
    )
    cols = lax.all_to_all(cols, BOTH, split_axis=2, concat_axis=1, tiled=True)
    wide = lax.all_gather(wide, BOTH, axis=1, tiled=True)
    encoded = second.reshape(OWN, SEG, D).at[:, 0].set(fourth[:OWN].astype(BF)).reshape(ROWS, D)
    dx, dw, small0 = backward(
        cot, dlead, tokens, n1, rs1, n2, rs2, first, qkv, p, ctx, act, gp, aw, an, mw, ms
    )
    red = lax.psum_scatter(dw, BOTH, scatter_dimension=1, tiled=True)
    small = lax.psum(jnp.concatenate([small0, small1], axis=0), BOTH)
    ga, gm = place(red, cols, wide)
    return (
        encoded,
        dx,
        ga,
        jnp.stack([small[0:3], small[12:15]]),
        jnp.stack([small[3:5], small[15:17]]),
        gm,
        jnp.stack([small[5:9].reshape(FF), small[17:21].reshape(FF)]),
        jnp.stack([small[9:12], small[21:24]]),
        small[24:32],
    )


def solution(mesh):
    return jax.shard_map(
        on_device,
        mesh=mesh,
        in_specs=(P(BOTH, None), P("dp", None)) + (P(),) * 7 + (P(BOTH, None),),
        out_specs=(
            P(BOTH, None),
            P(BOTH, None),
            P(None, None, BOTH),
            P(),
            P(),
            P(None, None, None, BOTH),
            P(),
            P(),
            P(),
        ),
        check_vma=False,
    )
```

```python
import functools

import jax
import jax.numpy as jnp
from jax import lax
from jax.experimental import pallas as pl
from jax.experimental.pallas import tpu as pltpu
from jax.sharding import PartitionSpec as P

F32 = jnp.float32
BF = jnp.bfloat16
D = 768
FF = 3072
SEG = 128
HEAD = 64
HEADS = 12
PAIRS = 6
MICRO = 2
SEGS = 12
OWN = 6
ROWS = OWN * SEG
BOTH = ("dp", "section")
MASKED = -1e30
VM = pl.BlockSpec(memory_space=pltpu.VMEM)
SM = pl.BlockSpec(memory_space=pltpu.SMEM)
ANY = pl.BlockSpec(memory_space=pl.ANY)
MESH = pl.DeviceIdType.MESH


def dot(a, b):
    return jnp.dot(a, b, preferred_element_type=F32)


def dot_nt(a, b):
    return lax.dot_general(a, b, (((1,), (1,)), ((), ())), preferred_element_type=F32)


def dot_tn(a, b):
    return lax.dot_general(a, b, (((0,), (0,)), ((), ())), preferred_element_type=F32)


def gelu_parts(h):
    e = jnp.exp(-0.5 * h * h)
    t = 1.0 / (1.0 + (0.3275911 * 0.7071067811865476) * jnp.abs(h))
    poly = t * (
        0.127414796
        + t * (-0.142248368 + t * (0.7107068705 + t * (-0.7265760135 + t * 0.5307027145)))
    )
    tail = poly * e
    phi = jnp.where(h >= 0.0, 1.0 - tail, tail)
    return h * phi, phi + h * (0.3989422804014327 * e)


def norm_rows(r):
    center = r - jnp.mean(r, axis=-1, keepdims=True)
    rstd = lax.rsqrt(jnp.mean(center * center, axis=-1, keepdims=True) + 1e-5)
    return center * rstd, rstd


def norm_back(dy, n, rstd, gain):
    dyg = dy * gain
    return (
        dyg
        - jnp.mean(dyg, axis=-1, keepdims=True)
        - n * jnp.mean(dyg * n, axis=-1, keepdims=True)
    ) * rstd


def halves(v):
    lane = lax.broadcasted_iota(jnp.int32, v.shape, 1)
    zero = jnp.zeros_like(v)
    return jnp.concatenate([jnp.where(lane < HEAD, v, zero), jnp.where(lane < HEAD, zero, v)], 0)


def unhalve(v):
    top, bottom = v[:SEG], v[SEG:]
    lane = lax.broadcasted_iota(jnp.int32, top.shape, 1)
    return jnp.where(lane < HEAD, top, bottom)


def fold8(v):
    return jnp.sum(v.reshape(v.shape[0] // 8, 8, v.shape[1]), axis=0)


def row(ref, *idx):
    i = idx[-1]
    return ref[idx[:-1] + (slice(i, i + 1), slice(None))].astype(F32)


class Copies:
    def __init__(self, sems):
        self.sems, self.all = sems, []

    def start(self, src, dst):
        copy = pltpu.make_async_copy(src, dst, self.sems.at[len(self.all)])
        copy.start()
        self.all.append(copy)
        return copy


def fwd_kernel(
    x_ref, aw, ab, an, mw, mb, ms,
    second_o, first_o, n1_o, rs1_o, n2_o, rs2_o, qkv_o, p_o, ctx_o, act_o, gp_o, cls_o,
    wq, w1, w2, second, first, n1, rs1, n2, rs2, qkv, p, ctx, act, gp, r, wsem, osem,
):
    outs, loads = Copies(osem), Copies(wsem)
    for j in range(4):
        s = slice(j * D, (j + 1) * D)
        loads.start(aw.at[0, :, s], wq.at[:, s])
    loads.start(mw.at[0, 0], w1)
    loads.start(mw.at[0, 1], w2)
    loads = loads.all
    x = x_ref[...]
    for j in range(3):
        loads[j].wait()
        s = slice(j * D, (j + 1) * D)
        v = dot(x, wq[:, s])
        if j != 1:
            v = v + row(ab, 0, j // 2)
        qkv[:, s] = v.astype(BF)
    outs.start(qkv, qkv_o)

    @pl.loop(0, OWN)
    def _(g):
        rows = pl.ds(pl.multiple_of(g * SEG, SEG), SEG)
        for h in range(PAIRS):
            c = slice(h * 128, (h + 1) * 128)
            q = qkv[rows, c] * jnp.asarray(0.125, BF)
            kc = halves(qkv[rows, D + h * 128 : D + (h + 1) * 128])
            vc = halves(qkv[rows, 2 * D + h * 128 : 2 * D + (h + 1) * 128])
            s = dot_nt(q, kc)
            ps = []
            for i in range(2):
                si = s[:, i * 128 : (i + 1) * 128]
                e = jnp.exp(si - jnp.max(si, axis=-1, keepdims=True))
                ps.append((e / jnp.sum(e, axis=-1, keepdims=True)).astype(BF))
            pp = jnp.concatenate(ps, axis=1)
            p[pl.ds(pl.multiple_of(g * ROWS + h * SEG, SEG), SEG), :] = pp
            ctx[rows, c] = dot(pp, vc).astype(BF)

    outs.start(p, p_o)
    outs.start(ctx, ctx_o)
    loads[3].wait()
    r[...] = x.astype(F32) + dot(ctx[...], wq[:, 3 * D :]) + row(ab, 0, 2)

    @pl.loop(0, ROWS // 64)
    def _(i):
        rows = pl.ds(pl.multiple_of(i * 64, 64), 64)
        n, rs = norm_rows(r[rows, :])
        n1[rows, :] = n.astype(BF)
        rs1[rows, :] = rs
        first[rows, :] = (n * row(an, 0, 0) + row(an, 0, 1)).astype(BF)

    outs.start(n1, n1_o)
    outs.start(rs1, rs1_o)
    outs.start(first, first_o)
    loads[4].wait()
    for j in range(4):
        s = slice(j * D, (j + 1) * D)
        r[...] = dot(first[...], w1[:, s]) + mb[0:1, s].astype(F32)

        @pl.loop(0, ROWS // 32)
        def _(i):
            rows = pl.ds(pl.multiple_of(i * 32, 32), 32)
            a, g = gelu_parts(r[rows, :])
            act[rows, s] = a.astype(BF)
            gp[rows, s] = g.astype(BF)

    outs.start(act, act_o)
    outs.start(gp, gp_o)
    loads[5].wait()
    r[...] = first[...].astype(F32) + dot_nt(act[...], w2[...]) + row(ms, 0, 0)
    cls_o[...] = jnp.zeros_like(cls_o)

    @pl.loop(0, OWN)
    def _(g):
        for part in range(2):
            rows = pl.ds(pl.multiple_of(g * SEG + part * 64, 64), 64)
            n, rs = norm_rows(r[rows, :])
            n2[rows, :] = n.astype(BF)
            rs2[rows, :] = rs
            value = (n * row(ms, 0, 1) + row(ms, 0, 2)).astype(BF)
            second[rows, :] = value
            if part == 0:
                cls_o[pl.ds(g, 1), :] = value[0:1].astype(F32)

    outs.start(n2, n2_o)
    outs.start(rs2, rs2_o)
    outs.start(second, second_o)
    for copy in outs.all:
        copy.wait()


def forward(x, aw, ab, an, mw, mb, ms):
    def big(width, dt=BF):
        return ((ROWS, width), dt)

    specs = [big(D), big(D), big(D), big(1, F32), big(D), big(1, F32), big(3 * D)]
    specs += [((OWN * ROWS, 256), BF), big(D), big(FF), big(FF)]
    shapes = [jax.ShapeDtypeStruct(*s) for s in specs] + [jax.ShapeDtypeStruct((8, D), F32)]
    return pl.pallas_call(
        fwd_kernel,
        out_shape=shapes,
        in_specs=[VM, ANY, VM, VM, ANY, VM, VM],
        out_specs=[ANY] * len(specs) + [VM],
        scratch_shapes=[pltpu.VMEM((D, FF), BF)] * 3
        + [pltpu.VMEM(*s) for s in specs]
        + [
            pltpu.VMEM((ROWS, D), F32),
            pltpu.SemaphoreType.DMA((6,)),
            pltpu.SemaphoreType.DMA((len(specs),)),
        ],
        compiler_params=pltpu.CompilerParams(vmem_limit_bytes=56 * 2**20),
    )(x, aw, ab, an, mw, mb, ms)


def cls_kernel(
    own_ref, other_ref, cown_ref, cother_ref, counts, aw, ab, an, mw, mb, ms, embed,
    fourth_o, dlead_o, cols_o, wide_o, small_o,
    wq, w1, w2, wsem,
):
    loads = Copies(wsem)
    loads.start(aw.at[1], wq)
    loads.start(mw.at[1, 0], w1)
    loads.start(mw.at[1, 1], w2)
    loads = loads.all
    section = lax.axis_index("section")
    per_micro = lax.axis_size("section") // MICRO
    half = lax.rem(section, per_micro)
    micro = section // per_micro
    ends = [counts[micro, 0], counts[micro, 0] + counts[micro, 1]]

    def layout(shape, axis):
        r = lax.broadcasted_iota(jnp.int32, shape, axis)
        seg = jnp.where(r < 8, r, r - 2)
        valid = (r < 6) | ((r >= 8) & (r < 14))
        doc = jnp.where(seg >= ends[0], 1, 0) + jnp.where(seg >= ends[1], 1, 0)
        start = jnp.where(doc == 0, 0, jnp.where(doc == 1, ends[0], ends[1]))
        pos = jnp.where(valid, seg - start, -1)
        return jnp.where(valid, doc, jnp.where(r < 16, 100 + r, -1)), pos, valid

    def order(a_ref, b_ref):
        a, b = a_ref[...], b_ref[...]
        first = half == 0
        return jnp.concatenate([jnp.where(first, a, b), jnp.where(first, b, a)], axis=0)

    def mine(v):
        return jnp.where(half == 0, v[:8], v[8:])

    doc_q, pos, valid = layout((16, 128), 0)
    doc_k, _, _ = layout((16, 128), 1)
    allowed = jnp.concatenate([doc_q == doc_k] * HEADS, axis=0)
    lanes8 = lax.broadcasted_iota(jnp.int32, (16, 8), 1)
    onehot = (pos[:, :8] == lanes8).astype(BF)
    leaders = order(own_ref, other_ref) + dot(onehot, embed[...])
    low = leaders.astype(BF)
    lane = lax.broadcasted_iota(jnp.int32, (16, D), 1) // HEAD

    def stack(v):
        return jnp.concatenate([jnp.where(lane == h, v, jnp.zeros_like(v)) for h in range(HEADS)], 0)

    def unstack(v):
        total = jnp.where(lane == 0, v[:16], 0.0)
        for h in range(1, HEADS):
            total = total + jnp.where(lane == h, v[h * 16 : (h + 1) * 16], 0.0)
        return total

    def deep(v):
        return jnp.concatenate([v, jnp.zeros((112, D), BF)], axis=0)

    loads[0].wait()
    q = (dot(low, wq[:, :D]) + row(ab, 1, 0)).astype(BF)
    k = dot(low, wq[:, D : 2 * D]).astype(BF)
    v = (dot(low, wq[:, 2 * D : 3 * D]) + row(ab, 1, 1)).astype(BF)
    qs, kd, vd = stack(q), deep(k), deep(v)
    scores = jnp.where(allowed, dot_nt(qs, kd) * 0.125, MASKED)
    e = jnp.exp(scores - jnp.max(scores, axis=-1, keepdims=True))
    probs = e / jnp.sum(e, axis=-1, keepdims=True)
    probs_low = probs.astype(BF)
    ctx = unstack(dot(probs_low, vd)).astype(BF)
    n1, rs1 = norm_rows(leaders + dot(ctx, wq[:, 3 * D :]) + row(ab, 1, 2))
    third = (n1 * row(an, 1, 0) + row(an, 1, 1)).astype(BF)
    loads[1].wait()
    act, gp = gelu_parts(dot(third, w1[...]) + mb[1:2, :].astype(F32))
    act = act.astype(BF)
    loads[2].wait()
    n2, rs2 = norm_rows(third.astype(F32) + dot_nt(act, w2[...]) + row(ms, 1, 0))
    fourth_o[...] = mine(n2 * row(ms, 1, 1) + row(ms, 1, 2))

    dy = order(cown_ref, cother_ref)
    small_o[10:11, :] = jnp.sum(mine(dy * n2), axis=0, keepdims=True)
    small_o[11:12, :] = jnp.sum(mine(dy), axis=0, keepdims=True)
    dr = norm_back(dy, n2, rs2, row(ms, 1, 1))
    dbf = dr.astype(BF)
    small_o[9:10, :] = jnp.sum(mine(dbf.astype(F32)), axis=0, keepdims=True)
    dh = (dot(dbf, w2[...]) * gp).astype(BF)
    dh_mine = mine(dh.astype(F32))
    dh_sum = jnp.sum(dh_mine, axis=0, keepdims=True)
    for j in range(4):
        small_o[5 + j : 6 + j, :] = dh_sum[:, j * D : (j + 1) * D]
    dthird = (dr + dot_nt(dh, w1[...])).astype(BF).astype(F32)
    small_o[3:4, :] = jnp.sum(mine(dthird * n1), axis=0, keepdims=True)
    small_o[4:5, :] = jnp.sum(mine(dthird), axis=0, keepdims=True)
    dr = norm_back(dthird, n1, rs1, row(an, 1, 0))
    dba = dr.astype(BF)
    small_o[2:3, :] = jnp.sum(mine(dba.astype(F32)), axis=0, keepdims=True)
    dctx = stack(dot_nt(dba, wq[:, 3 * D :]).astype(BF))
    dp = dot_nt(dctx, vd)
    dv = dot_tn(probs_low, dctx)[:16].astype(BF)
    ds = (probs * (dp - jnp.sum(dp * probs, axis=-1, keepdims=True))).astype(BF)
    dq = (unstack(dot(ds, kd)) * 0.125).astype(BF)
    dk = (dot_tn(ds, qs)[:16] * 0.125).astype(BF)
    small_o[0:1, :] = jnp.sum(mine(dq.astype(F32)), axis=0, keepdims=True)
    small_o[1:2, :] = jnp.sum(mine(dv.astype(F32)), axis=0, keepdims=True)
    dlead = dr + dot_nt(dq, wq[:, :D]) + dot_nt(dk, wq[:, D : 2 * D])
    dlead = dlead + dot_nt(dv, wq[:, 2 * D : 3 * D])
    dlead_mine = mine(dlead)
    dlead_o[...] = dlead_mine
    pos_mine = jnp.where(half == 0, pos[:8], pos[8:])
    for i in range(8):
        hit = jnp.where(pos_mine[:, 0:1] == i, dlead_mine, 0.0)
        small_o[12 + i : 13 + i, :] = jnp.sum(hit, axis=0, keepdims=True)
    zeros = jnp.zeros((8, D), F32)

    def pack(top, bottom):
        return jnp.concatenate([top, bottom], axis=0).astype(BF)

    cols_o[0] = pack(dh_mine, mine(act.astype(F32)))
    for j, piece in enumerate((dq, dk, dv)):
        cols_o[1, :, j * D : (j + 1) * D] = pack(mine(piece.astype(F32)), zeros)
    cols_o[1, :, 3 * D :] = pack(zeros, mine(dba.astype(F32)))
    wide_o[0] = pack(mine(third.astype(F32)), mine(dbf.astype(F32)))
    wide_o[1] = pack(mine(low.astype(F32)), mine(ctx.astype(F32)))


def cls_chain(own, other, cown, cother, counts, aw, ab, an, mw, mb, ms, embed):
    shapes = [((8, D), F32), ((8, D), F32), ((2, 16, FF), BF), ((2, 16, D), BF), ((20, D), F32)]
    return pl.pallas_call(
        cls_kernel,
        out_shape=[jax.ShapeDtypeStruct(*s) for s in shapes],
        in_specs=[VM, VM, VM, VM, SM, ANY, VM, VM, ANY, VM, VM, VM],
        out_specs=[VM] * 5,
        scratch_shapes=[pltpu.VMEM((D, FF), BF)] * 3 + [pltpu.SemaphoreType.DMA((3,))],
        compiler_params=pltpu.CompilerParams(vmem_limit_bytes=56 * 2**20),
    )(own, other, cown, cother, counts, aw, ab, an, mw, mb, ms, embed)


def bwd_kernel(
    cot, dlead, x, n1_i, rs1_i, n2_i, rs2_i, first_i, qkv_i, p_i, ctx_i, act_i, gp_i,
    aw, an, mw, ms,
    dx_o, dw_o, small_o,
    wq, w1, w2, first, n1, rs1, n2, rs2, qkv, p, ctx, act, gp,
    r, db, dqkv, dctx, dw, sums, wsem, osem,
):
    loads = Copies(wsem)
    for src, dst in (
        (n2_i, n2), (rs2_i, rs2), (act_i, act), (mw.at[0, 1], w2), (gp_i, gp), (first_i, first),
        (mw.at[0, 0], w1), (n1_i, n1), (rs1_i, rs1), (ctx_i, ctx), (aw.at[0], wq), (qkv_i, qkv), (p_i, p),
    ):
        loads.start(src, dst)
    loads = loads.all
    pending = [None, None]
    count = [0]

    def put(value, which, start):
        slot = count[0] % 2
        if pending[slot] is not None:
            pending[slot].wait()
        dw[slot] = value.astype(BF)
        copy = pltpu.make_async_copy(dw.at[slot], dw_o.at[which, start : start + D, :], osem.at[slot])
        copy.start()
        pending[slot] = copy
        count[0] += 1

    sums[...] = jnp.zeros_like(sums)

    def norm_step(rows, dy, n_ref, rs_ref, gain, at):
        n = n_ref[rows, :].astype(F32)
        dr = norm_back(dy, n, rs_ref[rows, :], gain)
        r[rows, :] = dr
        low = dr.astype(BF)
        db[rows, :] = low
        sums[at] += fold8(low.astype(F32))
        sums[at + 1] += fold8(dy * n)
        sums[at + 2] += fold8(dy)

    loads[0].wait()
    loads[1].wait()

    @pl.loop(0, OWN)
    def _(g):
        for part in range(2):
            rows = pl.ds(pl.multiple_of(g * SEG + part * 64, 64), 64)
            dy = cot[rows, :].astype(F32)
            if part == 0:
                cls = lax.broadcasted_iota(jnp.int32, (64, D), 0) == 0
                lead = dlead[pl.ds(g, 1), :].astype(BF).astype(F32)
                dy = jnp.where(cls, lead, dy)
            norm_step(rows, dy, n2, rs2, row(ms, 0, 1), 0)

    loads[2].wait()
    for j in range(4):
        put(dot_tn(act[:, j * D : (j + 1) * D], db[...]), 2, j * D)
    loads[3].wait()
    loads[4].wait()
    for j in range(4):
        s = slice(j * D, (j + 1) * D)
        low = (dot(db[...], w2[:, s]) * gp[:, s].astype(F32)).astype(BF)
        gp[:, s] = low
        sums[6 + j] = fold8(low.astype(F32))
    loads[5].wait()
    for j in range(4):
        put(dot_tn(gp[:, j * D : (j + 1) * D], first[...]), 1, j * D)
    loads[6].wait()
    r[...] += dot_nt(gp[...], w1[...])
    loads[7].wait()
    loads[8].wait()

    @pl.loop(0, ROWS // 64)
    def _(i):
        rows = pl.ds(pl.multiple_of(i * 64, 64), 64)
        dy = r[rows, :].astype(BF).astype(F32)
        norm_step(rows, dy, n1, rs1, row(an, 0, 0), 3)

    loads[9].wait()
    put(dot_tn(db[...], ctx[...]), 0, 3 * D)
    loads[10].wait()
    dctx[...] = dot_nt(db[...], wq[:, 3 * D :]).astype(BF)
    loads[11].wait()
    loads[12].wait()

    @pl.loop(0, OWN)
    def _(g):
        rows = pl.ds(pl.multiple_of(g * SEG, SEG), SEG)
        for h in range(PAIRS):
            cq = slice(h * 128, (h + 1) * 128)
            ck = slice(D + h * 128, D + (h + 1) * 128)
            cv = slice(2 * D + h * 128, 2 * D + (h + 1) * 128)
            q = qkv[rows, cq]
            kc, vc = halves(qkv[rows, ck]), halves(qkv[rows, cv])
            dc = dctx[rows, cq]
            pp = p[pl.ds(pl.multiple_of(g * ROWS + h * SEG, SEG), SEG), :]
            dp = dot_nt(dc, vc)
            pf = pp.astype(F32)
            ds = []
            for i in range(2):
                c = slice(i * 128, (i + 1) * 128)
                pi, di = pf[:, c], dp[:, c]
                ds.append((pi * (di - jnp.sum(di * pi, axis=-1, keepdims=True))).astype(BF))
            ds = jnp.concatenate(ds, axis=1)
            dqkv[rows, cq] = (dot(ds, kc) * 0.125).astype(BF)
            dqkv[rows, ck] = (unhalve(dot_tn(ds, q)) * 0.125).astype(BF)
            dqkv[rows, cv] = unhalve(dot_tn(pp, dc)).astype(BF)

    for j in range(3):
        s = slice(j * D, (j + 1) * D)
        put(dot_tn(dqkv[:, s], x[...]), 0, j * D)
        if j != 1:
            sums[10 + j // 2] = fold8(dqkv[:, s].astype(F32))
    dx_o[...] = (r[...] + dot_nt(dqkv[...], wq[:, : 3 * D])).astype(BF)
    for i, at in enumerate((10, 11, 3, 4, 5, 6, 7, 8, 9, 0, 1, 2)):
        small_o[i : i + 1, :] = jnp.sum(sums[at], axis=0, keepdims=True)
    for copy in pending:
        copy.wait()


def backward(cot, dlead, x, n1, rs1, n2, rs2, first, qkv, p, ctx, act, gp, aw, an, mw, ms):
    shapes = [((ROWS, D), BF), ((3, FF, D), BF), ((12, D), F32)]
    kept = (first, n1, rs1, n2, rs2, qkv, p, ctx, act, gp)
    return pl.pallas_call(
        bwd_kernel,
        out_shape=[jax.ShapeDtypeStruct(*s) for s in shapes],
        in_specs=[VM, VM, VM] + [ANY] * 11 + [VM, ANY, VM],
        out_specs=[VM, ANY, VM],
        scratch_shapes=[pltpu.VMEM((D, FF), BF)] * 3
        + [pltpu.VMEM(a.shape, a.dtype) for a in kept]
        + [
            pltpu.VMEM((ROWS, D), F32),
            pltpu.VMEM((ROWS, D), BF),
            pltpu.VMEM((ROWS, 3 * D), BF),
            pltpu.VMEM((ROWS, D), BF),
            pltpu.VMEM((2, D, D), BF),
            pltpu.VMEM((12, 8, D), F32),
            pltpu.SemaphoreType.DMA((13,)),
            pltpu.SemaphoreType.DMA((2,)),
        ],
        compiler_params=pltpu.CompilerParams(vmem_limit_bytes=60 * 2**20),
    )(cot, dlead, x, n1, rs1, n2, rs2, first, qkv, p, ctx, act, gp, aw, an, mw, ms)


def cls_grads(wide, cols, ga_o, gm_o, pick):
    w0, c0 = wide[0], cols[0]
    low = lax.rem(lax.broadcasted_iota(jnp.int32, c0.shape, 0), 16) < 8
    zero = jnp.zeros_like(c0)
    gm_o[1, 0] = dot_tn(w0, pick(jnp.where(low, c0, zero)))
    gm_o[1, 1] = dot_tn(w0, pick(jnp.where(low, zero, c0)))
    ga_o[1] = dot_tn(wide[1], pick(cols[1]))


def place_kernel(red, cols, wide, ga_o, gm_o):
    ga_o[0] = red[0].astype(F32).T
    gm_o[0, 0] = red[1].astype(F32).T
    gm_o[0, 1] = red[2].astype(F32).T
    cls_grads(wide, cols, ga_o, gm_o, lambda v: v)


def place(red, cols, wide):
    width = red.shape[1]
    return pl.pallas_call(
        place_kernel,
        out_shape=[
            jax.ShapeDtypeStruct((2, D, width), F32),
            jax.ShapeDtypeStruct((2, 2, D, width), F32),
        ],
        in_specs=[VM] * 3,
        out_specs=[VM] * 2,
        compiler_params=pltpu.CompilerParams(vmem_limit_bytes=56 * 2**20),
    )(red, cols, wide)


class Place:
    def __init__(self):
        self.dp, self.section = lax.axis_index("dp"), lax.axis_index("section")
        self.n_dp = lax.axis_size("dp")
        self.nz = self.n_dp // 2
        self.z, self.x = self.dp // 2, lax.rem(self.dp, 2)
        self.y, self.c = self.section // 2, lax.rem(self.section, 2)

    def at(self, dz=0, x=None, y=None, c=None):
        x = self.x if x is None else x
        y = self.y if y is None else y
        c = self.c if c is None else c
        return ((self.z + dz) * 2 + x, y * 2 + c)

    def to_x(self):
        return self.at(x=1 - self.x)

    def to_y(self):
        return self.at(y=1 - self.y)

    def to_c(self):
        return self.at(c=1 - self.c)

    def greet(self):
        barrier = pltpu.get_barrier_semaphore()
        peers = [self.to_c(), self.to_y()]
        peers += [(lax.rem(self.dp + k, self.n_dp), self.section) for k in range(1, self.n_dp)]
        for peer in peers:
            pl.semaphore_signal(barrier, inc=1, device_id=peer, device_id_type=MESH)
        pl.semaphore_wait(barrier, len(peers))


class Links:
    def __init__(self, sends, recvs):
        self.sends, self.recvs, self.used = sends, recvs, 0

    def copy(self, src, dst, peer):
        i = self.used
        self.used += 1
        return pltpu.make_async_remote_copy(
            src_ref=src, dst_ref=dst, send_sem=self.sends.at[i], recv_sem=self.recvs.at[i],
            device_id=peer, device_id_type=MESH,
        )


HALF = D // 2
LEFT, RIGHT = slice(0, HALF), slice(HALF, D)


class Scatter:
    def __init__(self, me, links, given, held, core, xa, yb, ya, xb, right, left):
        self.me, self.held = me, held
        self.core, self.xa, self.yb, self.ya, self.xb = core, xa, yb, ya, xb
        self.right, self.left = right, left
        x, y, c, nz = me.x, me.y, me.c, me.nz
        every = slice(None)
        cols_a, cols_b = pl.ds(0, HALF), pl.ds(HALF, HALF)
        self.core_copy = links.copy(given, core, me.to_c())
        self.xa_copy = links.copy(held.at[:, 1 - x, :, :, cols_a], xa, me.to_x())
        self.yb_copy = links.copy(held.at[:, :, 1 - y, :, cols_b], yb, me.to_y())
        self.ya_copy = links.copy(held.at[:, x, 1 - y, :, cols_a], ya, me.to_y())
        self.xb_copy = links.copy(held.at[:, 1 - x, y, :, cols_b], xb, me.to_x())
        self.r_copy, self.l_copy = {}, {}
        for k in range(nz - 1):
            d = nz - 1 - k
            self.r_copy[d] = links.copy(held.at[d, x, y], right.at[d], me.at(dz=1))
            self.l_copy[k] = links.copy(held.at[k, x, y], left.at[k], me.at(dz=-1))

    def add(self, z, x, y, cols, value):
        self.held[z, x, y, :, cols] = self.held[z, x, y, :, cols] + value

    def start(self):
        self.core_copy.start()

    def first(self):
        me, core = self.me, self.core
        x, y = me.x, me.y
        self.core_copy.wait_recv()

        @pl.loop(0, me.nz)
        def _(z):
            for i in range(2):
                self.add(z, 1 - x, i, LEFT, core[z, 1 - x, i, :, LEFT])

        self.xa_copy.start()

        @pl.loop(0, me.nz)
        def _(z):
            for i in range(2):
                self.add(z, i, 1 - y, RIGHT, core[z, i, 1 - y, :, RIGHT])

        self.yb_copy.start()

        @pl.loop(0, me.nz)
        def _(z):
            for i in range(2):
                self.add(z, x, i, LEFT, core[z, x, i, :, LEFT])
                self.add(z, i, y, RIGHT, core[z, i, y, :, RIGHT])

    def second(self):
        me = self.me
        x, y = me.x, me.y
        self.xa_copy.wait_recv()

        @pl.loop(0, me.nz)
        def _(z):
            self.add(z, x, 1 - y, LEFT, self.xa[z, 1 - y])

        self.ya_copy.start()
        self.yb_copy.wait_recv()

        @pl.loop(0, me.nz)
        def _(z):
            self.add(z, 1 - x, y, RIGHT, self.yb[z, 1 - x])

        self.xb_copy.start()

        @pl.loop(0, me.nz)
        def _(z):
            self.add(z, x, y, LEFT, self.xa[z, y])
            self.add(z, x, y, RIGHT, self.yb[z, x])

    def third(self):
        me = self.me
        self.ya_copy.wait_recv()
        self.xb_copy.wait_recv()

        @pl.loop(0, me.nz)
        def _(z):
            self.add(z, me.x, me.y, LEFT, self.ya[z])
            self.add(z, me.x, me.y, RIGHT, self.xb[z])

    def along(self, k):
        me, nz, z = self.me, self.me.nz, self.me.z
        d = nz - 1 - k
        every = slice(None)

        @pl.when(z < d)
        def _():
            @pl.when(z > 0)
            def _():
                self.r_copy[d].wait_recv()
                self.add(d, me.x, me.y, every, self.right[d])

            self.r_copy[d].start()

        @pl.when(z > k)
        def _():
            @pl.when(z < nz - 1)
            def _():
                self.l_copy[k].wait_recv()
                self.add(k, me.x, me.y, every, self.left[k])

            self.l_copy[k].start()

    def finish(self, total):
        me, nz, z = self.me, self.me.nz, self.me.z
        for copy in (self.core_copy, self.xa_copy, self.yb_copy, self.ya_copy, self.xb_copy):
            copy.wait_send()
        total[...] = self.held[z, me.x, me.y].astype(F32)
        for d in range(nz):
            if d > 0:

                @pl.when(z < d)
                def _():
                    self.r_copy[d].wait_send()

                @pl.when(z == d)
                def _():
                    self.r_copy[d].wait_recv()
                    total[...] += self.right[d].astype(F32)

            if d < nz - 1:

                @pl.when(z > d)
                def _():
                    self.l_copy[d].wait_send()

                @pl.when(z == d)
                def _():
                    self.l_copy[d].wait_recv()
                    total[...] += self.left[d].astype(F32)


def scatter_buffers(nz, width):
    shapes = [(nz, 2, 2, width, D)] * 2 + [(nz, 2, width, HALF)] * 2 + [(nz, width, HALF)] * 2
    return shapes + [(nz, width, D)] * 2


def scatter_copies(nz):
    return 5 + 2 * (nz - 1)


class Gather:
    def __init__(self, me, links, wide, cols, all_wide, all_cols):
        self.me, self.all_wide, self.all_cols = me, all_wide, all_cols
        self.wide, self.cols = wide, cols
        span = cols.shape[-1] // me.n_dp
        here = (me.dp, me.y, me.c)
        self.first_copies = []
        for k in range(1, me.n_dp):
            peer = lax.rem(me.dp + k, me.n_dp)
            part = pl.ds(pl.multiple_of(peer * span, 128), span)
            self.first_copies.append(links.copy(wide, all_wide.at[here], (peer, me.section)))
            self.first_copies.append(links.copy(cols.at[:, :, part], all_cols.at[here], (peer, me.section)))
        across = (slice(None), me.y, me.c)
        self.second_copies = [links.copy(a.at[across], a.at[across], me.to_y()) for a in (all_wide, all_cols)]
        beside = (slice(None), slice(None), me.c)
        self.third_copies = [links.copy(a.at[beside], a.at[beside], me.to_c()) for a in (all_wide, all_cols)]

    def start(self):
        me = self.me
        span = self.cols.shape[-1] // me.n_dp
        for copy in self.first_copies:
            copy.start()
        self.all_wide[me.dp, me.y, me.c] = self.wide[...]
        part = pl.ds(pl.multiple_of(me.dp * span, 128), span)
        self.all_cols[me.dp, me.y, me.c] = self.cols[:, :, part]

    def second(self):
        for copy in self.first_copies:
            copy.wait()
        for copy in self.second_copies:
            copy.start()

    def third(self):
        for copy in self.second_copies:
            copy.wait()
        for copy in self.third_copies:
            copy.start()

    def finish(self):
        for copy in self.third_copies:
            copy.wait()


class Total:
    def __init__(self, me, links, acc, got):
        self.acc, self.got, self.copies = acc, got, []
        peers = [me.to_c(), me.to_y()]
        step = 1
        while step < me.n_dp:
            bit = lax.rem(me.dp // step, 2)
            peers.append((me.dp + step * (1 - 2 * bit), me.section))
            step *= 2
        for i, peer in enumerate(peers):
            self.copies.append(links.copy(acc, got.at[i], peer))

    def start(self, i):
        self.copies[i].start()

    def add(self, i):
        self.copies[i].wait()
        self.acc[...] += self.got[i]


def pick_own(me, width):
    def pick(v):
        out = v[:, :width]
        for s in range(1, 4):
            out = jnp.where(me.section == s, v[:, s * width : (s + 1) * width], out)
        return out

    return pick


def comm_kernel(dw, small, wide, cols, ga_o, gm_o, small_o, *scratch):
    n_scatter = 8
    sets = [scratch[i * n_scatter : (i + 1) * n_scatter] for i in range(3)]
    all_wide, all_cols, got, total, sends, recvs, local = scratch[3 * n_scatter :]
    me, links = Place(), Links(sends, recvs)
    loads = []
    for m in range(3):
        loads.append(pltpu.make_async_copy(dw.at[m, :, :, :, me.c], sets[m][0], local.at[m]))
        loads[m].start()
    scat = [Scatter(me, links, dw.at[m, :, :, :, 1 - me.c], *sets[m]) for m in range(3)]
    gather = Gather(me, links, wide, cols, all_wide, all_cols)
    small_o[...] = small[...]
    summed = Total(me, links, small_o, got)
    me.greet()
    for s in scat:
        s.start()
    gather.start()
    summed.start(0)
    for load in loads:
        load.wait()
    a, b, c = scat
    a.first()
    b.first()
    summed.add(0)
    summed.start(1)
    a.second()
    gather.second()
    c.first()
    summed.add(1)
    summed.start(2)
    a.third()
    a.along(0)
    b.second()
    a.along(1)
    gather.third()
    b.third()
    b.along(0)
    a.along(2)
    summed.add(2)
    summed.start(3)
    c.second()
    b.along(1)
    gather.finish()
    width = total.shape[0]
    rows = 16 * 4 * me.n_dp
    wide_all = [all_wide[:, :, :, i].reshape(rows, D) for i in range(2)]
    cols_all = [all_cols[:, :, :, i].reshape(rows, 4 * width) for i in range(2)]
    cls_grads(wide_all, cols_all, ga_o, gm_o, pick_own(me, width))
    c.third()
    c.along(0)
    b.along(2)
    a.finish(total)
    ga_o[0] = total[...].T
    summed.add(3)
    summed.start(4)
    c.along(1)
    b.finish(total)
    gm_o[0, 0] = total[...].T
    c.along(2)
    summed.add(4)
    c.finish(total)
    gm_o[0, 1] = total[...].T


def combine(dw, small, wide, cols, n_dp):
    nz, width = n_dp // 2, FF // (4 * n_dp)
    dw = dw.reshape(3, nz, 2, 2, 2, width, D)
    steps = 2 + (n_dp - 1).bit_length()
    count = 3 * scatter_copies(nz) + 2 * (n_dp - 1) + 4 + steps
    return pl.pallas_call(
        comm_kernel,
        out_shape=[
            jax.ShapeDtypeStruct((2, D, width), F32),
            jax.ShapeDtypeStruct((2, 2, D, width), F32),
            jax.ShapeDtypeStruct(small.shape, F32),
        ],
        in_specs=[ANY, VM, VM, VM],
        out_specs=[VM] * 3,
        scratch_shapes=[pltpu.VMEM(s, BF) for s in scatter_buffers(nz, width) * 3]
        + [
            pltpu.VMEM((n_dp, 2, 2, 2, 16, D), BF),
            pltpu.VMEM((n_dp, 2, 2, 2, 16, 4 * width), BF),
            pltpu.VMEM((steps,) + small.shape, F32),
            pltpu.VMEM((width, D), F32),
            pltpu.SemaphoreType.DMA((count,)),
            pltpu.SemaphoreType.DMA((count,)),
            pltpu.SemaphoreType.DMA((3,)),
        ],
        compiler_params=pltpu.CompilerParams(
            vmem_limit_bytes=56 * 2**20, collective_id=0, has_side_effects=True
        ),
    )(dw, small, wide, cols)


def swap_half(v):
    size = lax.axis_size("section")
    per_micro = size // MICRO
    return lax.ppermute(v, "section", [(i, i - i % per_micro + (i + 1) % per_micro) for i in range(size)])


def on_device(tokens, counts, aw, ab, an, mw, mb, ms, embed, cot):
    cls_cot = jnp.pad(cot.reshape(OWN, SEG, D)[:, 0].astype(F32), ((0, 2), (0, 0)))
    cls_cot_other = swap_half(cls_cot)
    second, first, n1, rs1, n2, rs2, qkv, p, ctx, act, gp, cls = forward(tokens, aw, ab, an, mw, mb, ms)
    fourth, dlead, cols, wide, small1 = cls_chain(
        cls, swap_half(cls), cls_cot, cls_cot_other, counts, aw, ab, an, mw, mb, ms, embed
    )
    encoded = second.reshape(OWN, SEG, D).at[:, 0].set(fourth[:OWN].astype(BF)).reshape(ROWS, D)
    dx, dw, small0 = backward(
        cot, dlead, tokens, n1, rs1, n2, rs2, first, qkv, p, ctx, act, gp, aw, an, mw, ms
    )
    small = jnp.concatenate([small0, small1], axis=0)
    n_dp, n_section = lax.axis_size("dp"), lax.axis_size("section")
    width = FF // (n_dp * n_section)
    if n_section == 4 and n_dp & (n_dp - 1) == 0 and width % 16 == 0 and 4 * width % 128 == 0:
        ga, gm, small = combine(dw, small, wide, cols, n_dp)
    else:
        cols = lax.all_to_all(cols, BOTH, split_axis=2, concat_axis=1, tiled=True)
        wide = lax.all_gather(wide, BOTH, axis=1, tiled=True)
        red = lax.psum_scatter(dw, BOTH, scatter_dimension=1, tiled=True)
        small = lax.psum(small, BOTH)
        ga, gm = place(red, cols, wide)
    return (
        encoded,
        dx,
        ga,
        jnp.stack([small[0:3], small[12:15]]),
        jnp.stack([small[3:5], small[15:17]]),
        gm,
        jnp.stack([small[5:9].reshape(FF), small[17:21].reshape(FF)]),
        jnp.stack([small[9:12], small[21:24]]),
        small[24:32],
    )


def solution(mesh):
    return jax.shard_map(
        on_device,
        mesh=mesh,
        in_specs=(P(BOTH, None), P("dp", None)) + (P(),) * 7 + (P(BOTH, None),),
        out_specs=(
            P(BOTH, None),
            P(BOTH, None),
            P(None, None, BOTH),
            P(),
            P(),
            P(None, None, None, BOTH),
            P(),
            P(),
            P(),
        ),
        check_vma=False,
    )
```

```python
import functools

import jax
import jax.numpy as jnp
from jax import lax
from jax.experimental import pallas as pl
from jax.experimental.pallas import tpu as pltpu
from jax.sharding import PartitionSpec as P

F32 = jnp.float32
BF = jnp.bfloat16
D = 768
FF = 3072
SEG = 128
HEAD = 64
HEADS = 12
PAIRS = 6
MICRO = 2
SEGS = 12
OWN = 6
ROWS = OWN * SEG
BLOCKS = (4, 2, 2, 2, 96, D)
BOTH = ("dp", "section")
MASKED = -1e30
VM = pl.BlockSpec(memory_space=pltpu.VMEM)
SM = pl.BlockSpec(memory_space=pltpu.SMEM)
ANY = pl.BlockSpec(memory_space=pl.ANY)
MESH = pl.DeviceIdType.MESH


def dot(a, b):
    return jnp.dot(a, b, preferred_element_type=F32)


def dot_nt(a, b):
    return lax.dot_general(a, b, (((1,), (1,)), ((), ())), preferred_element_type=F32)


def dot_tn(a, b):
    return lax.dot_general(a, b, (((0,), (0,)), ((), ())), preferred_element_type=F32)


def gelu_parts(h):
    e = jnp.exp(-0.5 * h * h)
    t = 1.0 / (1.0 + (0.3275911 * 0.7071067811865476) * jnp.abs(h))
    poly = t * (
        0.127414796
        + t * (-0.142248368 + t * (0.7107068705 + t * (-0.7265760135 + t * 0.5307027145)))
    )
    tail = poly * e
    phi = jnp.where(h >= 0.0, 1.0 - tail, tail)
    return h * phi, phi + h * (0.3989422804014327 * e)


def norm_rows(r):
    center = r - jnp.mean(r, axis=-1, keepdims=True)
    rstd = lax.rsqrt(jnp.mean(center * center, axis=-1, keepdims=True) + 1e-5)
    return center * rstd, rstd


def norm_back(dy, n, rstd, gain):
    dyg = dy * gain
    return (
        dyg
        - jnp.mean(dyg, axis=-1, keepdims=True)
        - n * jnp.mean(dyg * n, axis=-1, keepdims=True)
    ) * rstd


def halves(v):
    lane = lax.broadcasted_iota(jnp.int32, v.shape, 1)
    zero = jnp.zeros_like(v)
    return jnp.concatenate([jnp.where(lane < HEAD, v, zero), jnp.where(lane < HEAD, zero, v)], 0)


def unhalve(v):
    top, bottom = v[:SEG], v[SEG:]
    lane = lax.broadcasted_iota(jnp.int32, top.shape, 1)
    return jnp.where(lane < HEAD, top, bottom)


def fold8(v):
    return jnp.sum(v.reshape(v.shape[0] // 8, 8, v.shape[1]), axis=0)


def block(ref, j):
    return ref[j].reshape(D, D)


def row(ref, *idx):
    i = idx[-1]
    return ref[idx[:-1] + (slice(i, i + 1), slice(None))].astype(F32)


class Copies:
    def __init__(self, sems):
        self.sems, self.all = sems, []

    def start(self, src, dst):
        copy = pltpu.make_async_copy(src, dst, self.sems.at[len(self.all)])
        copy.start()
        self.all.append(copy)
        return copy


def fwd_kernel(
    x_ref, aw, ab, an, mw, mb, ms,
    second_o, first_o, n1_o, rs1_o, n2_o, rs2_o, qkv_o, p_o, ctx_o, act_o, gp_o, cls_o,
    wq, w1, w2, second, first, n1, rs1, n2, rs2, qkv, p, ctx, act, gp, r, wsem, osem,
):
    outs, loads = Copies(osem), Copies(wsem)
    for j in range(4):
        s = slice(j * D, (j + 1) * D)
        loads.start(aw.at[0, :, s], wq.at[:, s])
    loads.start(mw.at[0, 0], w1)
    loads.start(mw.at[0, 1], w2)
    loads = loads.all
    x = x_ref[...]
    for j in range(3):
        loads[j].wait()
        s = slice(j * D, (j + 1) * D)
        v = dot(x, wq[:, s])
        if j != 1:
            v = v + row(ab, 0, j // 2)
        qkv[:, s] = v.astype(BF)
    outs.start(qkv, qkv_o)

    @pl.loop(0, OWN)
    def _(g):
        rows = pl.ds(pl.multiple_of(g * SEG, SEG), SEG)
        for h in range(PAIRS):
            c = slice(h * 128, (h + 1) * 128)
            q = qkv[rows, c] * jnp.asarray(0.125, BF)
            kc = halves(qkv[rows, D + h * 128 : D + (h + 1) * 128])
            vc = halves(qkv[rows, 2 * D + h * 128 : 2 * D + (h + 1) * 128])
            s = dot_nt(q, kc)
            ps = []
            for i in range(2):
                si = s[:, i * 128 : (i + 1) * 128]
                e = jnp.exp(si - jnp.max(si, axis=-1, keepdims=True))
                ps.append((e / jnp.sum(e, axis=-1, keepdims=True)).astype(BF))
            pp = jnp.concatenate(ps, axis=1)
            p[pl.ds(pl.multiple_of(g * ROWS + h * SEG, SEG), SEG), :] = pp
            ctx[rows, c] = dot(pp, vc).astype(BF)

    outs.start(p, p_o)
    outs.start(ctx, ctx_o)
    loads[3].wait()
    r[...] = x.astype(F32) + dot(ctx[...], wq[:, 3 * D :]) + row(ab, 0, 2)

    @pl.loop(0, ROWS // 64)
    def _(i):
        rows = pl.ds(pl.multiple_of(i * 64, 64), 64)
        n, rs = norm_rows(r[rows, :])
        n1[rows, :] = n.astype(BF)
        rs1[rows, :] = rs
        first[rows, :] = (n * row(an, 0, 0) + row(an, 0, 1)).astype(BF)

    outs.start(n1, n1_o)
    outs.start(rs1, rs1_o)
    outs.start(first, first_o)
    loads[4].wait()
    for j in range(4):
        s = slice(j * D, (j + 1) * D)
        r[...] = dot(first[...], w1[:, s]) + mb[0:1, s].astype(F32)

        for b in range(8):

            @pl.loop(0, 3)
            def _(i):
                rows = pl.ds(pl.multiple_of(i * 32, 32), 32)
                a, g = gelu_parts(r[pl.ds(pl.multiple_of(b * 96 + i * 32, 32), 32), :])
                at = (j, b // 4, b // 2 % 2, b % 2, rows, slice(None))
                act[at] = a.astype(BF)
                gp[at] = g.astype(BF)

    outs.start(act, act_o)
    outs.start(gp, gp_o)
    loads[5].wait()
    r[...] = first[...].astype(F32) + row(ms, 0, 0)
    for j in range(4):
        r[...] += dot_nt(block(act, j), w2[:, j * D : (j + 1) * D])
    cls_o[...] = jnp.zeros_like(cls_o)

    @pl.loop(0, OWN)
    def _(g):
        for part in range(2):
            rows = pl.ds(pl.multiple_of(g * SEG + part * 64, 64), 64)
            n, rs = norm_rows(r[rows, :])
            n2[rows, :] = n.astype(BF)
            rs2[rows, :] = rs
            value = (n * row(ms, 0, 1) + row(ms, 0, 2)).astype(BF)
            second[rows, :] = value
            if part == 0:
                cls_o[pl.ds(g, 1), :] = value[0:1].astype(F32)

    outs.start(n2, n2_o)
    outs.start(rs2, rs2_o)
    outs.start(second, second_o)
    for copy in outs.all:
        copy.wait()


def forward(x, aw, ab, an, mw, mb, ms):
    def big(width, dt=BF):
        return ((ROWS, width), dt)

    specs = [big(D), big(D), big(D), big(1, F32), big(D), big(1, F32), big(3 * D)]
    specs += [((OWN * ROWS, 256), BF), big(D), (BLOCKS, BF), (BLOCKS, BF)]
    shapes = [jax.ShapeDtypeStruct(*s) for s in specs] + [jax.ShapeDtypeStruct((8, D), F32)]
    return pl.pallas_call(
        fwd_kernel,
        out_shape=shapes,
        in_specs=[VM, ANY, VM, VM, ANY, VM, VM],
        out_specs=[ANY] * len(specs) + [VM],
        scratch_shapes=[pltpu.VMEM((D, FF), BF)] * 3
        + [pltpu.VMEM(*s) for s in specs]
        + [
            pltpu.VMEM((ROWS, D), F32),
            pltpu.SemaphoreType.DMA((6,)),
            pltpu.SemaphoreType.DMA((len(specs),)),
        ],
        compiler_params=pltpu.CompilerParams(vmem_limit_bytes=56 * 2**20),
    )(x, aw, ab, an, mw, mb, ms)


def cls_kernel(
    own_ref, other_ref, cown_ref, cother_ref, counts, aw, ab, an, mw, mb, ms, embed,
    fourth_o, dlead_o, cols_o, wide_o, small_o,
    wq, w1, w2, wsem,
):
    loads = Copies(wsem)
    loads.start(aw.at[1], wq)
    loads.start(mw.at[1, 0], w1)
    loads.start(mw.at[1, 1], w2)
    loads = loads.all
    section = lax.axis_index("section")
    per_micro = lax.axis_size("section") // MICRO
    half = lax.rem(section, per_micro)
    micro = section // per_micro
    ends = [counts[micro, 0], counts[micro, 0] + counts[micro, 1]]

    def layout(shape, axis):
        r = lax.broadcasted_iota(jnp.int32, shape, axis)
        seg = jnp.where(r < 8, r, r - 2)
        valid = (r < 6) | ((r >= 8) & (r < 14))
        doc = jnp.where(seg >= ends[0], 1, 0) + jnp.where(seg >= ends[1], 1, 0)
        start = jnp.where(doc == 0, 0, jnp.where(doc == 1, ends[0], ends[1]))
        pos = jnp.where(valid, seg - start, -1)
        return jnp.where(valid, doc, jnp.where(r < 16, 100 + r, -1)), pos, valid

    def order(a_ref, b_ref):
        a, b = a_ref[...], b_ref[...]
        first = half == 0
        return jnp.concatenate([jnp.where(first, a, b), jnp.where(first, b, a)], axis=0)

    def mine(v):
        return jnp.where(half == 0, v[:8], v[8:])

    doc_q, pos, valid = layout((16, 128), 0)
    doc_k, _, _ = layout((16, 128), 1)
    allowed = jnp.concatenate([doc_q == doc_k] * HEADS, axis=0)
    lanes8 = lax.broadcasted_iota(jnp.int32, (16, 8), 1)
    onehot = (pos[:, :8] == lanes8).astype(BF)
    leaders = order(own_ref, other_ref) + dot(onehot, embed[...])
    low = leaders.astype(BF)
    lane = lax.broadcasted_iota(jnp.int32, (16, D), 1) // HEAD

    def stack(v):
        return jnp.concatenate([jnp.where(lane == h, v, jnp.zeros_like(v)) for h in range(HEADS)], 0)

    def unstack(v):
        total = jnp.where(lane == 0, v[:16], 0.0)
        for h in range(1, HEADS):
            total = total + jnp.where(lane == h, v[h * 16 : (h + 1) * 16], 0.0)
        return total

    def deep(v):
        return jnp.concatenate([v, jnp.zeros((112, D), BF)], axis=0)

    loads[0].wait()
    q = (dot(low, wq[:, :D]) + row(ab, 1, 0)).astype(BF)
    k = dot(low, wq[:, D : 2 * D]).astype(BF)
    v = (dot(low, wq[:, 2 * D : 3 * D]) + row(ab, 1, 1)).astype(BF)
    qs, kd, vd = stack(q), deep(k), deep(v)
    scores = jnp.where(allowed, dot_nt(qs, kd) * 0.125, MASKED)
    e = jnp.exp(scores - jnp.max(scores, axis=-1, keepdims=True))
    probs = e / jnp.sum(e, axis=-1, keepdims=True)
    probs_low = probs.astype(BF)
    ctx = unstack(dot(probs_low, vd)).astype(BF)
    n1, rs1 = norm_rows(leaders + dot(ctx, wq[:, 3 * D :]) + row(ab, 1, 2))
    third = (n1 * row(an, 1, 0) + row(an, 1, 1)).astype(BF)
    loads[1].wait()
    act, gp = gelu_parts(dot(third, w1[...]) + mb[1:2, :].astype(F32))
    act = act.astype(BF)
    loads[2].wait()
    n2, rs2 = norm_rows(third.astype(F32) + dot_nt(act, w2[...]) + row(ms, 1, 0))
    fourth_o[...] = mine(n2 * row(ms, 1, 1) + row(ms, 1, 2))

    dy = order(cown_ref, cother_ref)
    small_o[10:11, :] = jnp.sum(mine(dy * n2), axis=0, keepdims=True)
    small_o[11:12, :] = jnp.sum(mine(dy), axis=0, keepdims=True)
    dr = norm_back(dy, n2, rs2, row(ms, 1, 1))
    dbf = dr.astype(BF)
    small_o[9:10, :] = jnp.sum(mine(dbf.astype(F32)), axis=0, keepdims=True)
    dh = (dot(dbf, w2[...]) * gp).astype(BF)
    dh_mine = mine(dh.astype(F32))
    dh_sum = jnp.sum(dh_mine, axis=0, keepdims=True)
    for j in range(4):
        small_o[5 + j : 6 + j, :] = dh_sum[:, j * D : (j + 1) * D]
    dthird = (dr + dot_nt(dh, w1[...])).astype(BF).astype(F32)
    small_o[3:4, :] = jnp.sum(mine(dthird * n1), axis=0, keepdims=True)
    small_o[4:5, :] = jnp.sum(mine(dthird), axis=0, keepdims=True)
    dr = norm_back(dthird, n1, rs1, row(an, 1, 0))
    dba = dr.astype(BF)
    small_o[2:3, :] = jnp.sum(mine(dba.astype(F32)), axis=0, keepdims=True)
    dctx = stack(dot_nt(dba, wq[:, 3 * D :]).astype(BF))
    dp = dot_nt(dctx, vd)
    dv = dot_tn(probs_low, dctx)[:16].astype(BF)
    ds = (probs * (dp - jnp.sum(dp * probs, axis=-1, keepdims=True))).astype(BF)
    dq = (unstack(dot(ds, kd)) * 0.125).astype(BF)
    dk = (dot_tn(ds, qs)[:16] * 0.125).astype(BF)
    small_o[0:1, :] = jnp.sum(mine(dq.astype(F32)), axis=0, keepdims=True)
    small_o[1:2, :] = jnp.sum(mine(dv.astype(F32)), axis=0, keepdims=True)
    dlead = dr + dot_nt(dq, wq[:, :D]) + dot_nt(dk, wq[:, D : 2 * D])
    dlead = dlead + dot_nt(dv, wq[:, 2 * D : 3 * D])
    dlead_mine = mine(dlead)
    dlead_o[...] = dlead_mine
    pos_mine = jnp.where(half == 0, pos[:8], pos[8:])
    for i in range(8):
        hit = jnp.where(pos_mine[:, 0:1] == i, dlead_mine, 0.0)
        small_o[12 + i : 13 + i, :] = jnp.sum(hit, axis=0, keepdims=True)
    zeros = jnp.zeros((8, D), F32)

    def pack(top, bottom):
        return jnp.concatenate([top, bottom], axis=0).astype(BF)

    cols_o[0] = pack(dh_mine, mine(act.astype(F32)))
    for j, piece in enumerate((dq, dk, dv)):
        cols_o[1, :, j * D : (j + 1) * D] = pack(mine(piece.astype(F32)), zeros)
    cols_o[1, :, 3 * D :] = pack(zeros, mine(dba.astype(F32)))
    wide_o[0] = pack(mine(third.astype(F32)), mine(dbf.astype(F32)))
    wide_o[1] = pack(mine(low.astype(F32)), mine(ctx.astype(F32)))


def cls_chain(own, other, cown, cother, counts, aw, ab, an, mw, mb, ms, embed):
    shapes = [((8, D), F32), ((8, D), F32), ((2, 16, FF), BF), ((2, 16, D), BF), ((20, D), F32)]
    return pl.pallas_call(
        cls_kernel,
        out_shape=[jax.ShapeDtypeStruct(*s) for s in shapes],
        in_specs=[VM, VM, VM, VM, SM, ANY, VM, VM, ANY, VM, VM, VM],
        out_specs=[VM] * 5,
        scratch_shapes=[pltpu.VMEM((D, FF), BF)] * 3 + [pltpu.SemaphoreType.DMA((3,))],
        compiler_params=pltpu.CompilerParams(vmem_limit_bytes=56 * 2**20),
    )(own, other, cown, cother, counts, aw, ab, an, mw, mb, ms, embed)


def cls_grads(wide, cols, ga_o, gm_o, pick):
    w0, c0 = wide[0], cols[0]
    low = lax.rem(lax.broadcasted_iota(jnp.int32, c0.shape, 0), 16) < 8
    zero = jnp.zeros_like(c0)
    gm_o[1, 0] = dot_tn(w0, pick(jnp.where(low, c0, zero)))
    gm_o[1, 1] = dot_tn(w0, pick(jnp.where(low, zero, c0)))
    ga_o[1] = dot_tn(wide[1], pick(cols[1]))


def place_kernel(red, cols, wide, ga_o, gm_o):
    ga_o[0] = red[0].astype(F32).T
    gm_o[0, 0] = red[1].astype(F32).T
    gm_o[0, 1] = red[2].astype(F32).T
    cls_grads(wide, cols, ga_o, gm_o, lambda v: v)


def place(red, cols, wide):
    width = red.shape[1]
    return pl.pallas_call(
        place_kernel,
        out_shape=[
            jax.ShapeDtypeStruct((2, D, width), F32),
            jax.ShapeDtypeStruct((2, 2, D, width), F32),
        ],
        in_specs=[VM] * 3,
        out_specs=[VM] * 2,
        compiler_params=pltpu.CompilerParams(vmem_limit_bytes=56 * 2**20),
    )(red, cols, wide)


class Place:
    def __init__(self):
        self.dp, self.section = lax.axis_index("dp"), lax.axis_index("section")
        self.n_dp = lax.axis_size("dp")
        self.nz = self.n_dp // 2
        self.z, self.x = self.dp // 2, lax.rem(self.dp, 2)
        self.y, self.c = self.section // 2, lax.rem(self.section, 2)

    def at(self, dz=0, x=None, y=None, c=None):
        x = self.x if x is None else x
        y = self.y if y is None else y
        c = self.c if c is None else c
        return ((self.z + dz) * 2 + x, y * 2 + c)

    def to_x(self):
        return self.at(x=1 - self.x)

    def to_y(self):
        return self.at(y=1 - self.y)

    def to_c(self):
        return self.at(c=1 - self.c)

    def greet(self):
        barrier = pltpu.get_barrier_semaphore()
        peers = [self.to_c(), self.to_y()]
        peers += [(lax.rem(self.dp + k, self.n_dp), self.section) for k in range(1, self.n_dp)]
        for peer in peers:
            pl.semaphore_signal(barrier, inc=1, device_id=peer, device_id_type=MESH)
        pl.semaphore_wait(barrier, len(peers))


class Links:
    def __init__(self, sends, recvs):
        self.sends, self.recvs, self.used = sends, recvs, 0

    def copy(self, src, dst, peer):
        i = self.used
        self.used += 1
        return pltpu.make_async_remote_copy(
            src_ref=src, dst_ref=dst, send_sem=self.sends.at[i], recv_sem=self.recvs.at[i],
            device_id=peer, device_id_type=MESH,
        )


HALF = D // 2
LEFT, RIGHT = slice(0, HALF), slice(HALF, D)


class Scatter:
    def __init__(self, me, links, held, core, xa, yb, ya, xb, right, left):
        self.me, self.held = me, held
        self.core, self.xa, self.yb, self.ya, self.xb = core, xa, yb, ya, xb
        self.right, self.left = right, left
        x, y, c, nz = me.x, me.y, me.c, me.nz
        cols_a, cols_b = pl.ds(0, HALF), pl.ds(HALF, HALF)
        self.core_copy = links.copy(held.at[:, :, :, 1 - c], core, me.to_c())
        self.xa_copy = links.copy(held.at[:, 1 - x, :, c, :, cols_a], xa, me.to_x())
        self.yb_copy = links.copy(held.at[:, :, 1 - y, c, :, cols_b], yb, me.to_y())
        self.ya_copy = links.copy(held.at[:, x, 1 - y, c, :, cols_a], ya, me.to_y())
        self.xb_copy = links.copy(held.at[:, 1 - x, y, c, :, cols_b], xb, me.to_x())
        self.r_copy, self.l_copy = {}, {}
        for k in range(nz - 1):
            d = nz - 1 - k
            self.r_copy[d] = links.copy(held.at[d, x, y, c], right.at[d], me.at(dz=1))
            self.l_copy[k] = links.copy(held.at[k, x, y, c], left.at[k], me.at(dz=-1))

    def add(self, z, x, y, cols, value):
        c = self.me.c
        self.held[z, x, y, c, :, cols] = self.held[z, x, y, c, :, cols] + value

    def start(self):
        self.core_copy.start()

    def first(self):
        me, core = self.me, self.core
        x, y = me.x, me.y
        self.core_copy.wait_recv()

        @pl.loop(0, me.nz)
        def _(z):
            for i in range(2):
                self.add(z, 1 - x, i, LEFT, core[z, 1 - x, i, :, LEFT])

        self.xa_copy.start()

        @pl.loop(0, me.nz)
        def _(z):
            for i in range(2):
                self.add(z, i, 1 - y, RIGHT, core[z, i, 1 - y, :, RIGHT])

        self.yb_copy.start()

        @pl.loop(0, me.nz)
        def _(z):
            for i in range(2):
                self.add(z, x, i, LEFT, core[z, x, i, :, LEFT])
                self.add(z, i, y, RIGHT, core[z, i, y, :, RIGHT])

    def second(self):
        me = self.me
        x, y = me.x, me.y
        self.xa_copy.wait_recv()

        @pl.loop(0, me.nz)
        def _(z):
            self.add(z, x, 1 - y, LEFT, self.xa[z, 1 - y])

        self.ya_copy.start()
        self.yb_copy.wait_recv()

        @pl.loop(0, me.nz)
        def _(z):
            self.add(z, 1 - x, y, RIGHT, self.yb[z, 1 - x])

        self.xb_copy.start()

        @pl.loop(0, me.nz)
        def _(z):
            self.add(z, x, y, LEFT, self.xa[z, y])
            self.add(z, x, y, RIGHT, self.yb[z, x])

    def third(self):
        me = self.me
        self.ya_copy.wait_recv()
        self.xb_copy.wait_recv()

        @pl.loop(0, me.nz)
        def _(z):
            self.add(z, me.x, me.y, LEFT, self.ya[z])
            self.add(z, me.x, me.y, RIGHT, self.xb[z])

    def along(self, k):
        me, nz, z = self.me, self.me.nz, self.me.z
        d = nz - 1 - k
        every = slice(None)

        @pl.when(z < d)
        def _():
            @pl.when(z > 0)
            def _():
                self.r_copy[d].wait_recv()
                self.add(d, me.x, me.y, every, self.right[d])

            self.r_copy[d].start()

        @pl.when(z > k)
        def _():
            @pl.when(z < nz - 1)
            def _():
                self.l_copy[k].wait_recv()
                self.add(k, me.x, me.y, every, self.left[k])

            self.l_copy[k].start()

    def finish(self, total):
        me, nz, z = self.me, self.me.nz, self.me.z
        for copy in (self.core_copy, self.xa_copy, self.yb_copy, self.ya_copy, self.xb_copy):
            copy.wait_send()
        total[...] = self.held[z, me.x, me.y, me.c].astype(F32)
        for d in range(nz):
            if d > 0:

                @pl.when(z < d)
                def _():
                    self.r_copy[d].wait_send()

                @pl.when(z == d)
                def _():
                    self.r_copy[d].wait_recv()
                    total[...] += self.right[d].astype(F32)

            if d < nz - 1:

                @pl.when(z > d)
                def _():
                    self.l_copy[d].wait_send()

                @pl.when(z == d)
                def _():
                    self.l_copy[d].wait_recv()
                    total[...] += self.left[d].astype(F32)


def scatter_buffers(nz, width):
    shapes = [(nz, 2, 2, width, D)] + [(nz, 2, width, HALF)] * 2 + [(nz, width, HALF)] * 2
    return shapes + [(nz, width, D)] * 2


def scatter_copies(nz):
    return 5 + 2 * (nz - 1)


class Gather:
    def __init__(self, me, links, wide, cols, all_wide, all_cols):
        self.me, self.all_wide, self.all_cols = me, all_wide, all_cols
        self.wide, self.cols = wide, cols
        span = cols.shape[-1] // me.n_dp
        here = (me.dp, me.y, me.c)
        self.first_copies = []
        for k in range(1, me.n_dp):
            peer = lax.rem(me.dp + k, me.n_dp)
            part = pl.ds(pl.multiple_of(peer * span, 128), span)
            self.first_copies.append(links.copy(wide, all_wide.at[here], (peer, me.section)))
            self.first_copies.append(links.copy(cols.at[:, :, part], all_cols.at[here], (peer, me.section)))
        across = (slice(None), me.y, me.c)
        self.second_copies = [links.copy(a.at[across], a.at[across], me.to_y()) for a in (all_wide, all_cols)]
        beside = (slice(None), slice(None), me.c)
        self.third_copies = [links.copy(a.at[beside], a.at[beside], me.to_c()) for a in (all_wide, all_cols)]

    def start(self):
        me = self.me
        span = self.cols.shape[-1] // me.n_dp
        for copy in self.first_copies:
            copy.start()
        self.all_wide[me.dp, me.y, me.c] = self.wide[...]
        part = pl.ds(pl.multiple_of(me.dp * span, 128), span)
        self.all_cols[me.dp, me.y, me.c] = self.cols[:, :, part]

    def second(self):
        for copy in self.first_copies:
            copy.wait()
        for copy in self.second_copies:
            copy.start()

    def third(self):
        for copy in self.second_copies:
            copy.wait()
        for copy in self.third_copies:
            copy.start()

    def finish(self):
        for copy in self.third_copies:
            copy.wait()


class Total:
    def __init__(self, me, links, acc, got):
        self.acc, self.got, self.copies = acc, got, []
        peers = [me.to_c(), me.to_y()]
        step = 1
        while step < me.n_dp:
            bit = lax.rem(me.dp // step, 2)
            peers.append((me.dp + step * (1 - 2 * bit), me.section))
            step *= 2
        for i, peer in enumerate(peers):
            self.copies.append(links.copy(acc, got.at[i], peer))

    def start(self, i):
        self.copies[i].start()

    def add(self, i):
        self.copies[i].wait()
        self.acc[...] += self.got[i]


def pick_own(me, width):
    def pick(v):
        out = v[:, :width]
        for s in range(1, 4):
            out = jnp.where(me.section == s, v[:, s * width : (s + 1) * width], out)
        return out

    return pick


N_SET = 7


class Net:
    def __init__(self, mats, small, wide, cols, ga_o, gm_o, scratch):
        sets = [scratch[i * N_SET : (i + 1) * N_SET] for i in range(3)]
        all_wide, all_cols, got, self.total, sends, recvs = scratch[3 * N_SET :]
        self.me, self.ga, self.gm, self.small = Place(), ga_o, gm_o, small
        links = Links(sends, recvs)
        self.attn, self.win, self.wout = [Scatter(self.me, links, mats[m], *sets[m]) for m in range(3)]
        self.gather = Gather(self.me, links, wide, cols, all_wide, all_cols)
        self.summed = Total(self.me, links, small, got)

    def cls(self):
        self.gather.finish()
        width = self.total.shape[0]
        rows = 16 * 4 * self.me.n_dp
        wide = [self.gather.all_wide[:, :, :, i].reshape(rows, D) for i in range(2)]
        cols = [self.gather.all_cols[:, :, :, i].reshape(rows, 4 * width) for i in range(2)]
        cls_grads(wide, cols, self.ga, self.gm, pick_own(self.me, width))

    def place(self, which, out):
        which.finish(self.total)
        out[...] = self.total[...].T


def bwd_kernel(
    fused,
    cot, dlead, x, small1, wide, cols, n1_i, rs1_i, n2_i, rs2_i, first_i, qkv_i, p_i, ctx_i, act_i, gp_i,
    aw, an, mw, ms,
    *refs,
):
    if fused:
        dx_o, small_o, ga_o, gm_o = refs[:4]
        refs = refs[4:]
    else:
        dx_o, small_o, dw_o = refs[:3]
        refs = refs[3:]
    w1, w2, first, n1, rs1, n2, rs2, qkv, p, ctx, act, gp, dwout, r, db, sums, wsem, osem = refs[:18]
    loads = Copies(wsem)
    for src, dst in (
        (cot, dx_o), (n2_i, n2), (rs2_i, rs2), (act_i, act), (mw.at[0, 1], w2), (gp_i, gp), (first_i, first),
        (mw.at[0, 0], w1), (n1_i, n1), (rs1_i, rs1), (ctx_i, ctx), (qkv_i, qkv), (p_i, p),
    ):
        loads.start(src, dst)
    loads = loads.all
    mats = (gp, act, dwout)
    if fused:
        net = Net(mats, small_o, wide, cols, ga_o, gm_o, refs[18:])
        attn, win, wout, summed = net.attn, net.win, net.wout, net.summed
        net.me.greet()
        net.gather.start()
    else:
        outs = Copies(osem)
    sums[...] = jnp.zeros_like(sums)

    def norm_step(rows, dy, n_ref, rs_ref, gain, at):
        n = n_ref[rows, :].astype(F32)
        dr = norm_back(dy, n, rs_ref[rows, :], gain)
        r[rows, :] = dr
        low = dr.astype(BF)
        db[rows, :] = low
        sums[at] += fold8(low.astype(F32))
        sums[at + 1] += fold8(dy * n)
        sums[at + 2] += fold8(dy)

    def put(ref, j, value):
        ref[j] = value.astype(BF).reshape(BLOCKS[1:])

    def done(which):
        if fused:
            (attn, win, wout)[which].start()
        else:
            outs.start(mats[which], dw_o.at[which])

    for i in range(3):
        loads[i].wait()

    @pl.loop(0, OWN)
    def _(g):
        for part in range(2):
            rows = pl.ds(pl.multiple_of(g * SEG + part * 64, 64), 64)
            dy = dx_o[rows, :].astype(F32)
            if part == 0:
                cls = lax.broadcasted_iota(jnp.int32, (64, D), 0) == 0
                lead = dlead[pl.ds(g, 1), :].astype(BF).astype(F32)
                dy = jnp.where(cls, lead, dy)
            norm_step(rows, dy, n2, rs2, row(ms, 0, 1), 0)

    loads[3].wait()
    for j in range(4):
        put(dwout, j, dot_tn(block(act, j), db[...]))
    done(2)
    loads[4].wait()
    loads[5].wait()
    for j in range(4):
        low = (dot(db[...], w2[:, j * D : (j + 1) * D]) * block(gp, j).astype(F32)).astype(BF)
        put(gp, j, low)
        sums[6 + j] = fold8(low.astype(F32))
    load_wq = pltpu.make_async_copy(aw.at[0], w2, wsem.at[13])
    load_wq.start()
    if fused:
        wout.first()
    loads[6].wait()
    for j in range(4):
        put(act, j, dot_tn(block(gp, j), first[...]))
    done(1)
    if fused:
        net.gather.second()
    loads[7].wait()
    for j in range(4):
        r[...] += dot_nt(block(gp, j), w1[:, j * D : (j + 1) * D])
    if fused:
        win.first()
    loads[8].wait()
    loads[9].wait()

    @pl.loop(0, ROWS // 64)
    def _(i):
        rows = pl.ds(pl.multiple_of(i * 64, 64), 64)
        dy = r[rows, :].astype(BF).astype(F32)
        norm_step(rows, dy, n1, rs1, row(an, 0, 0), 3)

    loads[10].wait()
    put(gp, 3, dot_tn(db[...], ctx[...]))
    load_wq.wait()
    wq, dctx = w2, n2
    dctx[...] = dot_nt(db[...], wq[:, 3 * D :]).astype(BF)
    if fused:
        wout.second()
    loads[11].wait()
    loads[12].wait()

    def attention(g):
        rows = pl.ds(pl.multiple_of(g * SEG, SEG), SEG)
        for h in range(PAIRS):
            cq = slice(h * 128, (h + 1) * 128)
            ck = slice(D + h * 128, D + (h + 1) * 128)
            cv = slice(2 * D + h * 128, 2 * D + (h + 1) * 128)
            q = qkv[rows, cq]
            kc, vc = halves(qkv[rows, ck]), halves(qkv[rows, cv])
            dc = dctx[rows, cq]
            pp = p[pl.ds(pl.multiple_of(g * ROWS + h * SEG, SEG), SEG), :]
            dp = dot_nt(dc, vc)
            pf = pp.astype(F32)
            ds = []
            for i in range(2):
                c = slice(i * 128, (i + 1) * 128)
                pi, di = pf[:, c], dp[:, c]
                ds.append((pi * (di - jnp.sum(di * pi, axis=-1, keepdims=True))).astype(BF))
            ds = jnp.concatenate(ds, axis=1)
            qkv[rows, cq] = (dot(ds, kc) * 0.125).astype(BF)
            qkv[rows, ck] = (unhalve(dot_tn(ds, q)) * 0.125).astype(BF)
            qkv[rows, cv] = unhalve(dot_tn(pp, dc)).astype(BF)

    pl.loop(0, OWN // 2)(attention)
    if fused:
        net.gather.third()
        wout.third()
        wout.along(0)
    pl.loop(OWN // 2, OWN)(attention)
    if fused:
        win.second()
        wout.along(1)
    for j in range(3):
        s = slice(j * D, (j + 1) * D)
        put(gp, j, dot_tn(qkv[:, s], x[...]))
        if j != 1:
            sums[10 + j // 2] = fold8(qkv[:, s].astype(F32))
    done(0)
    for i, at in enumerate((10, 11, 3, 4, 5, 6, 7, 8, 9, 0, 1, 2)):
        small_o[i : i + 1, :] = jnp.sum(sums[at], axis=0, keepdims=True)
    small_o[12:, :] = small1[...]
    if fused:
        summed.start(0)
        wout.along(2)
        win.third()
        win.along(0)
    dx_o[...] = (r[...] + dot_nt(qkv[...], wq[:, : 3 * D])).astype(BF)
    if not fused:
        for copy in outs.all:
            copy.wait()
        return
    attn.first()
    win.along(1)
    summed.add(0)
    summed.start(1)
    net.cls()
    net.place(wout, gm_o.at[0, 1])
    win.along(2)
    summed.add(1)
    summed.start(2)
    attn.second()
    net.place(win, gm_o.at[0, 0])
    summed.add(2)
    summed.start(3)
    attn.third()
    attn.along(0)
    summed.add(3)
    summed.start(4)
    attn.along(1)
    attn.along(2)
    summed.add(4)
    net.place(attn, ga_o.at[0])


def backward(fused, n_dp, cot, dlead, x, small1, wide, cols, kept, aw, an, mw, ms):
    width = FF // (4 * n_dp)
    if fused:
        shapes = [((ROWS, D), BF), ((32, D), F32), ((2, D, width), F32), ((2, 2, D, width), F32)]
    else:
        shapes = [((ROWS, D), BF), ((32, D), F32), ((3,) + BLOCKS, BF)]
    first, n1, rs1, n2, rs2, qkv, p, ctx, act, gp = kept
    scratch = [pltpu.VMEM((D, FF), BF)] * 2 + [pltpu.VMEM(a.shape, a.dtype) for a in kept]
    scratch += [
        pltpu.VMEM(BLOCKS, BF),
        pltpu.VMEM((ROWS, D), F32),
        pltpu.VMEM((ROWS, D), BF),
        pltpu.VMEM((12, 8, D), F32),
        pltpu.SemaphoreType.DMA((14,)),
        pltpu.SemaphoreType.DMA((3,)),
    ]
    params = {}
    if fused:
        steps = 2 + (n_dp - 1).bit_length()
        count = 3 * scatter_copies(n_dp // 2) + 2 * (n_dp - 1) + 4 + steps
        scratch += [pltpu.VMEM(s, BF) for s in scatter_buffers(n_dp // 2, width) * 3]
        scratch += [
            pltpu.VMEM((n_dp, 2, 2, 2, 16, D), BF),
            pltpu.VMEM((n_dp, 2, 2, 2, 16, 4 * width), BF),
            pltpu.VMEM((steps, 32, D), F32),
            pltpu.VMEM((width, D), F32),
            pltpu.SemaphoreType.DMA((count,)),
            pltpu.SemaphoreType.DMA((count,)),
        ]
        params = dict(collective_id=0, has_side_effects=True)
    return pl.pallas_call(
        functools.partial(bwd_kernel, fused),
        out_shape=[jax.ShapeDtypeStruct(*s) for s in shapes],
        in_specs=[ANY, VM, VM, VM, VM, VM] + [ANY] * 11 + [VM, ANY, VM],
        out_specs=[VM] * 4 if fused else [VM, VM, ANY],
        scratch_shapes=scratch,
        compiler_params=pltpu.CompilerParams(vmem_limit_bytes=63 * 2**20, **params),
    )(cot, dlead, x, small1, wide, cols, n1, rs1, n2, rs2, first, qkv, p, ctx, act, gp, aw, an, mw, ms)


def swap_half(v):
    size = lax.axis_size("section")
    per_micro = size // MICRO
    return lax.ppermute(v, "section", [(i, i - i % per_micro + (i + 1) % per_micro) for i in range(size)])


def on_device(tokens, counts, aw, ab, an, mw, mb, ms, embed, cot):
    cls_cot = jnp.pad(cot.reshape(OWN, SEG, D)[:, 0].astype(F32), ((0, 2), (0, 0)))
    cls_cot_other = swap_half(cls_cot)
    second, first, n1, rs1, n2, rs2, qkv, p, ctx, act, gp, cls = forward(tokens, aw, ab, an, mw, mb, ms)
    fourth, dlead, cols, wide, small1 = cls_chain(
        cls, swap_half(cls), cls_cot, cls_cot_other, counts, aw, ab, an, mw, mb, ms, embed
    )
    encoded = second.reshape(OWN, SEG, D).at[:, 0].set(fourth[:OWN].astype(BF)).reshape(ROWS, D)
    n_dp, n_section = lax.axis_size("dp"), lax.axis_size("section")
    kept = (first, n1, rs1, n2, rs2, qkv, p, ctx, act, gp)
    args = (cot, dlead, tokens, small1, wide, cols, kept, aw, an, mw, ms)
    if (n_dp // 2, 2, 2, 2, FF // (n_dp * n_section), D) == BLOCKS and n_section == 4:
        dx, small, ga, gm = backward(True, n_dp, *args)
    else:
        dx, small, dw = backward(False, n_dp, *args)
        cols = lax.all_to_all(cols, BOTH, split_axis=2, concat_axis=1, tiled=True)
        wide = lax.all_gather(wide, BOTH, axis=1, tiled=True)
        red = lax.psum_scatter(dw.reshape(3, FF, D), BOTH, scatter_dimension=1, tiled=True)
        small = lax.psum(small, BOTH)
        ga, gm = place(red, cols, wide)
    return (
        encoded,
        dx,
        ga,
        jnp.stack([small[0:3], small[12:15]]),
        jnp.stack([small[3:5], small[15:17]]),
        gm,
        jnp.stack([small[5:9].reshape(FF), small[17:21].reshape(FF)]),
        jnp.stack([small[9:12], small[21:24]]),
        small[24:32],
    )


def solution(mesh):
    return jax.shard_map(
        on_device,
        mesh=mesh,
        in_specs=(P(BOTH, None), P("dp", None)) + (P(),) * 7 + (P(BOTH, None),),
        out_specs=(
            P(BOTH, None),
            P(BOTH, None),
            P(None, None, BOTH),
            P(),
            P(),
            P(None, None, None, BOTH),
            P(),
            P(),
            P(),
        ),
        check_vma=False,
    )
```

```python
import functools

import jax
import jax.numpy as jnp
from jax import lax
from jax.experimental import pallas as pl
from jax.experimental.pallas import tpu as pltpu
from jax.sharding import PartitionSpec as P

F32 = jnp.float32
BF = jnp.bfloat16
D = 768
FF = 3072
SEG = 128
HEAD = 64
HEADS = 12
PAIRS = 6
MICRO = 2
SEGS = 12
OWN = 6
ROWS = OWN * SEG
BLOCKS = (4, 2, 2, 2, 96, D)
BOTH = ("dp", "section")
MASKED = -1e30
VM = pl.BlockSpec(memory_space=pltpu.VMEM)
SM = pl.BlockSpec(memory_space=pltpu.SMEM)
ANY = pl.BlockSpec(memory_space=pl.ANY)
MESH = pl.DeviceIdType.MESH


def dot(a, b):
    return jnp.dot(a, b, preferred_element_type=F32)


def dot_nt(a, b):
    return lax.dot_general(a, b, (((1,), (1,)), ((), ())), preferred_element_type=F32)


def dot_tn(a, b):
    return lax.dot_general(a, b, (((0,), (0,)), ((), ())), preferred_element_type=F32)


def gelu_parts(h):
    e = jnp.exp(-0.5 * h * h)
    t = 1.0 / (1.0 + (0.3275911 * 0.7071067811865476) * jnp.abs(h))
    poly = t * (
        0.127414796
        + t * (-0.142248368 + t * (0.7107068705 + t * (-0.7265760135 + t * 0.5307027145)))
    )
    tail = poly * e
    phi = jnp.where(h >= 0.0, 1.0 - tail, tail)
    return h * phi, phi + h * (0.3989422804014327 * e)


def norm_rows(r):
    center = r - jnp.mean(r, axis=-1, keepdims=True)
    rstd = lax.rsqrt(jnp.mean(center * center, axis=-1, keepdims=True) + 1e-5)
    return center * rstd, rstd


def norm_back(dy, n, rstd, gain):
    dyg = dy * gain
    return (
        dyg
        - jnp.mean(dyg, axis=-1, keepdims=True)
        - n * jnp.mean(dyg * n, axis=-1, keepdims=True)
    ) * rstd


def halves(v):
    lane = lax.broadcasted_iota(jnp.int32, v.shape, 1)
    zero = jnp.zeros_like(v)
    return jnp.concatenate([jnp.where(lane < HEAD, v, zero), jnp.where(lane < HEAD, zero, v)], 0)


def unhalve(v):
    top, bottom = v[:SEG], v[SEG:]
    lane = lax.broadcasted_iota(jnp.int32, top.shape, 1)
    return jnp.where(lane < HEAD, top, bottom)


def fold8(v):
    return jnp.sum(v.reshape(v.shape[0] // 8, 8, v.shape[1]), axis=0)


def block(ref, j):
    return ref[j].reshape(D, D)


def row(ref, *idx):
    i = idx[-1]
    return ref[idx[:-1] + (slice(i, i + 1), slice(None))].astype(F32)


class Copies:
    def __init__(self, sems):
        self.sems, self.all = sems, []

    def start(self, src, dst):
        copy = pltpu.make_async_copy(src, dst, self.sems.at[len(self.all)])
        copy.start()
        self.all.append(copy)
        return copy


def fwd_kernel(
    x_ref, aw, ab, an, mw, mb, ms,
    second_o, first_o, n1_o, rs1_o, n2_o, rs2_o, qkv_o, p_o, ctx_o, act_o, gp_o, cls_o,
    wq, w1, w2, second, first, n1, rs1, n2, rs2, qkv, p, ctx, act, gp, r, wsem, osem,
):
    outs, loads = Copies(osem), Copies(wsem)
    for j in range(4):
        s = slice(j * D, (j + 1) * D)
        loads.start(aw.at[0, :, s], wq.at[:, s])
    loads.start(mw.at[0, 0], w1)
    loads.start(mw.at[0, 1], w2)
    loads = loads.all
    x = x_ref[...]
    for j in range(3):
        loads[j].wait()
        s = slice(j * D, (j + 1) * D)
        v = dot(x, wq[:, s])
        if j != 1:
            v = v + row(ab, 0, j // 2)
        qkv[:, s] = v.astype(BF)
    outs.start(qkv, qkv_o)

    @pl.loop(0, OWN)
    def _(g):
        rows = pl.ds(pl.multiple_of(g * SEG, SEG), SEG)
        for h in range(PAIRS):
            c = slice(h * 128, (h + 1) * 128)
            q = qkv[rows, c] * jnp.asarray(0.125, BF)
            kc = halves(qkv[rows, D + h * 128 : D + (h + 1) * 128])
            vc = halves(qkv[rows, 2 * D + h * 128 : 2 * D + (h + 1) * 128])
            s = dot_nt(q, kc)
            ps = []
            for i in range(2):
                si = s[:, i * 128 : (i + 1) * 128]
                e = jnp.exp(si - jnp.max(si, axis=-1, keepdims=True))
                ps.append((e / jnp.sum(e, axis=-1, keepdims=True)).astype(BF))
            pp = jnp.concatenate(ps, axis=1)
            p[pl.ds(pl.multiple_of(g * ROWS + h * SEG, SEG), SEG), :] = pp
            ctx[rows, c] = dot(pp, vc).astype(BF)

    outs.start(p, p_o)
    outs.start(ctx, ctx_o)
    loads[3].wait()
    r[...] = x.astype(F32) + dot(ctx[...], wq[:, 3 * D :]) + row(ab, 0, 2)

    @pl.loop(0, ROWS // 64)
    def _(i):
        rows = pl.ds(pl.multiple_of(i * 64, 64), 64)
        n, rs = norm_rows(r[rows, :])
        n1[rows, :] = n.astype(BF)
        rs1[rows, :] = rs
        first[rows, :] = (n * row(an, 0, 0) + row(an, 0, 1)).astype(BF)

    outs.start(n1, n1_o)
    outs.start(rs1, rs1_o)
    outs.start(first, first_o)
    loads[4].wait()
    for j in range(4):
        s = slice(j * D, (j + 1) * D)
        r[...] = dot(first[...], w1[:, s]) + mb[0:1, s].astype(F32)

        for b in range(8):

            @pl.loop(0, 3)
            def _(i):
                rows = pl.ds(pl.multiple_of(i * 32, 32), 32)
                a, g = gelu_parts(r[pl.ds(pl.multiple_of(b * 96 + i * 32, 32), 32), :])
                at = (j, b // 4, b // 2 % 2, b % 2, rows, slice(None))
                act[at] = a.astype(BF)
                gp[at] = g.astype(BF)

    outs.start(act, act_o)
    outs.start(gp, gp_o)
    loads[5].wait()
    r[...] = first[...].astype(F32) + row(ms, 0, 0)
    for j in range(4):
        r[...] += dot_nt(block(act, j), w2[:, j * D : (j + 1) * D])
    cls_o[...] = jnp.zeros_like(cls_o)

    @pl.loop(0, OWN)
    def _(g):
        for part in range(2):
            rows = pl.ds(pl.multiple_of(g * SEG + part * 64, 64), 64)
            n, rs = norm_rows(r[rows, :])
            n2[rows, :] = n.astype(BF)
            rs2[rows, :] = rs
            value = (n * row(ms, 0, 1) + row(ms, 0, 2)).astype(BF)
            second[rows, :] = value
            if part == 0:
                cls_o[pl.ds(g, 1), :] = value[0:1].astype(F32)

    outs.start(n2, n2_o)
    outs.start(rs2, rs2_o)
    outs.start(second, second_o)
    for copy in outs.all:
        copy.wait()


def forward(x, aw, ab, an, mw, mb, ms):
    def big(width, dt=BF):
        return ((ROWS, width), dt)

    specs = [big(D), big(D), big(D), big(1, F32), big(D), big(1, F32), big(3 * D)]
    specs += [((OWN * ROWS, 256), BF), big(D), (BLOCKS, BF), (BLOCKS, BF)]
    shapes = [jax.ShapeDtypeStruct(*s) for s in specs] + [jax.ShapeDtypeStruct((8, D), F32)]
    return pl.pallas_call(
        fwd_kernel,
        out_shape=shapes,
        in_specs=[VM, ANY, VM, VM, ANY, VM, VM],
        out_specs=[ANY] * len(specs) + [VM],
        scratch_shapes=[pltpu.VMEM((D, FF), BF)] * 3
        + [pltpu.VMEM(*s) for s in specs]
        + [
            pltpu.VMEM((ROWS, D), F32),
            pltpu.SemaphoreType.DMA((6,)),
            pltpu.SemaphoreType.DMA((len(specs),)),
        ],
        compiler_params=pltpu.CompilerParams(vmem_limit_bytes=56 * 2**20),
    )(x, aw, ab, an, mw, mb, ms)


def cls_kernel(
    own_ref, other_ref, cown_ref, cother_ref, counts, aw, ab, an, mw, mb, ms, embed,
    fourth_o, dlead_o, cols_o, wide_o, small_o,
    wq, w1, w2, wsem,
):
    loads = Copies(wsem)
    loads.start(aw.at[1], wq)
    loads.start(mw.at[1, 0], w1)
    loads.start(mw.at[1, 1], w2)
    loads = loads.all
    section = lax.axis_index("section")
    per_micro = lax.axis_size("section") // MICRO
    half = lax.rem(section, per_micro)
    micro = section // per_micro
    ends = [counts[micro, 0], counts[micro, 0] + counts[micro, 1]]

    def layout(shape, axis):
        r = lax.broadcasted_iota(jnp.int32, shape, axis)
        seg = jnp.where(r < 8, r, r - 2)
        valid = (r < 6) | ((r >= 8) & (r < 14))
        doc = jnp.where(seg >= ends[0], 1, 0) + jnp.where(seg >= ends[1], 1, 0)
        start = jnp.where(doc == 0, 0, jnp.where(doc == 1, ends[0], ends[1]))
        pos = jnp.where(valid, seg - start, -1)
        return jnp.where(valid, doc, jnp.where(r < 16, 100 + r, -1)), pos, valid

    def order(a_ref, b_ref):
        a, b = a_ref[...], b_ref[...]
        first = half == 0
        return jnp.concatenate([jnp.where(first, a, b), jnp.where(first, b, a)], axis=0)

    def mine(v):
        return jnp.where(half == 0, v[:8], v[8:])

    doc_q, pos, valid = layout((16, 128), 0)
    doc_k, _, _ = layout((16, 128), 1)
    allowed = jnp.concatenate([doc_q == doc_k] * HEADS, axis=0)
    lanes8 = lax.broadcasted_iota(jnp.int32, (16, 8), 1)
    onehot = (pos[:, :8] == lanes8).astype(BF)
    leaders = order(own_ref, other_ref) + dot(onehot, embed[...])
    low = leaders.astype(BF)
    lane = lax.broadcasted_iota(jnp.int32, (16, D), 1) // HEAD

    def stack(v):
        return jnp.concatenate([jnp.where(lane == h, v, jnp.zeros_like(v)) for h in range(HEADS)], 0)

    def unstack(v):
        total = jnp.where(lane == 0, v[:16], 0.0)
        for h in range(1, HEADS):
            total = total + jnp.where(lane == h, v[h * 16 : (h + 1) * 16], 0.0)
        return total

    def deep(v):
        return jnp.concatenate([v, jnp.zeros((112, D), BF)], axis=0)

    loads[0].wait()
    q = (dot(low, wq[:, :D]) + row(ab, 1, 0)).astype(BF)
    k = dot(low, wq[:, D : 2 * D]).astype(BF)
    v = (dot(low, wq[:, 2 * D : 3 * D]) + row(ab, 1, 1)).astype(BF)
    qs, kd, vd = stack(q), deep(k), deep(v)
    scores = jnp.where(allowed, dot_nt(qs, kd) * 0.125, MASKED)
    e = jnp.exp(scores - jnp.max(scores, axis=-1, keepdims=True))
    probs = e / jnp.sum(e, axis=-1, keepdims=True)
    probs_low = probs.astype(BF)
    ctx = unstack(dot(probs_low, vd)).astype(BF)
    n1, rs1 = norm_rows(leaders + dot(ctx, wq[:, 3 * D :]) + row(ab, 1, 2))
    third = (n1 * row(an, 1, 0) + row(an, 1, 1)).astype(BF)
    loads[1].wait()
    act, gp = gelu_parts(dot(third, w1[...]) + mb[1:2, :].astype(F32))
    act = act.astype(BF)
    loads[2].wait()
    n2, rs2 = norm_rows(third.astype(F32) + dot_nt(act, w2[...]) + row(ms, 1, 0))
    fourth_o[...] = mine(n2 * row(ms, 1, 1) + row(ms, 1, 2))

    dy = order(cown_ref, cother_ref)
    small_o[10:11, :] = jnp.sum(mine(dy * n2), axis=0, keepdims=True)
    small_o[11:12, :] = jnp.sum(mine(dy), axis=0, keepdims=True)
    dr = norm_back(dy, n2, rs2, row(ms, 1, 1))
    dbf = dr.astype(BF)
    small_o[9:10, :] = jnp.sum(mine(dbf.astype(F32)), axis=0, keepdims=True)
    dh = (dot(dbf, w2[...]) * gp).astype(BF)
    dh_mine = mine(dh.astype(F32))
    dh_sum = jnp.sum(dh_mine, axis=0, keepdims=True)
    for j in range(4):
        small_o[5 + j : 6 + j, :] = dh_sum[:, j * D : (j + 1) * D]
    dthird = (dr + dot_nt(dh, w1[...])).astype(BF).astype(F32)
    small_o[3:4, :] = jnp.sum(mine(dthird * n1), axis=0, keepdims=True)
    small_o[4:5, :] = jnp.sum(mine(dthird), axis=0, keepdims=True)
    dr = norm_back(dthird, n1, rs1, row(an, 1, 0))
    dba = dr.astype(BF)
    small_o[2:3, :] = jnp.sum(mine(dba.astype(F32)), axis=0, keepdims=True)
    dctx = stack(dot_nt(dba, wq[:, 3 * D :]).astype(BF))
    dp = dot_nt(dctx, vd)
    dv = dot_tn(probs_low, dctx)[:16].astype(BF)
    ds = (probs * (dp - jnp.sum(dp * probs, axis=-1, keepdims=True))).astype(BF)
    dq = (unstack(dot(ds, kd)) * 0.125).astype(BF)
    dk = (dot_tn(ds, qs)[:16] * 0.125).astype(BF)
    small_o[0:1, :] = jnp.sum(mine(dq.astype(F32)), axis=0, keepdims=True)
    small_o[1:2, :] = jnp.sum(mine(dv.astype(F32)), axis=0, keepdims=True)
    dlead = dr + dot_nt(dq, wq[:, :D]) + dot_nt(dk, wq[:, D : 2 * D])
    dlead = dlead + dot_nt(dv, wq[:, 2 * D : 3 * D])
    dlead_mine = mine(dlead)
    dlead_o[...] = dlead_mine
    pos_mine = jnp.where(half == 0, pos[:8], pos[8:])
    for i in range(8):
        hit = jnp.where(pos_mine[:, 0:1] == i, dlead_mine, 0.0)
        small_o[12 + i : 13 + i, :] = jnp.sum(hit, axis=0, keepdims=True)
    zeros = jnp.zeros((8, D), F32)

    def pack(top, bottom):
        return jnp.concatenate([top, bottom], axis=0).astype(BF)

    cols_o[0] = pack(dh_mine, mine(act.astype(F32)))
    for j, piece in enumerate((dq, dk, dv)):
        cols_o[1, :, j * D : (j + 1) * D] = pack(mine(piece.astype(F32)), zeros)
    cols_o[1, :, 3 * D :] = pack(zeros, mine(dba.astype(F32)))
    wide_o[0] = pack(mine(third.astype(F32)), mine(dbf.astype(F32)))
    wide_o[1] = pack(mine(low.astype(F32)), mine(ctx.astype(F32)))


def cls_chain(own, other, cown, cother, counts, aw, ab, an, mw, mb, ms, embed):
    shapes = [((8, D), F32), ((8, D), F32), ((2, 16, FF), BF), ((2, 16, D), BF), ((20, D), F32)]
    return pl.pallas_call(
        cls_kernel,
        out_shape=[jax.ShapeDtypeStruct(*s) for s in shapes],
        in_specs=[VM, VM, VM, VM, SM, ANY, VM, VM, ANY, VM, VM, VM],
        out_specs=[VM] * 5,
        scratch_shapes=[pltpu.VMEM((D, FF), BF)] * 3 + [pltpu.SemaphoreType.DMA((3,))],
        compiler_params=pltpu.CompilerParams(vmem_limit_bytes=56 * 2**20),
    )(own, other, cown, cother, counts, aw, ab, an, mw, mb, ms, embed)


def cls_grads(wide, cols, ga_o, gm_o, pick):
    w0, c0 = wide[0], cols[0]
    low = lax.rem(lax.broadcasted_iota(jnp.int32, c0.shape, 0), 16) < 8
    zero = jnp.zeros_like(c0)
    gm_o[1, 0] = dot_tn(w0, pick(jnp.where(low, c0, zero)))
    gm_o[1, 1] = dot_tn(w0, pick(jnp.where(low, zero, c0)))
    ga_o[1] = dot_tn(wide[1], pick(cols[1]))


def place_kernel(red, cols, wide, ga_o, gm_o):
    ga_o[0] = red[0].astype(F32).T
    gm_o[0, 0] = red[1].astype(F32).T
    gm_o[0, 1] = red[2].astype(F32).T
    cls_grads(wide, cols, ga_o, gm_o, lambda v: v)


def place(red, cols, wide):
    width = red.shape[1]
    return pl.pallas_call(
        place_kernel,
        out_shape=[
            jax.ShapeDtypeStruct((2, D, width), F32),
            jax.ShapeDtypeStruct((2, 2, D, width), F32),
        ],
        in_specs=[VM] * 3,
        out_specs=[VM] * 2,
        compiler_params=pltpu.CompilerParams(vmem_limit_bytes=56 * 2**20),
    )(red, cols, wide)


class Place:
    def __init__(self):
        self.dp, self.section = lax.axis_index("dp"), lax.axis_index("section")
        self.n_dp = lax.axis_size("dp")
        self.nz = self.n_dp // 2
        self.z, self.x = self.dp // 2, lax.rem(self.dp, 2)
        self.y, self.c = self.section // 2, lax.rem(self.section, 2)

    def at(self, dz=0, x=None, y=None, c=None):
        x = self.x if x is None else x
        y = self.y if y is None else y
        c = self.c if c is None else c
        return ((self.z + dz) * 2 + x, y * 2 + c)

    def to_x(self):
        return self.at(x=1 - self.x)

    def to_y(self):
        return self.at(y=1 - self.y)

    def to_c(self):
        return self.at(c=1 - self.c)

    def greet(self):
        barrier = pltpu.get_barrier_semaphore()
        peers = [self.to_c(), self.to_y()]
        peers += [(lax.rem(self.dp + k, self.n_dp), self.section) for k in range(1, self.n_dp)]
        for peer in peers:
            pl.semaphore_signal(barrier, inc=1, device_id=peer, device_id_type=MESH)
        pl.semaphore_wait(barrier, len(peers))


class Links:
    def __init__(self, sends, recvs):
        self.sends, self.recvs, self.used = sends, recvs, 0

    def copy(self, src, dst, peer, recv=None):
        i = self.used
        self.used += 1
        return pltpu.make_async_remote_copy(
            src_ref=src, dst_ref=dst, send_sem=self.sends.at[i], recv_sem=self.recvs.at[i] if recv is None else recv,
            device_id=peer, device_id_type=MESH,
        )


HALF = D // 2
LEFT, RIGHT = slice(0, HALF), slice(HALF, D)


class Scatter:
    def __init__(self, me, links, held, core, xa, yb, ya, xb, zb, z_recv, j0, count):
        self.me, self.held, self.js = me, held, range(j0, j0 + count)
        self.core, self.xa, self.yb, self.ya, self.xb = core, xa, yb, ya, xb
        x, y, c = me.x, me.y, me.c
        js, cols_a, cols_b = pl.ds(j0, count), pl.ds(0, HALF), pl.ds(HALF, HALF)
        self.core_copy = links.copy(held.at[js, :, :, 1 - c], core.at[js], me.to_c())
        self.xa_copy = links.copy(held.at[js, 1 - x, :, c, :, cols_a], xa.at[js], me.to_x())
        self.yb_copy = links.copy(held.at[js, :, 1 - y, c, :, cols_b], yb.at[js], me.to_y())
        self.ya_copy = links.copy(held.at[js, x, 1 - y, c, :, cols_a], ya.at[js], me.to_y())
        self.xb_copy = links.copy(held.at[js, 1 - x, y, c, :, cols_b], xb.at[js], me.to_x())
        self.z_copies = [
            links.copy(held.at[j, x, y, c], zb.at[me.z], (j * 2 + x, me.section), z_recv.at[me.z])
            for j in self.js
        ]

    def add(self, j, x, y, cols, value):
        c = self.me.c
        self.held[j, x, y, c, :, cols] = self.held[j, x, y, c, :, cols] + value

    def start(self):
        self.core_copy.start()

    def first(self):
        me, core = self.me, self.core
        x, y = me.x, me.y
        self.core_copy.wait_recv()
        for j in self.js:
            for i in range(2):
                self.add(j, 1 - x, i, LEFT, core[j, 1 - x, i, :, LEFT])
        self.xa_copy.start()
        for j in self.js:
            for i in range(2):
                self.add(j, i, 1 - y, RIGHT, core[j, i, 1 - y, :, RIGHT])
        self.yb_copy.start()
        for j in self.js:
            for i in range(2):
                self.add(j, x, i, LEFT, core[j, x, i, :, LEFT])
                self.add(j, i, y, RIGHT, core[j, i, y, :, RIGHT])

    def second(self):
        me = self.me
        x, y = me.x, me.y
        self.xa_copy.wait_recv()
        for j in self.js:
            self.add(j, x, 1 - y, LEFT, self.xa[j, 1 - y])
        self.ya_copy.start()
        self.yb_copy.wait_recv()
        for j in self.js:
            self.add(j, 1 - x, y, RIGHT, self.yb[j, 1 - x])
        self.xb_copy.start()
        for j in self.js:
            self.add(j, x, y, LEFT, self.xa[j, y])
            self.add(j, x, y, RIGHT, self.yb[j, x])

    def third(self):
        me = self.me
        self.ya_copy.wait_recv()
        self.xb_copy.wait_recv()
        for i, j in enumerate(self.js):
            self.add(j, me.x, me.y, LEFT, self.ya[j])
            self.add(j, me.x, me.y, RIGHT, self.xb[j])

            @pl.when(me.z != j)
            def _():
                self.z_copies[i].start()

    def drain(self):
        for copy in (self.core_copy, self.xa_copy, self.yb_copy, self.ya_copy, self.xb_copy):
            copy.wait_send()
        for i, j in enumerate(self.js):

            @pl.when(self.me.z != j)
            def _():
                self.z_copies[i].wait_send()


class Matrix:
    def __init__(self, me, links, z_recv, held, *buffers, cuts):
        self.me, self.held, self.zb = me, held, buffers[-1]
        self.units = [Scatter(me, links, held, *buffers, z_recv, j0, n) for j0, n in cuts]
        self.arrivals = [
            pltpu.make_async_remote_copy(
                src_ref=self.zb.at[i], dst_ref=self.zb.at[i], send_sem=z_recv.at[i], recv_sem=z_recv.at[i],
                device_id=(me.dp, me.section), device_id_type=MESH,
            )
            for i in range(me.nz)
        ]

    def finish(self, total):
        me = self.me
        for unit in self.units:
            unit.drain()
        total[...] = self.held[me.z, me.x, me.y, me.c].astype(F32)
        for i in range(me.nz):

            @pl.when(me.z != i)
            def _():
                self.arrivals[i].wait_recv()
                total[...] += self.zb[i].astype(F32)


def scatter_buffers(nz, width):
    shapes = [(nz, 2, 2, width, D)] + [(nz, 2, width, HALF)] * 2 + [(nz, width, HALF)] * 2
    return shapes + [(nz, width, D)]


class Gather:
    def __init__(self, me, links, wide, cols, all_wide, all_cols):
        self.me, self.all_wide, self.all_cols = me, all_wide, all_cols
        self.wide, self.cols = wide, cols
        span = cols.shape[-1] // me.n_dp
        here = (me.dp, me.y, me.c)
        self.first_copies = []
        for k in range(1, me.n_dp):
            peer = lax.rem(me.dp + k, me.n_dp)
            part = pl.ds(pl.multiple_of(peer * span, 128), span)
            self.first_copies.append(links.copy(wide, all_wide.at[here], (peer, me.section)))
            self.first_copies.append(links.copy(cols.at[:, :, part], all_cols.at[here], (peer, me.section)))
        across = (slice(None), me.y, me.c)
        self.second_copies = [links.copy(a.at[across], a.at[across], me.to_y()) for a in (all_wide, all_cols)]
        beside = (slice(None), slice(None), me.c)
        self.third_copies = [links.copy(a.at[beside], a.at[beside], me.to_c()) for a in (all_wide, all_cols)]

    def start(self):
        me = self.me
        span = self.cols.shape[-1] // me.n_dp
        for copy in self.first_copies:
            copy.start()
        self.all_wide[me.dp, me.y, me.c] = self.wide[...]
        part = pl.ds(pl.multiple_of(me.dp * span, 128), span)
        self.all_cols[me.dp, me.y, me.c] = self.cols[:, :, part]

    def second(self):
        for copy in self.first_copies:
            copy.wait()
        for copy in self.second_copies:
            copy.start()

    def third(self):
        for copy in self.second_copies:
            copy.wait()
        for copy in self.third_copies:
            copy.start()

    def finish(self):
        for copy in self.third_copies:
            copy.wait()


class Total:
    def __init__(self, me, links, acc, got):
        self.acc, self.got, self.copies = acc, got, []
        peers = [me.to_c(), me.to_y()]
        step = 1
        while step < me.n_dp:
            bit = lax.rem(me.dp // step, 2)
            peers.append((me.dp + step * (1 - 2 * bit), me.section))
            step *= 2
        for i, peer in enumerate(peers):
            self.copies.append(links.copy(acc, got.at[i], peer))

    def start(self, i):
        self.copies[i].start()

    def add(self, i):
        self.copies[i].wait()
        self.acc[...] += self.got[i]


def pick_own(me, width):
    def pick(v):
        out = v[:, :width]
        for s in range(1, 4):
            out = jnp.where(me.section == s, v[:, s * width : (s + 1) * width], out)
        return out

    return pick


N_SET = 6
CUTS = (((0, 1), (1, 2), (3, 1)), ((0, 2), (2, 2)), ((0, 2), (2, 2)))


class Net:
    def __init__(self, mats, small, wide, cols, ga_o, gm_o, scratch):
        sets = [scratch[i * N_SET : (i + 1) * N_SET] for i in range(3)]
        all_wide, all_cols, got, self.total, sends, recvs, z_recvs = scratch[3 * N_SET :]
        self.me, self.ga, self.gm, self.small = Place(), ga_o, gm_o, small
        links = Links(sends, recvs)
        self.attn, self.win, self.wout = [
            Matrix(self.me, links, z_recvs.at[m], mats[m], *sets[m], cuts=CUTS[m]) for m in range(3)
        ]
        self.gather = Gather(self.me, links, wide, cols, all_wide, all_cols)
        self.summed = Total(self.me, links, small, got)

    def cls(self):
        self.gather.finish()
        width = self.total.shape[0]
        rows = 16 * 4 * self.me.n_dp
        wide = [self.gather.all_wide[:, :, :, i].reshape(rows, D) for i in range(2)]
        cols = [self.gather.all_cols[:, :, :, i].reshape(rows, 4 * width) for i in range(2)]
        cls_grads(wide, cols, self.ga, self.gm, pick_own(self.me, width))

    def place(self, which, out):
        which.finish(self.total)
        out[...] = self.total[...].T


def bwd_kernel(
    fused,
    cot, dlead, x, small1, wide, cols, n1_i, rs1_i, n2_i, rs2_i, first_i, qkv_i, p_i, ctx_i, act_i, gp_i,
    aw, an, mw, ms,
    *refs,
):
    if fused:
        dx_o, small_o, ga_o, gm_o = refs[:4]
        refs = refs[4:]
    else:
        dx_o, small_o, dw_o = refs[:3]
        refs = refs[3:]
    w1, w2, first, n1, rs1, n2, rs2, qkv, p, ctx, act, gp, dwout, r, db, sums, wsem, osem = refs[:18]
    loads = Copies(wsem)
    for src, dst in (
        (cot, dx_o), (n2_i, n2), (rs2_i, rs2), (act_i, act), (mw.at[0, 1], w2), (gp_i, gp), (first_i, first),
        (mw.at[0, 0], w1), (n1_i, n1), (rs1_i, rs1), (ctx_i, ctx), (qkv_i, qkv), (p_i, p),
    ):
        loads.start(src, dst)
    loads = loads.all
    mats = (gp, act, dwout)
    if fused:
        net = Net(mats, small_o, wide, cols, ga_o, gm_o, refs[18:])
        attn, win, wout, summed = net.attn.units, net.win.units, net.wout.units, net.summed
        net.me.greet()
        net.gather.start()
    else:
        outs = Copies(osem)
    sums[...] = jnp.zeros_like(sums)

    def norm_step(rows, dy, n_ref, rs_ref, gain, at):
        n = n_ref[rows, :].astype(F32)
        dr = norm_back(dy, n, rs_ref[rows, :], gain)
        r[rows, :] = dr
        low = dr.astype(BF)
        db[rows, :] = low
        sums[at] += fold8(low.astype(F32))
        sums[at + 1] += fold8(dy * n)
        sums[at + 2] += fold8(dy)

    def put(ref, j, value):
        ref[j] = value.astype(BF).reshape(BLOCKS[1:])

    for i in range(3):
        loads[i].wait()

    @pl.loop(0, OWN)
    def _(g):
        for part in range(2):
            rows = pl.ds(pl.multiple_of(g * SEG + part * 64, 64), 64)
            dy = dx_o[rows, :].astype(F32)
            if part == 0:
                cls = lax.broadcasted_iota(jnp.int32, (64, D), 0) == 0
                lead = dlead[pl.ds(g, 1), :].astype(BF).astype(F32)
                dy = jnp.where(cls, lead, dy)
            norm_step(rows, dy, n2, rs2, row(ms, 0, 1), 0)

    loads[3].wait()
    for j in range(4):
        put(dwout, j, dot_tn(block(act, j), db[...]))
        if fused and j % 2 == 1:
            wout[j // 2].start()
    loads[4].wait()
    loads[5].wait()
    for j in range(4):
        low = (dot(db[...], w2[:, j * D : (j + 1) * D]) * block(gp, j).astype(F32)).astype(BF)
        put(gp, j, low)
        sums[6 + j] = fold8(low.astype(F32))
        if fused and j % 2 == 1:
            wout[j // 2].first()
    load_wq = pltpu.make_async_copy(aw.at[0], w2, wsem.at[13])
    load_wq.start()
    loads[6].wait()
    for j in range(4):
        put(act, j, dot_tn(block(gp, j), first[...]))
        if fused and j % 2 == 1:
            win[j // 2].start()
    if fused:
        wout[0].second()
        win[0].first()
        net.gather.second()
    loads[7].wait()
    for j in range(4):
        r[...] += dot_nt(block(gp, j), w1[:, j * D : (j + 1) * D])
    if fused:
        wout[1].second()
        win[1].first()
    loads[8].wait()
    loads[9].wait()

    @pl.loop(0, ROWS // 64)
    def _(i):
        rows = pl.ds(pl.multiple_of(i * 64, 64), 64)
        dy = r[rows, :].astype(BF).astype(F32)
        norm_step(rows, dy, n1, rs1, row(an, 0, 0), 3)

    loads[10].wait()
    put(gp, 3, dot_tn(db[...], ctx[...]))
    if fused:
        attn[2].start()
        wout[0].third()
    load_wq.wait()
    wq, dctx = w2, n2
    dctx[...] = dot_nt(db[...], wq[:, 3 * D :]).astype(BF)
    loads[11].wait()
    loads[12].wait()
    if fused:
        attn[2].first()
        win[0].second()

    def attention(g):
        rows = pl.ds(pl.multiple_of(g * SEG, SEG), SEG)
        for h in range(PAIRS):
            cq = slice(h * 128, (h + 1) * 128)
            ck = slice(D + h * 128, D + (h + 1) * 128)
            cv = slice(2 * D + h * 128, 2 * D + (h + 1) * 128)
            q = qkv[rows, cq]
            kc, vc = halves(qkv[rows, ck]), halves(qkv[rows, cv])
            dc = dctx[rows, cq]
            pp = p[pl.ds(pl.multiple_of(g * ROWS + h * SEG, SEG), SEG), :]
            dp = dot_nt(dc, vc)
            pf = pp.astype(F32)
            ds = []
            for i in range(2):
                c = slice(i * 128, (i + 1) * 128)
                pi, di = pf[:, c], dp[:, c]
                ds.append((pi * (di - jnp.sum(di * pi, axis=-1, keepdims=True))).astype(BF))
            ds = jnp.concatenate(ds, axis=1)
            qkv[rows, cq] = (dot(ds, kc) * 0.125).astype(BF)
            qkv[rows, ck] = (unhalve(dot_tn(ds, q)) * 0.125).astype(BF)
            qkv[rows, cv] = unhalve(dot_tn(pp, dc)).astype(BF)

    pl.loop(0, OWN // 2)(attention)
    if fused:
        wout[1].third()
        net.gather.third()
    pl.loop(OWN // 2, OWN)(attention)
    if fused:
        win[1].second()
        win[0].third()
    for j in (1, 2, 0):
        s = slice(j * D, (j + 1) * D)
        put(gp, j, dot_tn(qkv[:, s], x[...]))
        if j != 1:
            sums[10 + j // 2] = fold8(qkv[:, s].astype(F32))
        if fused and j != 1:
            attn[j // 2].start()
    for i, at in enumerate((10, 11, 3, 4, 5, 6, 7, 8, 9, 0, 1, 2)):
        small_o[i : i + 1, :] = jnp.sum(sums[at], axis=0, keepdims=True)
    small_o[12:, :] = small1[...]
    if fused:
        summed.start(0)
        attn[1].first()
        attn[0].first()
        attn[2].second()
    else:
        for i in range(3):
            outs.start(mats[i], dw_o.at[i])
    dx_o[...] = (r[...] + dot_nt(qkv[...], wq[:, : 3 * D])).astype(BF)
    if not fused:
        for copy in outs.all:
            copy.wait()
        return
    win[1].third()
    summed.add(0)
    summed.start(1)
    net.cls()
    net.place(net.wout, gm_o.at[0, 1])
    attn[1].second()
    attn[0].second()
    summed.add(1)
    summed.start(2)
    attn[2].third()
    net.place(net.win, gm_o.at[0, 0])
    summed.add(2)
    summed.start(3)
    attn[1].third()
    attn[0].third()
    summed.add(3)
    summed.start(4)
    summed.add(4)
    net.place(net.attn, ga_o.at[0])


def backward(fused, n_dp, cot, dlead, x, small1, wide, cols, kept, aw, an, mw, ms):
    width = FF // (4 * n_dp)
    if fused:
        shapes = [((ROWS, D), BF), ((32, D), F32), ((2, D, width), F32), ((2, 2, D, width), F32)]
    else:
        shapes = [((ROWS, D), BF), ((32, D), F32), ((3,) + BLOCKS, BF)]
    first, n1, rs1, n2, rs2, qkv, p, ctx, act, gp = kept
    scratch = [pltpu.VMEM((D, FF), BF)] * 2 + [pltpu.VMEM(a.shape, a.dtype) for a in kept]
    scratch += [
        pltpu.VMEM(BLOCKS, BF),
        pltpu.VMEM((ROWS, D), F32),
        pltpu.VMEM((ROWS, D), BF),
        pltpu.VMEM((12, 8, D), F32),
        pltpu.SemaphoreType.DMA((14,)),
        pltpu.SemaphoreType.DMA((3,)),
    ]
    params = {}
    if fused:
        steps = 2 + (n_dp - 1).bit_length()
        count = 5 * sum(len(cuts) for cuts in CUTS) + 3 * (n_dp // 2) + 2 * (n_dp - 1) + 4 + steps
        scratch += [pltpu.VMEM(s, BF) for s in scatter_buffers(n_dp // 2, width) * 3]
        scratch += [
            pltpu.VMEM((n_dp, 2, 2, 2, 16, D), BF),
            pltpu.VMEM((n_dp, 2, 2, 2, 16, 4 * width), BF),
            pltpu.VMEM((steps, 32, D), F32),
            pltpu.VMEM((width, D), F32),
            pltpu.SemaphoreType.DMA((count,)),
            pltpu.SemaphoreType.DMA((count,)),
            pltpu.SemaphoreType.DMA((3, n_dp // 2)),
        ]
        params = dict(collective_id=0, has_side_effects=True)
    return pl.pallas_call(
        functools.partial(bwd_kernel, fused),
        out_shape=[jax.ShapeDtypeStruct(*s) for s in shapes],
        in_specs=[ANY, VM, VM, VM, VM, VM] + [ANY] * 11 + [VM, ANY, VM],
        out_specs=[VM] * 4 if fused else [VM, VM, ANY],
        scratch_shapes=scratch,
        compiler_params=pltpu.CompilerParams(vmem_limit_bytes=63 * 2**20, **params),
    )(cot, dlead, x, small1, wide, cols, n1, rs1, n2, rs2, first, qkv, p, ctx, act, gp, aw, an, mw, ms)


def swap_half(v):
    size = lax.axis_size("section")
    per_micro = size // MICRO
    return lax.ppermute(v, "section", [(i, i - i % per_micro + (i + 1) % per_micro) for i in range(size)])


def on_device(tokens, counts, aw, ab, an, mw, mb, ms, embed, cot):
    cls_cot = jnp.pad(cot.reshape(OWN, SEG, D)[:, 0].astype(F32), ((0, 2), (0, 0)))
    cls_cot_other = swap_half(cls_cot)
    second, first, n1, rs1, n2, rs2, qkv, p, ctx, act, gp, cls = forward(tokens, aw, ab, an, mw, mb, ms)
    fourth, dlead, cols, wide, small1 = cls_chain(
        cls, swap_half(cls), cls_cot, cls_cot_other, counts, aw, ab, an, mw, mb, ms, embed
    )
    encoded = second.reshape(OWN, SEG, D).at[:, 0].set(fourth[:OWN].astype(BF)).reshape(ROWS, D)
    n_dp, n_section = lax.axis_size("dp"), lax.axis_size("section")
    kept = (first, n1, rs1, n2, rs2, qkv, p, ctx, act, gp)
    args = (cot, dlead, tokens, small1, wide, cols, kept, aw, an, mw, ms)
    if (n_dp // 2, 2, 2, 2, FF // (n_dp * n_section), D) == BLOCKS and n_section == 4:
        dx, small, ga, gm = backward(True, n_dp, *args)
    else:
        dx, small, dw = backward(False, n_dp, *args)
        cols = lax.all_to_all(cols, BOTH, split_axis=2, concat_axis=1, tiled=True)
        wide = lax.all_gather(wide, BOTH, axis=1, tiled=True)
        red = lax.psum_scatter(dw.reshape(3, FF, D), BOTH, scatter_dimension=1, tiled=True)
        small = lax.psum(small, BOTH)
        ga, gm = place(red, cols, wide)
    return (
        encoded,
        dx,
        ga,
        jnp.stack([small[0:3], small[12:15]]),
        jnp.stack([small[3:5], small[15:17]]),
        gm,
        jnp.stack([small[5:9].reshape(FF), small[17:21].reshape(FF)]),
        jnp.stack([small[9:12], small[21:24]]),
        small[24:32],
    )


def solution(mesh):
    return jax.shard_map(
        on_device,
        mesh=mesh,
        in_specs=(P(BOTH, None), P("dp", None)) + (P(),) * 7 + (P(BOTH, None),),
        out_specs=(
            P(BOTH, None),
            P(BOTH, None),
            P(None, None, BOTH),
            P(),
            P(),
            P(None, None, None, BOTH),
            P(),
            P(),
            P(),
        ),
        check_vma=False,
    )
```

```python
import functools
import itertools

import jax
import jax.numpy as jnp
from jax import lax
from jax.experimental import pallas as pl
from jax.experimental.pallas import tpu as pltpu
from jax.sharding import PartitionSpec as P

F32 = jnp.float32
BF = jnp.bfloat16
D = 768
FF = 3072
SEG = 128
HEAD = 64
HEADS = 12
PAIRS = 6
MICRO = 2
SEGS = 12
OWN = 6
ROWS = OWN * SEG
BLOCKS = (4, 2, 2, 2, 96, D)
BOTH = ("dp", "section")
MASKED = -1e30
VM = pl.BlockSpec(memory_space=pltpu.VMEM)
SM = pl.BlockSpec(memory_space=pltpu.SMEM)
ANY = pl.BlockSpec(memory_space=pl.ANY)
MESH = pl.DeviceIdType.MESH


def dot(a, b):
    return jnp.dot(a, b, preferred_element_type=F32)


def dot_nt(a, b):
    return lax.dot_general(a, b, (((1,), (1,)), ((), ())), preferred_element_type=F32)


def dot_tn(a, b):
    return lax.dot_general(a, b, (((0,), (0,)), ((), ())), preferred_element_type=F32)


def gelu_parts(h):
    phi = 0.5 + 0.5 * lax.erf(h * 0.7071067811865476)
    return h * phi, phi + h * (0.3989422804014327 * jnp.exp2((h * h) * -0.7213475204444817))


def norm_rows(r):
    center = r - jnp.mean(r, axis=-1, keepdims=True)
    rstd = lax.rsqrt(jnp.mean(center * center, axis=-1, keepdims=True) + 1e-5)
    return center * rstd, rstd


def norm_back(dy, n, rstd, gain):
    dyg = dy * gain
    return (
        dyg
        - jnp.mean(dyg, axis=-1, keepdims=True)
        - n * jnp.mean(dyg * n, axis=-1, keepdims=True)
    ) * rstd


def halves(v):
    lane = lax.broadcasted_iota(jnp.int32, v.shape, 1)
    zero = jnp.zeros_like(v)
    return jnp.concatenate([jnp.where(lane < HEAD, v, zero), jnp.where(lane < HEAD, zero, v)], 0)


def unhalve(v):
    top, bottom = v[:SEG], v[SEG:]
    lane = lax.broadcasted_iota(jnp.int32, top.shape, 1)
    return jnp.where(lane < HEAD, top, bottom)


def fold8(v):
    return jnp.sum(v.reshape(v.shape[0] // 8, 8, v.shape[1]), axis=0)


def pair_rows(g, h):
    start = (g * PAIRS + h) * 2 * SEG
    return slice(start, start + 2 * SEG)


def block(ref, j):
    return ref[j].reshape(D, D)


def row(ref, *idx):
    if isinstance(ref, tuple):
        return row(ref[idx[0] // 6], idx[0] % 3, idx[0] // 3 % 2)
    i = idx[-1]
    return ref[idx[:-1] + (slice(i, i + 1), slice(None))].astype(F32)


class Copies:
    def __init__(self, sems):
        self.sems, self.all = sems, []

    def start(self, src, dst):
        copy = pltpu.make_async_copy(src, dst, self.sems.at[len(self.all)])
        copy.start()
        self.all.append(copy)
        return copy


def cls_chain(
    own, other, counts, wq, w1, w2, par, an, mb, embed, cols_o, wide_o, small_o
):
    section = lax.axis_index("section")
    per_micro = lax.axis_size("section") // MICRO
    half = lax.rem(section, per_micro)
    micro = section // per_micro
    ends = [counts[micro, 0], counts[micro, 0] + counts[micro, 1]]

    def layout(shape, axis):
        r = lax.broadcasted_iota(jnp.int32, shape, axis)
        seg = jnp.where(r < 8, r, r - 2)
        valid = (r < 6) | ((r >= 8) & (r < 14))
        doc = jnp.where(seg >= ends[0], 1, 0) + jnp.where(seg >= ends[1], 1, 0)
        start = jnp.where(doc == 0, 0, jnp.where(doc == 1, ends[0], ends[1]))
        pos = jnp.where(valid, seg - start, -1)
        return jnp.where(valid, doc, jnp.where(r < 16, 100 + r, -1)), pos, valid

    def order(a, b):
        first = half == 0
        return jnp.concatenate([jnp.where(first, a, b), jnp.where(first, b, a)], axis=0)

    def mine(v):
        return jnp.where(half == 0, v[:8], v[8:])

    doc_q, pos, valid = layout((16, 128), 0)
    doc_k, _, _ = layout((16, 128), 1)
    allowed = jnp.concatenate([doc_q == doc_k] * HEADS, axis=0)
    lanes8 = lax.broadcasted_iota(jnp.int32, (16, 8), 1)
    onehot = (pos[:, :8] == lanes8).astype(BF)
    leaders = order(own[0], other[0]) + dot(onehot, embed[...])
    low = leaders.astype(BF)
    lane = lax.broadcasted_iota(jnp.int32, (16, D), 1) // HEAD

    def stack(v):
        return jnp.concatenate([jnp.where(lane == h, v, jnp.zeros_like(v)) for h in range(HEADS)], 0)

    def unstack(v):
        total = jnp.where(lane == 0, v[:16], 0.0)
        for h in range(1, HEADS):
            total = total + jnp.where(lane == h, v[h * 16 : (h + 1) * 16], 0.0)
        return total

    def deep(v):
        return jnp.concatenate([v, jnp.zeros((112, D), BF)], axis=0)

    q = (dot(low, block(wq, 0)) + row(par, 3)).astype(BF)
    k = dot(low, block(wq, 1)).astype(BF)
    v = (dot(low, block(wq, 2)) + row(par, 4)).astype(BF)
    qs, kd, vd = stack(q), deep(k), deep(v)
    scores = jnp.where(allowed, dot_nt(qs, kd) * 0.125, MASKED)
    e = jnp.exp(scores - jnp.max(scores, axis=-1, keepdims=True))
    probs = e / jnp.sum(e, axis=-1, keepdims=True)
    probs_low = probs.astype(BF)
    ctx = unstack(dot(probs_low, vd)).astype(BF)
    n1, rs1 = norm_rows(leaders + dot(ctx, block(wq, 3)) + row(par, 5))
    third = (n1 * row(an, 1, 0) + row(an, 1, 1)).astype(BF)
    act, gp, v = [], [], third.astype(F32) + row(par, 9)
    for j in range(4):
        a, g = gelu_parts(dot(third, block(w1, j)) + mb[1:2, j * D : (j + 1) * D].astype(F32))
        act.append(a.astype(BF))
        gp.append(g)
        v = v + dot_nt(act[j], block(w2, j))
    n2, rs2 = norm_rows(v)
    fourth = mine(n2 * row(par, 10) + row(par, 11))

    dy = order(own[1], other[1])
    small_o[22] = jnp.sum(mine(dy * n2), axis=0, keepdims=True)
    small_o[23] = jnp.sum(mine(dy), axis=0, keepdims=True)
    dr = norm_back(dy, n2, rs2, row(par, 10))
    dbf = dr.astype(BF)
    small_o[21] = jnp.sum(mine(dbf.astype(F32)), axis=0, keepdims=True)
    dthird = dr
    for j in range(4):
        dh = (dot(dbf, block(w2, j)) * gp[j]).astype(BF)
        dh_mine = mine(dh.astype(F32))
        small_o[17 + j] = jnp.sum(dh_mine, axis=0, keepdims=True)
        cols_o[0, :, j * D : (j + 1) * D] = dh
        cols_o[1, :, j * D : (j + 1) * D] = act[j]
        dthird = dthird + dot_nt(dh, block(w1, j))
    dthird = dthird.astype(BF).astype(F32)
    small_o[15] = jnp.sum(mine(dthird * n1), axis=0, keepdims=True)
    small_o[16] = jnp.sum(mine(dthird), axis=0, keepdims=True)
    dr = norm_back(dthird, n1, rs1, row(an, 1, 0))
    dba = dr.astype(BF)
    small_o[14] = jnp.sum(mine(dba.astype(F32)), axis=0, keepdims=True)
    dctx = stack(dot_nt(dba, block(wq, 3)).astype(BF))
    dp = dot_nt(dctx, vd)
    dv = dot_tn(probs_low, dctx)[:16].astype(BF)
    ds = (probs * (dp - jnp.sum(dp * probs, axis=-1, keepdims=True))).astype(BF)
    dq = (unstack(dot(ds, kd)) * 0.125).astype(BF)
    dk = (dot_tn(ds, qs)[:16] * 0.125).astype(BF)
    small_o[12] = jnp.sum(mine(dq.astype(F32)), axis=0, keepdims=True)
    small_o[13] = jnp.sum(mine(dv.astype(F32)), axis=0, keepdims=True)
    dlead = dr
    for j, piece in enumerate((dq, dk, dv)):
        dlead = dlead + dot_nt(piece, block(wq, j))
    dlead_mine = mine(dlead)
    pos_mine = jnp.where(half == 0, pos[:8], pos[8:])
    for i in range(8):
        hit = jnp.where(pos_mine[:, 0:1] == i, dlead_mine, 0.0)
        small_o[24 + i] = jnp.sum(hit, axis=0, keepdims=True)
    for j, piece in enumerate((dq, dk, dv, dba)):
        cols_o[2, :, j * D : (j + 1) * D] = piece
    for j, piece in enumerate((third, dbf, low, ctx)):
        wide_o[j] = piece
    return fourth, dlead_mine


class Place:
    def __init__(self):
        self.dp, self.section = lax.axis_index("dp"), lax.axis_index("section")
        self.n_dp, self.n_section = lax.axis_size("dp"), lax.axis_size("section")
        self.nz = self.n_dp // 2
        self.z, self.x = self.dp // 2, lax.rem(self.dp, 2)
        self.y, self.c = self.section // 2, lax.rem(self.section, 2)

    def at(self, dz=0, x=None, y=None, c=None):
        x = self.x if x is None else x
        y = self.y if y is None else y
        c = self.c if c is None else c
        return ((self.z + dz) * 2 + x, y * 2 + c)

    def to_x(self):
        return self.at(x=1 - self.x)

    def to_y(self):
        return self.at(y=1 - self.y)

    def to_c(self):
        return self.at(c=1 - self.c)

    def device(self, index):
        return (index // self.n_section, lax.rem(index, self.n_section))


class Links:
    def __init__(self, sends, recvs):
        self.sends, self.recvs, self.used = sends, recvs, 0

    def copy(self, src, dst, peer, recv=None):
        i = self.used
        self.used += 1
        return pltpu.make_async_remote_copy(
            src_ref=src, dst_ref=dst, send_sem=self.sends.at[i], recv_sem=self.recvs.at[i] if recv is None else recv,
            device_id=peer, device_id_type=MESH,
        )


HALF = D // 2
LEFT, RIGHT = slice(0, HALF), slice(HALF, D)


class Scatter:
    def __init__(self, me, links, held, core, xa, yb, ya, xb, zb, z_recv, j0, count):
        self.me, self.held, self.js = me, held, range(j0, j0 + count)
        self.core, self.xa, self.yb, self.ya, self.xb = core, xa, yb, ya, xb
        x, y, c = me.x, me.y, me.c
        js, cols_a, cols_b = pl.ds(j0, count), pl.ds(0, HALF), pl.ds(HALF, HALF)
        self.core_copy = links.copy(held.at[js, :, :, 1 - c], core.at[js], me.to_c())
        self.xa_copy = links.copy(held.at[js, 1 - x, :, c, :, cols_a], xa.at[js], me.to_x())
        self.yb_copy = links.copy(held.at[js, :, 1 - y, c, :, cols_b], yb.at[js], me.to_y())
        self.ya_copy = links.copy(held.at[js, x, 1 - y, c, :, cols_a], ya.at[js], me.to_y())
        self.xb_copy = links.copy(held.at[js, 1 - x, y, c, :, cols_b], xb.at[js], me.to_x())
        self.z_copies = [
            links.copy(held.at[j, x, y, c], zb.at[me.z], (j * 2 + x, me.section), z_recv.at[me.z])
            for j in self.js
        ]

    def add(self, j, x, y, cols, value):
        c = self.me.c
        self.held[j, x, y, c, :, cols] = self.held[j, x, y, c, :, cols] + value

    def start(self):
        self.core_copy.start()

    def first(self):
        me, core = self.me, self.core
        x, y = me.x, me.y
        self.core_copy.wait_recv()
        for j in self.js:
            for i in range(2):
                self.add(j, 1 - x, i, LEFT, core[j, 1 - x, i, :, LEFT])
        self.xa_copy.start()
        for j in self.js:
            for i in range(2):
                self.add(j, i, 1 - y, RIGHT, core[j, i, 1 - y, :, RIGHT])
        self.yb_copy.start()
        for j in self.js:
            for i in range(2):
                self.add(j, x, i, LEFT, core[j, x, i, :, LEFT])
                self.add(j, i, y, RIGHT, core[j, i, y, :, RIGHT])

    def second(self):
        me = self.me
        x, y = me.x, me.y
        self.xa_copy.wait_recv()
        for j in self.js:
            self.add(j, x, 1 - y, LEFT, self.xa[j, 1 - y])
        self.ya_copy.start()
        self.yb_copy.wait_recv()
        for j in self.js:
            self.add(j, 1 - x, y, RIGHT, self.yb[j, 1 - x])
        self.xb_copy.start()
        for j in self.js:
            self.add(j, x, y, LEFT, self.xa[j, y])
            self.add(j, x, y, RIGHT, self.yb[j, x])

    def third(self):
        me = self.me
        self.ya_copy.wait_recv()
        self.xb_copy.wait_recv()
        for i, j in enumerate(self.js):
            self.add(j, me.x, me.y, LEFT, self.ya[j])
            self.add(j, me.x, me.y, RIGHT, self.xb[j])

            @pl.when(me.z != j)
            def _():
                self.z_copies[i].start()

    def drain(self):
        for copy in (self.core_copy, self.xa_copy, self.yb_copy, self.ya_copy, self.xb_copy):
            copy.wait_send()
        for i, j in enumerate(self.js):

            @pl.when(self.me.z != j)
            def _():
                self.z_copies[i].wait_send()


class Matrix:
    def __init__(self, me, links, z_recv, held, *buffers, cuts):
        self.me, self.held, self.zb = me, held, buffers[-1]
        self.units = [Scatter(me, links, held, *buffers, z_recv, j0, n) for j0, n in cuts]
        self.arrivals = [
            pltpu.make_async_remote_copy(
                src_ref=self.zb.at[i], dst_ref=self.zb.at[i], send_sem=z_recv.at[i], recv_sem=z_recv.at[i],
                device_id=(me.dp, me.section), device_id_type=MESH,
            )
            for i in range(me.nz)
        ]

    def finish(self, total):
        me = self.me
        for unit in self.units:
            unit.drain()
        total[...] = self.held[me.z, me.x, me.y, me.c].astype(F32)
        for i in range(me.nz):

            @pl.when(me.z != i)
            def _():
                self.arrivals[i].wait_recv()
                total[...] += self.zb[i].astype(F32)


def scatter_buffers(nz, width):
    shapes = [(nz, 2, 2, width, D)] + [(nz, 2, width, HALF)] * 2 + [(nz, width, HALF)] * 2
    return shapes + [(nz, width, D)]


class Gather:
    def __init__(self, me, links, wide, cols, all_wide, all_cols):
        self.me, self.all_wide, self.all_cols = me, all_wide, all_cols
        self.wide, self.cols = wide, cols
        self.span = cols.shape[-1] // me.n_dp
        self.copies = [[], [], []]
        for c in range(2):
            w, k = (pl.ds(0, 2), pl.ds(0, 1)) if c == 0 else (pl.ds(2, 1), pl.ds(1, 2))
            given = [wide.at[me.y, pl.ds(2 * c, 2)], cols.at[me.y, k]]
            self.copies[0].append([links.copy(a, a, me.to_y()) for a in given])
            spread = []
            for i in range(1, me.n_dp):
                peer = lax.rem(me.dp + i, me.n_dp)
                spread.append(links.copy(self.given(c, peer), all_wide.at[me.dp, :, w], (peer, me.section)))
                spread.append(links.copy(self.part(k, peer), all_cols.at[me.dp, :, k], (peer, me.section)))
            self.copies[1].append(spread)
            beside = [all_wide.at[:, :, w], all_cols.at[:, :, k]]
            self.copies[2].append([links.copy(a, a, me.to_c()) for a in beside])

    def given(self, c, peer):
        if c == 0:
            return self.wide.at[:, pl.ds(0, 2)]
        return self.wide.at[:, pl.ds(2 + peer * self.span // (3 * D), 1)]

    def part(self, k, peer):
        return self.cols.at[:, k, :, pl.ds(pl.multiple_of(peer * self.span, 128), self.span)]

    def each(self, do):
        for c in range(2):

            @pl.when(self.me.c == c)
            def _():
                do(c)

    def start(self):
        def go(c):
            for copy in self.copies[0][c]:
                copy.start()

        self.each(go)

    def second(self):
        me = self.me

        def go(c):
            for copy in self.copies[0][c]:
                copy.wait()
            for copy in self.copies[1][c]:
                copy.start()
            w, k = (slice(0, 2), slice(0, 1)) if c == 0 else (slice(2, 3), slice(1, 3))
            self.all_wide[me.dp, :, w] = self.given(c, me.dp)[...]
            self.all_cols[me.dp, :, k] = self.part(pl.ds(k.start, k.stop - k.start), me.dp)[...]

        self.each(go)

    def third(self):
        def go(c):
            for copy in self.copies[1][c]:
                copy.wait()
            for copy in self.copies[2][c]:
                copy.start()

        self.each(go)

    def finish(self):
        def go(c):
            for copy in self.copies[2][c]:
                copy.wait_send()
            for copy in self.copies[2][1 - c]:
                copy.wait_recv()

        self.each(go)


class Total:
    def __init__(self, me, acc, got, out, sems):
        self.me, self.acc, self.got, self.out, self.sems = me, acc, got, out, sems
        self.count = acc.shape[0]
        self.index = me.dp * me.n_section + me.section

    def send(self, phase):
        @pl.loop(1, self.count)
        def _(i):
            peer = lax.rem(self.index + i, self.count)
            src = self.acc.at[peer] if phase == 0 else self.out.at[self.index]
            dst = (self.got if phase == 0 else self.out).at[self.index]
            pltpu.make_async_remote_copy(
                src_ref=src, dst_ref=dst, send_sem=self.sems.at[2 * phase], recv_sem=self.sems.at[2 * phase + 1],
                device_id=self.me.device(peer), device_id_type=MESH,
            ).start()

    def wait(self, phase):
        rows = self.got.at[pl.ds(0, self.count - 1)]
        for i in range(2):
            pltpu.make_async_copy(rows, rows, self.sems.at[2 * phase + i]).wait()

    def step(self, i):
        if i == 0:
            self.got[self.index] = self.acc[self.index]
            self.send(0)
        elif i == 1:
            self.wait(0)
            self.out[self.index] = jnp.sum(self.got[...], axis=0)
            self.send(1)
        else:
            self.wait(1)


def pick_own(me, width):
    def pick(v):
        out = v[:, :width]
        for s in range(1, 4):
            out = jnp.where(me.section == s, v[:, s * width : (s + 1) * width], out)
        return out

    return pick


N_SET = 6
BLOCK_ORDER = (1, 2, 0, 3)
QKV_ORDER = (0, 1, 2)
PLAN = {
    "ffnout0": (
        ("g", 0, 0),
    ),
    "dwout1": (
        ("o", 1, 0),
    ),
    "dwout2": (
        ("o", 2, 0),
    ),
    "dwout0": (
        ("o", 0, 0),
    ),
    "dwout3": (
        ("o", 3, 0),
    ),
    "dh0": (
        ("o", 1, 1),
    ),
    "dh3": (
        ("o", 2, 1),
    ),
    "dwin1": (
        ("i", 1, 0),
    ),
    "dwin2": (
        ("i", 2, 0),
        ("o", 0, 1),
    ),
    "dwin0": (
        ("i", 0, 0),
    ),
    "dwin3": (
        ("i", 3, 0),
        ("o", 1, 2),
    ),
    "dfirst0": (
        ("o", 2, 2),
    ),
    "dfirst1": (
        ("o", 3, 1),
        ("f", 0, 0),
    ),
    "dwo": (
        ("f", 0, 1),
        ("a", 3, 0),
        ("o", 0, 2),
        ("g", 1, 0),
    ),
    "dctx": (
        ("o", 1, 3),
        ("i", 1, 1),
        ("o", 2, 3),
    ),
    "att1": (
        ("g", 2, 0),
        ("o", 3, 2),
    ),
    "att2": (
        ("o", 0, 3),
        ("i", 2, 1),
    ),
    "att4": (
        ("i", 1, 2),
    ),
    "att5": (
        ("o", 3, 3),
        ("i", 0, 1),
    ),
    "dwqkv0": (
        ("a", 0, 0),
    ),
    "dwqkv1": (
        ("a", 1, 0),
        ("i", 2, 2),
    ),
    "dwqkv2": (
        ("a", 2, 0),
        ("i", 3, 1),
        ("i", 1, 3),
    ),
    "sums": (
        ("s", 0, 0),
        ("i", 0, 2),
    ),
    "dx0": (
        ("i", 2, 3),
    ),
    "dx1": (
        ("a", 3, 1),
    ),
    "tail": (
        ("i", 3, 2),
        ("p", 3, 0),
        ("a", 0, 1),
        ("i", 0, 3),
        ("a", 1, 1),
        ("a", 3, 2),
        ("s", 1, 0),
        ("i", 3, 3),
        ("a", 0, 2),
        ("a", 2, 1),
        ("a", 1, 2),
        ("a", 3, 3),
        ("a", 0, 3),
        ("a", 2, 2),
        ("p", 2, 0),
        ("s", 2, 0),
        ("a", 1, 3),
        ("a", 2, 3),
        ("p", 0, 0),
    ),
}


def cls_grads(wide, cols, put, pick):
    for i, k in enumerate((4, 5, 1)):
        put(k, dot_tn(pick(cols[i]), wide[i]))


class Net:
    def __init__(self, mats, acc, out, wide, cols, grads, scratch):
        sets = [scratch[i * N_SET : (i + 1) * N_SET] for i in range(3)]
        sets[0] = sets[2][:1] + sets[0][1:]
        all_wide, all_cols, got, self.stage, sends, recvs, z_recvs, self.free, self.out_sems, sum_sems = scratch[3 * N_SET :]
        self.outs = []
        self.me, self.grads = Place(), grads
        links = Links(sends, recvs)
        self.attn, self.win, self.wout = [
            Matrix(self.me, links, z_recvs.at[m], mats[m], *sets[m], cuts=[(j, 1) for j in range(4)]) for m in range(3)
        ]
        self.gather = Gather(self.me, links, wide, cols, all_wide, all_cols)
        self.summed = Total(self.me, acc, got, out, sum_sems)

    def slot(self):
        i = len(self.outs)
        if i >= 2:
            self.outs[i - 2].wait()
        return self.stage.at[i % 2]

    def put(self, k):
        i = len(self.outs)
        copy = pltpu.make_async_copy(self.stage.at[i % 2], self.grads.at[k], self.out_sems.at[i % 2])
        copy.start()
        self.outs.append(copy)

    def cls(self):
        self.gather.finish()
        width = self.stage.shape[1]
        rows = 16 * 2 * self.me.n_dp
        wide = [self.gather.all_wide[:, :, i].reshape(rows, D) for i in range(3)]
        cols = [self.gather.all_cols[:, :, i].reshape(rows, 4 * width) for i in range(3)]

        def put(k, value):
            self.slot()[...] = value
            self.put(k)

        cls_grads(wide, cols, put, pick_own(self.me, width))

    def place(self, which, k):
        which.finish(self.slot())
        self.put(k)

    def after(self, name):
        kinds = {"a": self.attn.units, "i": self.win.units, "o": self.wout.units}
        for step in PLAN.get(name, ()):
            kind, number, phase = step
            if kind == "g":
                (self.gather.second, self.gather.third, self.cls)[number]()
            elif kind == "s":
                self.summed.step(number)
            elif kind == "p":
                self.place((self.attn, None, self.win, self.wout)[number], number)
            elif kind == "f":
                if phase == 0:
                    pl.semaphore_signal(self.free, inc=1, device_id=self.me.to_c(), device_id_type=MESH)
                else:
                    pl.semaphore_wait(self.free, 1)
            else:
                unit = kinds[kind][number]
                (unit.start, unit.first, unit.second, unit.third)[phase]()


def layer_kernel(fused, x, cot, counts, ab, ms, an, mb, embed, aw, mw, enc_o, dx_o, small_o, *refs):
    par = (ab, ms)
    if fused:
        grads_o, refs = refs[0], refs[1:]
    else:
        dw_o, refs = refs[0], refs[1:]
    cols, wide, a0, win0, wout0, a1, v1, v2, first, n1, db, rs1, qkv, p, ctx = refs[:15]
    heads, rows16, mine, theirs, sums, wsem, osem, ssem, rsem = refs[15:24]
    act, gp, dwout = v1, v2, a1
    mats = (gp, act, dwout)
    section = lax.axis_index("section")
    partner = (lax.axis_index("dp"), section + 1 - 2 * lax.rem(section, 2))
    barrier = pltpu.get_barrier_semaphore()
    if fused:
        small, refs = refs[24], refs[:24] + refs[25:]
        net = Net(mats, small, small_o, wide, cols, grads_o, refs[24:])
        expected = net.me.n_dp * net.me.n_section - 1

        @pl.loop(1, expected + 1)
        def _(i):
            peer = net.me.device(lax.rem(net.summed.index + i, expected + 1))
            pl.semaphore_signal(barrier, inc=1, device_id=peer, device_id_type=MESH)
    else:
        small, expected = small_o, 1
        pl.semaphore_signal(barrier, inc=1, device_id=partner, device_id_type=MESH)

    def after(name):
        if fused:
            net.after(name)

    swaps = [
        pltpu.make_async_remote_copy(
            src_ref=mine.at[i], dst_ref=theirs.at[i], send_sem=ssem.at[i], recv_sem=rsem.at[i],
            device_id=partner, device_id_type=MESH,
        )
        for i in range(2)
    ]

    loads = Copies(wsem)

    def load(src, dst):
        return [loads.start(src.at[:, :, :, :, j * D : (j + 1) * D], dst.at[j]) for j in range(4)]

    a0_in = load(aw.at[0], a0)
    heads_in = [loads.start(cot.at[pl.ds(g * SEG, 16)], heads.at[g]) for g in range(OWN)]
    win0_in, wout0_in = load(mw.at[0, 0], win0), load(mw.at[0, 1], wout0)
    cls_in = load(aw.at[1], a1) + load(mw.at[1, 0], v1) + load(mw.at[1, 1], v2)
    cot_in = loads.start(cot, db)

    for j in range(3):
        a0_in[j].wait()
        v = dot(x[...], block(a0, j))
        if j != 1:
            v = v + row(par, j // 2)
        qkv[:, j * D : (j + 1) * D] = v.astype(BF)
    for g, h in itertools.product(range(OWN), range(PAIRS)):
        rows, c = slice(g * SEG, (g + 1) * SEG), slice(h * 128, (h + 1) * 128)
        q = qkv[rows, c] * jnp.asarray(0.125, BF)
        kc = halves(qkv[rows, D + h * 128 : D + (h + 1) * 128])
        vc = halves(qkv[rows, 2 * D + h * 128 : 2 * D + (h + 1) * 128])
        scores = dot_nt(kc, q)
        ps = []
        for i in range(2):
            si = scores[i * SEG : (i + 1) * SEG]
            e = jnp.exp(si - jnp.max(si, axis=0, keepdims=True))
            ps.append((e / jnp.sum(e, axis=0, keepdims=True)).astype(BF))
        pt = jnp.concatenate(ps, axis=0)
        p[pair_rows(g, h), :] = pt
        ctx[rows, c] = dot_tn(pt, vc).astype(BF)

    mine[...] = jnp.zeros_like(mine)
    rows16[...] = jnp.zeros_like(rows16)
    for copy in heads_in:
        copy.wait()
    for g in range(OWN):
        mine[1, g : g + 1, :] = heads[g, 0:1, :].astype(F32)
        rows16[0, g : g + 1, :] = x[g * SEG : g * SEG + 1, :].astype(F32)
        rows16[1, g : g + 1, :] = ctx[g * SEG : g * SEG + 1, :].astype(F32)
    pl.semaphore_wait(barrier, expected)
    swaps[1].start()
    a0_in[3].wait()
    n, _ = norm_rows(rows16[0] + dot(rows16[1].astype(BF), block(a0, 3)) + row(par, 2))
    low = (n * row(an, 0, 0) + row(an, 0, 1)).astype(BF)
    v = low.astype(F32) + row(par, 6)
    for j in range(4):
        win0_in[j].wait()
        wout0_in[j].wait()
        a, _ = gelu_parts(dot(low, block(win0, j)) + mb[0:1, j * D : (j + 1) * D].astype(F32))
        v = v + dot_nt(a.astype(BF), block(wout0, j))
    n, _ = norm_rows(v)
    value = (n * row(par, 7) + row(par, 8)).astype(BF).astype(F32)
    mine[0] = jnp.where(lax.broadcasted_iota(jnp.int32, (8, D), 0) < OWN, value[:8], 0.0)
    swaps[0].start()
    for copy in cls_in:
        copy.wait()
    for swap in swaps:
        swap.wait()
    if fused:
        cols_o, wide_o = cols.at[net.me.y], wide.at[net.me.y]
    else:
        cols_o, wide_o = cols, wide
    fourth, dlead = cls_chain(mine, theirs, counts, a1, v1, v2, par, an, mb, embed, cols_o, wide_o, small)
    lead = dlead.astype(BF).astype(F32)
    if fused:
        net.gather.start()

    for half in range(2):
        rows = slice(half * 384, half * 384 + 384)
        v = dot(ctx[rows, :], block(a0, 3)) + x[rows, :].astype(F32) + row(par, 2)
        n, rs = norm_rows(v)
        n1[rows, :] = n.astype(BF)
        rs1[rows, :] = rs
        first[rows, :] = (n * row(an, 0, 0) + row(an, 0, 1)).astype(BF)
    after("out")
    for j in range(4):
        a, g = gelu_parts(dot(first[...], block(win0, j)) + mb[0:1, j * D : (j + 1) * D].astype(F32))
        act[j] = a.astype(BF).reshape(BLOCKS[1:])
        gp[j] = g.astype(BF).reshape(BLOCKS[1:])
        after(f"ffnin{j}")

    def norm_step(rows, dy, n, rs, gain, at):
        low = norm_back(dy, n, rs, gain).astype(BF)
        db[rows, :] = low
        for i, v in enumerate((low.astype(F32), dy * n, dy)):
            sums[at + i] = fold8(v) if rows.start == 0 else sums[at + i] + fold8(v)

    def put(ref, j, value):
        ref[j] = value.astype(BF).reshape(BLOCKS[1:])

    cot_in.wait()
    at = lax.broadcasted_iota(jnp.int32, (384, D), 0)
    for half in range(2):
        rows = slice(half * 384, half * 384 + 384)
        v = first[rows, :].astype(F32) + row(par, 6)
        for j in range(4):
            v = v + dot_nt(act[j, half].reshape(384, D), block(wout0, j))
        n, rs = norm_rows(v)
        value, dy = n * row(par, 7) + row(par, 8), db[rows, :].astype(F32)
        for g in range(3):
            value = jnp.where(at == g * SEG, fourth[3 * half + g : 3 * half + g + 1], value)
            dy = jnp.where(at == g * SEG, lead[3 * half + g : 3 * half + g + 1], dy)
        dwout[2, half] = value.astype(BF).reshape(BLOCKS[2:])
        norm_step(rows, dy, n, rs, row(par, 7), 0)
        after(f"ffnout{half}")
    enc_out = pltpu.make_async_copy(dwout.at[2], enc_o, osem.at[0])
    enc_out.start()

    for j in BLOCK_ORDER:
        if j == 2:
            enc_out.wait()
        put(dwout, j, dot_tn(block(act, j), db[...]))
        after(f"dwout{j}")
    for j in range(4):
        low = (dot(db[...], block(wout0, j)) * block(gp, j).astype(F32)).astype(BF)
        put(gp, j, low)
        sums[6 + j] = fold8(low.astype(F32))
        after(f"dh{j}")
    for j in BLOCK_ORDER:
        put(act, j, dot_tn(block(gp, j), first[...]))
        after(f"dwin{j}")
    for half in range(2):
        rows = slice(half * 384, half * 384 + 384)
        v = db[rows, :].astype(F32)
        for j in range(4):
            v = v + dot_nt(gp[j, half].reshape(384, D), block(win0, j))
        norm_step(rows, v.astype(BF).astype(F32), n1[rows, :].astype(F32), rs1[rows, :], row(an, 0, 0), 3)
        after(f"dfirst{half}")

    put(gp, 3, dot_tn(db[...], ctx[...]))
    after("dwo")
    dctx = first
    dctx[...] = dot_nt(db[...], block(a0, 3)).astype(BF)
    after("dctx")

    def attention(g):
        rows = slice(g * SEG, (g + 1) * SEG)
        for h in range(PAIRS):
            cq = slice(h * 128, (h + 1) * 128)
            ck = slice(D + h * 128, D + (h + 1) * 128)
            cv = slice(2 * D + h * 128, 2 * D + (h + 1) * 128)
            q, dc, pt = qkv[rows, cq], dctx[rows, cq], p[pair_rows(g, h), :]
            kc, vc = halves(qkv[rows, ck]), halves(qkv[rows, cv])
            dp, pf = dot_nt(vc, dc), pt.astype(F32)
            ds = []
            for i in range(2):
                pi, di = pf[i * SEG : (i + 1) * SEG], dp[i * SEG : (i + 1) * SEG]
                ds.append((pi * (di - jnp.sum(pi * di, axis=0, keepdims=True))).astype(BF))
            ds = jnp.concatenate(ds, axis=0)
            qkv[rows, cq] = (dot_tn(ds, kc) * 0.125).astype(BF)
            qkv[rows, ck] = (unhalve(dot(ds, q)) * 0.125).astype(BF)
            qkv[rows, cv] = unhalve(dot(pt, dc)).astype(BF)

    for g in range(OWN):
        attention(g)
        after(f"att{g}")
    for j in QKV_ORDER:
        s = slice(j * D, (j + 1) * D)
        put(gp, j, dot_tn(qkv[:, s], x[...]))
        if j != 1:
            sums[10 + j // 2] = fold8(qkv[:, s].astype(F32))
        after(f"dwqkv{j}")
    for i, k in enumerate((10, 11, 3, 4, 5, 6, 7, 8, 9, 0, 1, 2)):
        small[i] = jnp.sum(sums[k], axis=0, keepdims=True)
    after("sums")
    if not fused:
        outs = [pltpu.make_async_copy(mats[i], dw_o.at[i], osem.at[1 + i]) for i in range(3)]
        for copy in outs:
            copy.start()
    for half in range(2):
        rows = slice(half * 384, half * 384 + 384)
        v = db[rows, :].astype(F32)
        for j in range(3):
            v = v + dot_nt(qkv[rows, j * D : (j + 1) * D], block(a0, j))
        db[rows, :] = v.astype(BF)
        after(f"dx{half}")
    dx_out = pltpu.make_async_copy(db, dx_o, osem.at[0])
    dx_out.start()
    if not fused:
        for copy in outs + [dx_out]:
            copy.wait()
        return
    after("tail")
    dx_out.wait()
    for copy in net.outs[-2:]:
        copy.wait()


def layer(fused, n_dp, *args):
    width = FF // (4 * n_dp)
    outs = [(BLOCKS[1:], BF), ((ROWS, D), BF), ((32, 1, D), F32)]
    blocks = [((3, 16, FF), BF), ((4, 16, D), BF)]
    buffers = [(BLOCKS, BF)] * 6 + [((ROWS, D), BF)] * 3
    buffers += [((ROWS, 1), F32), ((ROWS, 3 * D), BF), ((OWN * PAIRS * 2 * SEG, SEG), BF), ((ROWS, D), BF)]
    buffers += [((OWN, 16, D), BF), ((2, 16, D), F32), ((2, 8, D), F32), ((2, 8, D), F32), ((12, 8, D), F32)]
    sems = [31, 4, 2, 2]
    vmem, extra = [pltpu.VMEM(*b) for b in buffers], []
    vmem += [pltpu.SemaphoreType.DMA((n,)) for n in sems]
    if fused:
        outs += [((6, width, D), F32)]
        out_specs = [ANY, ANY, VM, ANY]
        vmem = [pltpu.VMEM((2,) + shape, dt) for shape, dt in blocks] + vmem
        count = 6 * 3 * (n_dp // 2) + 4 * (n_dp - 1) + 8
        parts = [pltpu.VMEM(s, BF) for s in scatter_buffers(n_dp // 2, width)]
        extra = [pltpu.VMEM((32, 1, D), F32), pltpu.VMEM((16, 128), BF)] + parts[1:] + parts * 2
        extra += [
            pltpu.VMEM((n_dp, 2, 3, 16, D), BF),
            pltpu.VMEM((n_dp, 2, 3, 16, 4 * width), BF),
            pltpu.VMEM((32, 1, D), F32),
            pltpu.VMEM((2, width, D), F32),
            pltpu.SemaphoreType.DMA((count,)),
            pltpu.SemaphoreType.DMA((count,)),
            pltpu.SemaphoreType.DMA((3, n_dp // 2)),
            pltpu.SemaphoreType.REGULAR,
            pltpu.SemaphoreType.DMA((2,)),
            pltpu.SemaphoreType.DMA((4,)),
        ]
    else:
        outs += [((3,) + BLOCKS, BF)] + blocks
        out_specs = [ANY, ANY, VM, ANY, VM, VM]
    return pl.pallas_call(
        functools.partial(layer_kernel, fused),
        out_shape=[jax.ShapeDtypeStruct(*s) for s in outs],
        in_specs=[VM, ANY, SM, VM, VM, VM, VM, VM, ANY, ANY],
        out_specs=out_specs,
        scratch_shapes=vmem + extra,
        compiler_params=pltpu.CompilerParams(
            vmem_limit_bytes=63 * 2**20, collective_id=0 if fused else 1, has_side_effects=True
        ),
    )(*args)


def place_kernel(red, cols, wide, grads):
    width = red.shape[1]
    me = lax.axis_index("dp") * lax.axis_size("section") + lax.axis_index("section")
    last = jnp.where(me * width >= 3 * D, wide[3].astype(F32), wide[2].astype(F32)).astype(BF)
    for i, k in enumerate((0, 2, 3)):
        grads[k] = red[i].astype(F32)

    def put(k, value):
        grads[k] = value

    cls_grads([wide[0], wide[1], last], cols, put, lambda v: v)


def place(red, cols, wide):
    return pl.pallas_call(
        place_kernel,
        out_shape=jax.ShapeDtypeStruct((6,) + red.shape[1:], F32),
        in_specs=[VM] * 3,
        out_specs=VM,
        compiler_params=pltpu.CompilerParams(vmem_limit_bytes=56 * 2**20),
    )(red, cols, wide)


def finish_kernel(grads, small, enc, dx, enc_o, dx_o, ga, gm, ab, an, mb, ms, embed, grads_v, enc_v, dx_v, sems):
    loads, stores = Copies(sems.at[0]), Copies(sems.at[1])
    for src, dst in ((enc, enc_v), (dx, dx_v), (grads, grads_v)):
        loads.start(src, dst)
    for k in range(2):
        at = 12 * k
        for i in range(3):
            ab[i, k : k + 1, :] = small[at + i]
            ms[i, k : k + 1, :] = small[at + 9 + i]
        for i in range(2):
            an[k, i : i + 1, :] = small[at + 3 + i]
        for j in range(4):
            mb[k : k + 1, j * D : (j + 1) * D] = small[at + 5 + j]
    for i in range(8):
        embed[i : i + 1, :] = small[24 + i]
    for i, (src, dst) in enumerate(((enc_v, enc_o), (dx_v, dx_o), (grads_v.at[0:2], ga), (grads_v.at[2:6], gm))):
        if i < 3:
            loads.all[i].wait()
        stores.start(src, dst)
    for copy in stores.all:
        copy.wait()


def finish(grads, small, enc, dx):
    enc = enc.reshape(ROWS, D)
    width = grads.shape[1]
    shapes = [(2, width, D), (4, width, D), (3, 2, D), (2, 2, D), (2, FF), (3, 2, D), (8, D)]
    outs = [jax.ShapeDtypeStruct((ROWS, D), BF)] * 2 + [jax.ShapeDtypeStruct(s, F32) for s in shapes]
    return pl.pallas_call(
        finish_kernel,
        out_shape=outs,
        in_specs=[ANY, VM, ANY, ANY],
        out_specs=[ANY] * 4 + [VM] * 5,
        scratch_shapes=[
            pltpu.VMEM(grads.shape, F32),
            pltpu.VMEM((ROWS, D), BF),
            pltpu.VMEM((ROWS, D), BF),
            pltpu.SemaphoreType.DMA((2, 4)),
        ],
    )(grads, small, enc, dx)


def on_device(tokens, counts, aw, ab, an, mw, mb, ms, embed, cot):
    n_dp, n_section = lax.axis_size("dp"), lax.axis_size("section")
    ab, ms = ab.swapaxes(0, 1), ms.swapaxes(0, 1)
    aw, mw = aw.reshape((2,) + BLOCKS[1:5] + (4 * D,)), mw.reshape((2, 2) + BLOCKS[1:5] + (FF,))
    fused = (n_dp // 2, 2, 2, 2, FF // (n_dp * n_section), D) == BLOCKS and n_section == 4
    result = layer(fused, n_dp, tokens, cot, counts, ab, ms, an, mb, embed, aw, mw)
    if fused:
        encoded, dx, small, grads = result
    else:
        encoded, dx, small, dw, cols, wide = result
        own = jnp.arange(16) // 8 == lax.axis_index("section") % 2
        cols = jnp.where(own[None, :, None], cols, jnp.zeros_like(cols))
        cols = lax.all_to_all(cols, BOTH, split_axis=2, concat_axis=1, tiled=True)
        wide = lax.all_gather(wide, BOTH, axis=1, tiled=True)
        red = lax.psum_scatter(dw.reshape(3, FF, D), BOTH, scatter_dimension=1, tiled=True)
        small = lax.psum(small, BOTH)
        grads = place(red, cols, wide)
    encoded, dx, ga, gm, g_ab, g_an, g_mb, g_ms, g_embed = finish(grads, small, encoded, dx)
    gm = gm.reshape((2, 2) + gm.shape[1:])
    return (
        encoded,
        dx,
        ga.swapaxes(1, 2),
        g_ab.swapaxes(0, 1),
        g_an,
        gm.swapaxes(2, 3),
        g_mb,
        g_ms.swapaxes(0, 1),
        g_embed,
    )


def solution(mesh):
    return jax.shard_map(
        on_device,
        mesh=mesh,
        in_specs=(P(BOTH, None), P("dp", None)) + (P(),) * 7 + (P(BOTH, None),),
        out_specs=(
            P(BOTH, None),
            P(BOTH, None),
            P(None, None, BOTH),
            P(),
            P(),
            P(None, None, None, BOTH),
            P(),
            P(),
            P(),
        ),
        check_vma=False,
    )
```

```python
import functools
import itertools

import jax
import jax.numpy as jnp
from jax import lax
from jax.experimental import pallas as pl
from jax.experimental.pallas import tpu as pltpu
from jax.sharding import PartitionSpec as P

F32 = jnp.float32
BF = jnp.bfloat16
D = 768
FF = 3072
SEG = 128
HEAD = 64
HEADS = 12
PAIRS = 6
MICRO = 2
SEGS = 12
OWN = 6
ROWS = OWN * SEG
BLOCKS = (4, 2, 2, 2, 96, D)
BOTH = ("dp", "section")
MASKED = -1e30
VM = pl.BlockSpec(memory_space=pltpu.VMEM)
SM = pl.BlockSpec(memory_space=pltpu.SMEM)
ANY = pl.BlockSpec(memory_space=pl.ANY)
MESH = pl.DeviceIdType.MESH


def dot(a, b):
    return jnp.dot(a, b, preferred_element_type=F32)


def dot_nt(a, b):
    return lax.dot_general(a, b, (((1,), (1,)), ((), ())), preferred_element_type=F32)


def dot_tn(a, b):
    return lax.dot_general(a, b, (((0,), (0,)), ((), ())), preferred_element_type=F32)


def gelu_parts(h):
    phi = 0.5 + 0.5 * lax.erf(h * 0.7071067811865476)
    return h * phi, phi + h * (0.3989422804014327 * jnp.exp2((h * h) * -0.7213475204444817))


def norm_rows(r):
    center = r - jnp.mean(r, axis=-1, keepdims=True)
    rstd = lax.rsqrt(jnp.mean(center * center, axis=-1, keepdims=True) + 1e-5)
    return center * rstd, rstd


def norm_back(dy, n, rstd, gain):
    dyg = dy * gain
    return (
        dyg
        - jnp.mean(dyg, axis=-1, keepdims=True)
        - n * jnp.mean(dyg * n, axis=-1, keepdims=True)
    ) * rstd


def halves(v):
    lane = lax.broadcasted_iota(jnp.int32, v.shape, 1)
    zero = jnp.zeros_like(v)
    return jnp.concatenate([jnp.where(lane < HEAD, v, zero), jnp.where(lane < HEAD, zero, v)], 0)


def unhalve(v):
    top, bottom = v[:SEG], v[SEG:]
    lane = lax.broadcasted_iota(jnp.int32, top.shape, 1)
    return jnp.where(lane < HEAD, top, bottom)


def fold8(v):
    return jnp.sum(v.reshape(v.shape[0] // 8, 8, v.shape[1]), axis=0)


def pair_rows(g, h):
    start = (g * PAIRS + h) * 2 * SEG
    return slice(start, start + 2 * SEG)


def block(ref, j):
    return ref[j].reshape(D, D)


def row(ref, *idx):
    if isinstance(ref, tuple):
        return row(ref[idx[0] // 6], idx[0] % 3, idx[0] // 3 % 2)
    i = idx[-1]
    return ref[idx[:-1] + (slice(i, i + 1), slice(None))].astype(F32)


class Copies:
    def __init__(self, sems):
        self.sems, self.all = sems, []

    def start(self, src, dst):
        copy = pltpu.make_async_copy(src, dst, self.sems.at[len(self.all)])
        copy.start()
        self.all.append(copy)
        return copy


def cls_chain(
    own, other, counts, wq, w1, w2, par, an, mb, embed, cols_o, wide_o, small_o
):
    section = lax.axis_index("section")
    per_micro = lax.axis_size("section") // MICRO
    half = lax.rem(section, per_micro)
    micro = section // per_micro
    ends = [counts[micro, 0], counts[micro, 0] + counts[micro, 1]]

    def layout(shape, axis):
        r = lax.broadcasted_iota(jnp.int32, shape, axis)
        seg = jnp.where(r < 8, r, r - 2)
        valid = (r < 6) | ((r >= 8) & (r < 14))
        doc = jnp.where(seg >= ends[0], 1, 0) + jnp.where(seg >= ends[1], 1, 0)
        start = jnp.where(doc == 0, 0, jnp.where(doc == 1, ends[0], ends[1]))
        pos = jnp.where(valid, seg - start, -1)
        return jnp.where(valid, doc, jnp.where(r < 16, 100 + r, -1)), pos, valid

    def order(a, b):
        first = half == 0
        return jnp.concatenate([jnp.where(first, a, b), jnp.where(first, b, a)], axis=0)

    def mine(v):
        return jnp.where(half == 0, v[:8], v[8:])

    doc_q, pos, valid = layout((16, 128), 0)
    doc_k, _, _ = layout((16, 128), 1)
    allowed = jnp.concatenate([doc_q == doc_k] * HEADS, axis=0)
    lanes8 = lax.broadcasted_iota(jnp.int32, (16, 8), 1)
    onehot = (pos[:, :8] == lanes8).astype(BF)
    leaders = order(own[0], other[0]) + dot(onehot, embed[...])
    low = leaders.astype(BF)
    lane = lax.broadcasted_iota(jnp.int32, (16, D), 1) // HEAD

    def stack(v):
        return jnp.concatenate([jnp.where(lane == h, v, jnp.zeros_like(v)) for h in range(HEADS)], 0)

    def unstack(v):
        total = jnp.where(lane == 0, v[:16], 0.0)
        for h in range(1, HEADS):
            total = total + jnp.where(lane == h, v[h * 16 : (h + 1) * 16], 0.0)
        return total

    def deep(v):
        return jnp.concatenate([v, jnp.zeros((112, D), BF)], axis=0)

    q = (dot(low, block(wq, 0)) + row(par, 3)).astype(BF)
    k = dot(low, block(wq, 1)).astype(BF)
    v = (dot(low, block(wq, 2)) + row(par, 4)).astype(BF)
    qs, kd, vd = stack(q), deep(k), deep(v)
    scores = jnp.where(allowed, dot_nt(qs, kd) * 0.125, MASKED)
    e = jnp.exp(scores - jnp.max(scores, axis=-1, keepdims=True))
    probs = e / jnp.sum(e, axis=-1, keepdims=True)
    probs_low = probs.astype(BF)
    ctx = unstack(dot(probs_low, vd)).astype(BF)
    n1, rs1 = norm_rows(leaders + dot(ctx, block(wq, 3)) + row(par, 5))
    third = (n1 * row(an, 1, 0) + row(an, 1, 1)).astype(BF)
    act, gp, v = [], [], third.astype(F32) + row(par, 9)
    for j in range(4):
        a, g = gelu_parts(dot(third, block(w1, j)) + mb[1:2, j * D : (j + 1) * D].astype(F32))
        act.append(a.astype(BF))
        gp.append(g)
        v = v + dot_nt(act[j], block(w2, j))
    n2, rs2 = norm_rows(v)
    fourth = mine(n2 * row(par, 10) + row(par, 11))

    dy = order(own[1], other[1])
    small_o[22] = jnp.sum(mine(dy * n2), axis=0, keepdims=True)
    small_o[23] = jnp.sum(mine(dy), axis=0, keepdims=True)
    dr = norm_back(dy, n2, rs2, row(par, 10))
    dbf = dr.astype(BF)
    small_o[21] = jnp.sum(mine(dbf.astype(F32)), axis=0, keepdims=True)
    dthird = dr
    for j in range(4):
        dh = (dot(dbf, block(w2, j)) * gp[j]).astype(BF)
        dh_mine = mine(dh.astype(F32))
        small_o[17 + j] = jnp.sum(dh_mine, axis=0, keepdims=True)
        cols_o[0, :, j * D : (j + 1) * D] = dh
        cols_o[1, :, j * D : (j + 1) * D] = act[j]
        dthird = dthird + dot_nt(dh, block(w1, j))
    dthird = dthird.astype(BF).astype(F32)
    small_o[15] = jnp.sum(mine(dthird * n1), axis=0, keepdims=True)
    small_o[16] = jnp.sum(mine(dthird), axis=0, keepdims=True)
    dr = norm_back(dthird, n1, rs1, row(an, 1, 0))
    dba = dr.astype(BF)
    small_o[14] = jnp.sum(mine(dba.astype(F32)), axis=0, keepdims=True)
    dctx = stack(dot_nt(dba, block(wq, 3)).astype(BF))
    dp = dot_nt(dctx, vd)
    dv = dot_tn(probs_low, dctx)[:16].astype(BF)
    ds = (probs * (dp - jnp.sum(dp * probs, axis=-1, keepdims=True))).astype(BF)
    dq = (unstack(dot(ds, kd)) * 0.125).astype(BF)
    dk = (dot_tn(ds, qs)[:16] * 0.125).astype(BF)
    small_o[12] = jnp.sum(mine(dq.astype(F32)), axis=0, keepdims=True)
    small_o[13] = jnp.sum(mine(dv.astype(F32)), axis=0, keepdims=True)
    dlead = dr
    for j, piece in enumerate((dq, dk, dv)):
        dlead = dlead + dot_nt(piece, block(wq, j))
    dlead_mine = mine(dlead)
    pos_mine = jnp.where(half == 0, pos[:8], pos[8:])
    for i in range(8):
        hit = jnp.where(pos_mine[:, 0:1] == i, dlead_mine, 0.0)
        small_o[24 + i] = jnp.sum(hit, axis=0, keepdims=True)
    for j, piece in enumerate((dq, dk, dv, dba)):
        cols_o[2, :, j * D : (j + 1) * D] = piece
    for j, piece in enumerate((third, dbf, low, ctx)):
        wide_o[j] = piece
    return fourth, dlead_mine


class Place:
    def __init__(self):
        self.dp, self.section = lax.axis_index("dp"), lax.axis_index("section")
        self.n_dp, self.n_section = lax.axis_size("dp"), lax.axis_size("section")
        self.nz = self.n_dp // 2
        self.z, self.x = self.dp // 2, lax.rem(self.dp, 2)
        self.y, self.c = self.section // 2, lax.rem(self.section, 2)

    def at(self, dz=0, x=None, y=None, c=None):
        x = self.x if x is None else x
        y = self.y if y is None else y
        c = self.c if c is None else c
        return ((self.z + dz) * 2 + x, y * 2 + c)

    def to_x(self):
        return self.at(x=1 - self.x)

    def to_y(self):
        return self.at(y=1 - self.y)

    def to_c(self):
        return self.at(c=1 - self.c)

    def device(self, index):
        return (index // self.n_section, lax.rem(index, self.n_section))


class Links:
    def __init__(self, sends, recvs):
        self.sends, self.recvs, self.used = sends, recvs, 0

    def copy(self, src, dst, peer, recv=None):
        i = self.used
        self.used += 1
        return pltpu.make_async_remote_copy(
            src_ref=src, dst_ref=dst, send_sem=self.sends.at[i], recv_sem=self.recvs.at[i] if recv is None else recv,
            device_id=peer, device_id_type=MESH,
        )


HALF = D // 2
LEFT, RIGHT = slice(0, HALF), slice(HALF, D)


class Scatter:
    def __init__(self, me, links, held, core, xa, yb, ya, xb, zb, z_recv, j0, count):
        self.me, self.held, self.js = me, held, range(j0, j0 + count)
        self.core, self.xa, self.yb, self.ya, self.xb = core, xa, yb, ya, xb
        x, y, c = me.x, me.y, me.c
        js, cols_a, cols_b = pl.ds(j0, count), pl.ds(0, HALF), pl.ds(HALF, HALF)
        self.core_copy = links.copy(held.at[js, :, :, 1 - c], core.at[js], me.to_c())
        self.xa_copy = links.copy(held.at[js, 1 - x, :, c, :, cols_a], xa.at[js], me.to_x())
        self.yb_copy = links.copy(held.at[js, :, 1 - y, c, :, cols_b], yb.at[js], me.to_y())
        self.ya_copy = links.copy(held.at[js, x, 1 - y, c, :, cols_a], ya.at[js], me.to_y())
        self.xb_copy = links.copy(held.at[js, 1 - x, y, c, :, cols_b], xb.at[js], me.to_x())
        self.z_copies = [
            links.copy(held.at[j, x, y, c], zb.at[me.z], (j * 2 + x, me.section), z_recv.at[me.z])
            for j in self.js
        ]

    def add(self, j, x, y, cols, value):
        c = self.me.c
        self.held[j, x, y, c, :, cols] = self.held[j, x, y, c, :, cols] + value

    def start(self):
        self.core_copy.start()

    def first(self):
        me, core = self.me, self.core
        x, y = me.x, me.y
        self.core_copy.wait_recv()
        for j in self.js:
            for i in range(2):
                self.add(j, 1 - x, i, LEFT, core[j, 1 - x, i, :, LEFT])
        self.xa_copy.start()
        for j in self.js:
            for i in range(2):
                self.add(j, i, 1 - y, RIGHT, core[j, i, 1 - y, :, RIGHT])
        self.yb_copy.start()
        for j in self.js:
            for i in range(2):
                self.add(j, x, i, LEFT, core[j, x, i, :, LEFT])
                self.add(j, i, y, RIGHT, core[j, i, y, :, RIGHT])

    def second(self):
        me = self.me
        x, y = me.x, me.y
        self.xa_copy.wait_recv()
        for j in self.js:
            self.add(j, x, 1 - y, LEFT, self.xa[j, 1 - y])
        self.ya_copy.start()
        self.yb_copy.wait_recv()
        for j in self.js:
            self.add(j, 1 - x, y, RIGHT, self.yb[j, 1 - x])
        self.xb_copy.start()
        for j in self.js:
            self.add(j, x, y, LEFT, self.xa[j, y])
            self.add(j, x, y, RIGHT, self.yb[j, x])

    def third(self):
        me = self.me
        self.ya_copy.wait_recv()
        self.xb_copy.wait_recv()
        for i, j in enumerate(self.js):
            self.add(j, me.x, me.y, LEFT, self.ya[j])
            self.add(j, me.x, me.y, RIGHT, self.xb[j])

            @pl.when(me.z != j)
            def _():
                self.z_copies[i].start()

    def drain(self):
        for copy in (self.core_copy, self.xa_copy, self.yb_copy, self.ya_copy, self.xb_copy):
            copy.wait_send()
        for i, j in enumerate(self.js):

            @pl.when(self.me.z != j)
            def _():
                self.z_copies[i].wait_send()


class Matrix:
    def __init__(self, me, links, z_recv, held, *buffers, cuts):
        self.me, self.held, self.zb = me, held, buffers[-1]
        self.units = [Scatter(me, links, held, *buffers, z_recv, j0, n) for j0, n in cuts]
        self.arrivals = [
            pltpu.make_async_remote_copy(
                src_ref=self.zb.at[i], dst_ref=self.zb.at[i], send_sem=z_recv.at[i], recv_sem=z_recv.at[i],
                device_id=(me.dp, me.section), device_id_type=MESH,
            )
            for i in range(me.nz)
        ]

    def finish(self, total):
        me = self.me
        for unit in self.units:
            unit.drain()
        total[...] = self.held[me.z, me.x, me.y, me.c].astype(F32)
        for i in range(me.nz):

            @pl.when(me.z != i)
            def _():
                self.arrivals[i].wait_recv()
                total[...] += self.zb[i].astype(F32)


def scatter_buffers(nz, width):
    shapes = [(nz, 2, 2, width, D)] + [(nz, 2, width, HALF)] * 2 + [(nz, width, HALF)] * 2
    return shapes + [(nz, width, D)]


class Gather:
    def __init__(self, me, links, wide, cols, all_wide, all_cols):
        self.me, self.all_wide, self.all_cols = me, all_wide, all_cols
        self.wide, self.cols = wide, cols
        self.span = cols.shape[-1] // me.n_dp
        self.copies = [[], [], []]
        for c in range(2):
            w, k = (pl.ds(0, 2), pl.ds(0, 1)) if c == 0 else (pl.ds(2, 1), pl.ds(1, 2))
            given = [wide.at[me.y, pl.ds(2 * c, 2)], cols.at[me.y, k]]
            self.copies[0].append([links.copy(a, a, me.to_y()) for a in given])
            spread = []
            for i in range(1, me.n_dp):
                peer = lax.rem(me.dp + i, me.n_dp)
                spread.append(links.copy(self.given(c, peer), all_wide.at[me.dp, :, w], (peer, me.section)))
                spread.append(links.copy(self.part(k, peer), all_cols.at[me.dp, :, k], (peer, me.section)))
            self.copies[1].append(spread)
            beside = [all_wide.at[:, :, w], all_cols.at[:, :, k]]
            self.copies[2].append([links.copy(a, a, me.to_c()) for a in beside])

    def given(self, c, peer):
        if c == 0:
            return self.wide.at[:, pl.ds(0, 2)]
        return self.wide.at[:, pl.ds(2 + peer * self.span // (3 * D), 1)]

    def part(self, k, peer):
        return self.cols.at[:, k, :, pl.ds(pl.multiple_of(peer * self.span, 128), self.span)]

    def each(self, do):
        for c in range(2):

            @pl.when(self.me.c == c)
            def _():
                do(c)

    def start(self):
        def go(c):
            for copy in self.copies[0][c]:
                copy.start()

        self.each(go)

    def second(self):
        me = self.me

        def go(c):
            for copy in self.copies[0][c]:
                copy.wait()
            for copy in self.copies[1][c]:
                copy.start()
            w, k = (slice(0, 2), slice(0, 1)) if c == 0 else (slice(2, 3), slice(1, 3))
            self.all_wide[me.dp, :, w] = self.given(c, me.dp)[...]
            self.all_cols[me.dp, :, k] = self.part(pl.ds(k.start, k.stop - k.start), me.dp)[...]

        self.each(go)

    def third(self):
        def go(c):
            for copy in self.copies[1][c]:
                copy.wait()
            for copy in self.copies[2][c]:
                copy.start()

        self.each(go)

    def finish(self):
        def go(c):
            for copy in self.copies[2][c]:
                copy.wait_send()
            for copy in self.copies[2][1 - c]:
                copy.wait_recv()

        self.each(go)


class Total:
    def __init__(self, me, acc, got, out, sems):
        self.me, self.acc, self.got, self.out, self.sems = me, acc, got, out, sems
        self.count = acc.shape[0]
        self.index = me.dp * me.n_section + me.section

    def send(self, phase):
        @pl.loop(1, self.count)
        def _(i):
            peer = lax.rem(self.index + i, self.count)
            src = self.acc.at[peer] if phase == 0 else self.out.at[self.index]
            dst = (self.got if phase == 0 else self.out).at[self.index]
            pltpu.make_async_remote_copy(
                src_ref=src, dst_ref=dst, send_sem=self.sems.at[2 * phase], recv_sem=self.sems.at[2 * phase + 1],
                device_id=self.me.device(peer), device_id_type=MESH,
            ).start()

    def wait(self, phase):
        rows = self.got.at[pl.ds(0, self.count - 1)]
        for i in range(2):
            pltpu.make_async_copy(rows, rows, self.sems.at[2 * phase + i]).wait()

    def step(self, i):
        if i == 0:
            self.got[self.index] = self.acc[self.index]
            self.send(0)
        elif i == 1:
            self.wait(0)
            self.out[self.index] = jnp.sum(self.got[...], axis=0)
            self.send(1)
        else:
            self.wait(1)


def pick_own(me, width):
    def pick(v):
        out = v[:, :width]
        for s in range(1, 4):
            out = jnp.where(me.section == s, v[:, s * width : (s + 1) * width], out)
        return out

    return pick


N_SET = 6
BLOCK_ORDER = (1, 2, 0, 3)
QKV_ORDER = (0, 1, 2)
PLAN = {
    "ffnout0": (
        ("g", 0, 0),
    ),
    "dwout1": (
        ("o", 1, 0),
    ),
    "dwout2": (
        ("o", 2, 0),
    ),
    "dwout0": (
        ("o", 0, 0),
    ),
    "dwout3": (
        ("o", 3, 0),
    ),
    "dh0": (
        ("o", 1, 1),
    ),
    "dh3": (
        ("o", 2, 1),
    ),
    "dwin1": (
        ("i", 1, 0),
    ),
    "dwin2": (
        ("i", 2, 0),
        ("o", 0, 1),
    ),
    "dwin0": (
        ("i", 0, 0),
    ),
    "dwin3": (
        ("i", 3, 0),
        ("o", 1, 2),
    ),
    "dfirst0": (
        ("o", 2, 2),
    ),
    "dfirst1": (
        ("o", 3, 1),
        ("f", 0, 0),
    ),
    "dwo": (
        ("f", 0, 1),
        ("a", 3, 0),
        ("o", 0, 2),
        ("g", 1, 0),
    ),
    "dctx": (
        ("o", 1, 3),
        ("i", 1, 1),
        ("o", 2, 3),
    ),
    "att1": (
        ("g", 2, 0),
        ("o", 3, 2),
    ),
    "att2": (
        ("o", 0, 3),
        ("i", 2, 1),
    ),
    "att4": (
        ("i", 1, 2),
    ),
    "att5": (
        ("o", 3, 3),
        ("i", 0, 1),
    ),
    "dwqkv0": (
        ("a", 0, 0),
    ),
    "dwqkv1": (
        ("a", 1, 0),
        ("i", 2, 2),
    ),
    "dwqkv2": (
        ("a", 2, 0),
        ("i", 3, 1),
        ("i", 1, 3),
    ),
    "sums": (
        ("s", 0, 0),
        ("i", 0, 2),
    ),
    "dx0": (
        ("i", 2, 3),
    ),
    "dx1": (
        ("a", 3, 1),
    ),
    "tail": (
        ("i", 3, 2),
        ("p", 3, 0),
        ("a", 0, 1),
        ("i", 0, 3),
        ("a", 1, 1),
        ("a", 3, 2),
        ("s", 1, 0),
        ("i", 3, 3),
        ("a", 0, 2),
        ("a", 2, 1),
        ("a", 1, 2),
        ("a", 3, 3),
        ("a", 0, 3),
        ("a", 2, 2),
        ("p", 2, 0),
        ("s", 2, 0),
        ("a", 1, 3),
        ("a", 2, 3),
        ("p", 0, 0),
    ),
}


def cls_grads(wide, cols, put, pick):
    for i, k in enumerate((4, 5, 1)):
        put(k, dot_tn(pick(cols[i]), wide[i]))


class Net:
    def __init__(self, mats, acc, out, wide, cols, grads, scratch):
        sets = [scratch[i * N_SET : (i + 1) * N_SET] for i in range(3)]
        sets[0] = sets[2][:1] + sets[0][1:]
        all_wide, all_cols, got, self.stage, sends, recvs, z_recvs, self.free, self.out_sems, sum_sems = scratch[3 * N_SET :]
        self.outs = []
        self.me, self.grads = Place(), grads
        links = Links(sends, recvs)
        self.attn, self.win, self.wout = [
            Matrix(self.me, links, z_recvs.at[m], mats[m], *sets[m], cuts=[(j, 1) for j in range(4)]) for m in range(3)
        ]
        self.gather = Gather(self.me, links, wide, cols, all_wide, all_cols)
        self.summed = Total(self.me, acc, got, out, sum_sems)

    def slot(self):
        i = len(self.outs)
        if i >= 2:
            self.outs[i - 2].wait()
        return self.stage.at[i % 2]

    def put(self, k):
        i = len(self.outs)
        copy = pltpu.make_async_copy(self.stage.at[i % 2], self.grads.at[k], self.out_sems.at[i % 2])
        copy.start()
        self.outs.append(copy)

    def cls(self):
        self.gather.finish()
        width = self.stage.shape[1]
        rows = 16 * 2 * self.me.n_dp
        wide = [self.gather.all_wide[:, :, i].reshape(rows, D) for i in range(3)]
        cols = [self.gather.all_cols[:, :, i].reshape(rows, 4 * width) for i in range(3)]

        def put(k, value):
            self.slot()[...] = value
            self.put(k)

        cls_grads(wide, cols, put, pick_own(self.me, width))

    def place(self, which, k):
        which.finish(self.slot())
        self.put(k)

    def after(self, name):
        kinds = {"a": self.attn.units, "i": self.win.units, "o": self.wout.units}
        for step in PLAN.get(name, ()):
            kind, number, phase = step
            if kind == "g":
                (self.gather.second, self.gather.third, self.cls)[number]()
            elif kind == "s":
                self.summed.step(number)
            elif kind == "p":
                self.place((self.attn, None, self.win, self.wout)[number], number)
            elif kind == "f":
                if phase == 0:
                    pl.semaphore_signal(self.free, inc=1, device_id=self.me.to_c(), device_id_type=MESH)
                else:
                    pl.semaphore_wait(self.free, 1)
            else:
                unit = kinds[kind][number]
                (unit.start, unit.first, unit.second, unit.third)[phase]()


def layer_kernel(fused, x_i, cot, counts, ab, ms, an, mb, embed, aw, mw, enc_o, dx_o, small_o, *refs):
    par = (ab, ms)
    if fused:
        grads_o, refs = refs[0], refs[1:]
    else:
        dw_o, refs = refs[0], refs[1:]
    cols, wide, a0, win0, wout0, a1, v1, v2, first, n1, db, x, rs1, qkv, p, ctx = refs[:16]
    heads, rows16, mine, theirs, sums, wsem, osem, ssem, rsem = refs[16:25]
    act, gp, dwout = v1, v2, a1
    mats = (gp, act, dwout)
    loads = Copies(wsem)

    def load(src, dst):
        return [loads.start(src.at[:, :, :, :, j * D : (j + 1) * D], dst.at[j]) for j in range(4)]

    x_in = loads.start(x_i, x)
    a0_in = load(aw.at[0], a0)
    heads_in = [loads.start(cot.at[pl.ds(g * SEG, 16)], heads.at[g]) for g in range(OWN)]
    win0_in, wout0_in = load(mw.at[0, 0], win0), load(mw.at[0, 1], wout0)
    cls_in = load(aw.at[1], a1) + load(mw.at[1, 0], v1) + load(mw.at[1, 1], v2)
    cot_in = loads.start(cot, db)

    section = lax.axis_index("section")
    partner = (lax.axis_index("dp"), section + 1 - 2 * lax.rem(section, 2))
    barrier = pltpu.get_barrier_semaphore()
    if fused:
        small, refs = refs[25], refs[:25] + refs[26:]
        net = Net(mats, small, small_o, wide, cols, grads_o, refs[25:])
        expected = net.me.n_dp * net.me.n_section - 1

        @pl.loop(1, expected + 1)
        def _(i):
            peer = net.me.device(lax.rem(net.summed.index + i, expected + 1))
            pl.semaphore_signal(barrier, inc=1, device_id=peer, device_id_type=MESH)
    else:
        small, expected = small_o, 1
        pl.semaphore_signal(barrier, inc=1, device_id=partner, device_id_type=MESH)

    def after(name):
        if fused:
            net.after(name)

    swaps = [
        pltpu.make_async_remote_copy(
            src_ref=mine.at[i], dst_ref=theirs.at[i], send_sem=ssem.at[i], recv_sem=rsem.at[i],
            device_id=partner, device_id_type=MESH,
        )
        for i in range(2)
    ]

    x_in.wait()
    for j in range(3):
        a0_in[j].wait()
        v = dot(x[...], block(a0, j))
        if j != 1:
            v = v + row(par, j // 2)
        qkv[:, j * D : (j + 1) * D] = v.astype(BF)
    for g, h in itertools.product(range(OWN), range(PAIRS)):
        rows, c = slice(g * SEG, (g + 1) * SEG), slice(h * 128, (h + 1) * 128)
        q = qkv[rows, c] * jnp.asarray(0.125, BF)
        kc = halves(qkv[rows, D + h * 128 : D + (h + 1) * 128])
        vc = halves(qkv[rows, 2 * D + h * 128 : 2 * D + (h + 1) * 128])
        scores = dot_nt(kc, q)
        ps = []
        for i in range(2):
            si = scores[i * SEG : (i + 1) * SEG]
            e = jnp.exp(si - jnp.max(si, axis=0, keepdims=True))
            ps.append((e / jnp.sum(e, axis=0, keepdims=True)).astype(BF))
        pt = jnp.concatenate(ps, axis=0)
        p[pair_rows(g, h), :] = pt
        ctx[rows, c] = dot_tn(pt, vc).astype(BF)

    mine[...] = jnp.zeros_like(mine)
    rows16[...] = jnp.zeros_like(rows16)
    for copy in heads_in:
        copy.wait()
    for g in range(OWN):
        mine[1, g : g + 1, :] = heads[g, 0:1, :].astype(F32)
        rows16[0, g : g + 1, :] = x[g * SEG : g * SEG + 1, :].astype(F32)
        rows16[1, g : g + 1, :] = ctx[g * SEG : g * SEG + 1, :].astype(F32)
    pl.semaphore_wait(barrier, expected)
    swaps[1].start()
    a0_in[3].wait()
    n, _ = norm_rows(rows16[0] + dot(rows16[1].astype(BF), block(a0, 3)) + row(par, 2))
    low = (n * row(an, 0, 0) + row(an, 0, 1)).astype(BF)
    v = low.astype(F32) + row(par, 6)
    for j in range(4):
        win0_in[j].wait()
        wout0_in[j].wait()
        a, _ = gelu_parts(dot(low, block(win0, j)) + mb[0:1, j * D : (j + 1) * D].astype(F32))
        v = v + dot_nt(a.astype(BF), block(wout0, j))
    n, _ = norm_rows(v)
    value = (n * row(par, 7) + row(par, 8)).astype(BF).astype(F32)
    mine[0] = jnp.where(lax.broadcasted_iota(jnp.int32, (8, D), 0) < OWN, value[:8], 0.0)
    swaps[0].start()

    for half in range(2):
        rows = slice(half * 384, half * 384 + 384)
        v = dot(ctx[rows, :], block(a0, 3)) + x[rows, :].astype(F32) + row(par, 2)
        n, rs = norm_rows(v)
        n1[rows, :] = n.astype(BF)
        rs1[rows, :] = rs
        first[rows, :] = (n * row(an, 0, 0) + row(an, 0, 1)).astype(BF)
    for copy in cls_in:
        copy.wait()
    for swap in swaps:
        swap.wait()
    if fused:
        cols_o, wide_o = cols.at[net.me.y], wide.at[net.me.y]
    else:
        cols_o, wide_o = cols, wide
    fourth, dlead = cls_chain(mine, theirs, counts, a1, v1, v2, par, an, mb, embed, cols_o, wide_o, small)
    lead = dlead.astype(BF).astype(F32)

    for j in range(4):
        a, g = gelu_parts(dot(first[...], block(win0, j)) + mb[0:1, j * D : (j + 1) * D].astype(F32))
        act[j] = a.astype(BF).reshape(BLOCKS[1:])
        gp[j] = g.astype(BF).reshape(BLOCKS[1:])
        if fused and j == 0:
            net.gather.start()
        after(f"ffnin{j}")

    def norm_step(rows, dy, n, rs, gain, at):
        low = norm_back(dy, n, rs, gain).astype(BF)
        db[rows, :] = low
        for i, v in enumerate((low.astype(F32), dy * n, dy)):
            sums[at + i] = fold8(v) if rows.start == 0 else sums[at + i] + fold8(v)

    def put(ref, j, value):
        ref[j] = value.astype(BF).reshape(BLOCKS[1:])

    cot_in.wait()
    at = lax.broadcasted_iota(jnp.int32, (384, D), 0)
    for half in range(2):
        rows = slice(half * 384, half * 384 + 384)
        v = first[rows, :].astype(F32) + row(par, 6)
        for j in range(4):
            v = v + dot_nt(act[j, half].reshape(384, D), block(wout0, j))
        n, rs = norm_rows(v)
        value, dy = n * row(par, 7) + row(par, 8), db[rows, :].astype(F32)
        for g in range(3):
            value = jnp.where(at == g * SEG, fourth[3 * half + g : 3 * half + g + 1], value)
            dy = jnp.where(at == g * SEG, lead[3 * half + g : 3 * half + g + 1], dy)
        dwout[2, half] = value.astype(BF).reshape(BLOCKS[2:])
        norm_step(rows, dy, n, rs, row(par, 7), 0)
        after(f"ffnout{half}")
    enc_out = pltpu.make_async_copy(dwout.at[2], enc_o, osem.at[0])
    enc_out.start()

    for j in BLOCK_ORDER:
        if j == 2:
            enc_out.wait()
        put(dwout, j, dot_tn(block(act, j), db[...]))
        after(f"dwout{j}")
    for j in range(4):
        low = (dot(db[...], block(wout0, j)) * block(gp, j).astype(F32)).astype(BF)
        put(gp, j, low)
        sums[6 + j] = fold8(low.astype(F32))
        after(f"dh{j}")
    for j in BLOCK_ORDER:
        put(act, j, dot_tn(block(gp, j), first[...]))
        after(f"dwin{j}")
    for half in range(2):
        rows = slice(half * 384, half * 384 + 384)
        v = db[rows, :].astype(F32)
        for j in range(4):
            v = v + dot_nt(gp[j, half].reshape(384, D), block(win0, j))
        norm_step(rows, v.astype(BF).astype(F32), n1[rows, :].astype(F32), rs1[rows, :], row(an, 0, 0), 3)
        after(f"dfirst{half}")

    put(gp, 3, dot_tn(db[...], ctx[...]))
    after("dwo")
    dctx = first
    dctx[...] = dot_nt(db[...], block(a0, 3)).astype(BF)
    after("dctx")

    def attention(g):
        rows = slice(g * SEG, (g + 1) * SEG)
        for h in range(PAIRS):
            cq = slice(h * 128, (h + 1) * 128)
            ck = slice(D + h * 128, D + (h + 1) * 128)
            cv = slice(2 * D + h * 128, 2 * D + (h + 1) * 128)
            q, dc, pt = qkv[rows, cq], dctx[rows, cq], p[pair_rows(g, h), :]
            kc, vc = halves(qkv[rows, ck]), halves(qkv[rows, cv])
            dp, pf = dot_nt(vc, dc), pt.astype(F32)
            ds = []
            for i in range(2):
                pi, di = pf[i * SEG : (i + 1) * SEG], dp[i * SEG : (i + 1) * SEG]
                ds.append((pi * (di - jnp.sum(pi * di, axis=0, keepdims=True))).astype(BF))
            ds = jnp.concatenate(ds, axis=0)
            qkv[rows, cq] = (dot_tn(ds, kc) * 0.125).astype(BF)
            qkv[rows, ck] = (unhalve(dot(ds, q)) * 0.125).astype(BF)
            qkv[rows, cv] = unhalve(dot(pt, dc)).astype(BF)

    for g in range(OWN):
        attention(g)
        after(f"att{g}")
    for j in QKV_ORDER:
        s = slice(j * D, (j + 1) * D)
        put(gp, j, dot_tn(qkv[:, s], x[...]))
        if j != 1:
            sums[10 + j // 2] = fold8(qkv[:, s].astype(F32))
        after(f"dwqkv{j}")
    for i, k in enumerate((10, 11, 3, 4, 5, 6, 7, 8, 9, 0, 1, 2)):
        small[i] = jnp.sum(sums[k], axis=0, keepdims=True)
    after("sums")
    if not fused:
        outs = [pltpu.make_async_copy(mats[i], dw_o.at[i], osem.at[1 + i]) for i in range(3)]
        for copy in outs:
            copy.start()
    for half in range(2):
        rows = slice(half * 384, half * 384 + 384)
        v = db[rows, :].astype(F32)
        for j in range(3):
            v = v + dot_nt(qkv[rows, j * D : (j + 1) * D], block(a0, j))
        db[rows, :] = v.astype(BF)
        after(f"dx{half}")
    dx_out = pltpu.make_async_copy(db, dx_o, osem.at[0])
    dx_out.start()
    if not fused:
        for copy in outs + [dx_out]:
            copy.wait()
        return
    after("tail")
    dx_out.wait()
    for copy in net.outs[-2:]:
        copy.wait()


def layer(fused, n_dp, *args):
    width = FF // (4 * n_dp)
    outs = [(BLOCKS[1:], BF), ((ROWS, D), BF), ((32, 1, D), F32)]
    blocks = [((3, 16, FF), BF), ((4, 16, D), BF)]
    buffers = [(BLOCKS, BF)] * 6 + [((ROWS, D), BF)] * 4
    buffers += [((ROWS, 1), F32), ((ROWS, 3 * D), BF), ((OWN * PAIRS * 2 * SEG, SEG), BF), ((ROWS, D), BF)]
    buffers += [((OWN, 16, D), BF), ((2, 16, D), F32), ((2, 8, D), F32), ((2, 8, D), F32), ((12, 8, D), F32)]
    sems = [32, 4, 2, 2]
    vmem, extra = [pltpu.VMEM(*b) for b in buffers], []
    vmem += [pltpu.SemaphoreType.DMA((n,)) for n in sems]
    if fused:
        outs += [((6, width, D), F32)]
        out_specs = [ANY, ANY, VM, ANY]
        vmem = [pltpu.VMEM((2,) + shape, dt) for shape, dt in blocks] + vmem
        count = 6 * 3 * (n_dp // 2) + 4 * (n_dp - 1) + 8
        parts = [pltpu.VMEM(s, BF) for s in scatter_buffers(n_dp // 2, width)]
        extra = [pltpu.VMEM((32, 1, D), F32), pltpu.VMEM((16, 128), BF)] + parts[1:] + parts * 2
        extra += [
            pltpu.VMEM((n_dp, 2, 3, 16, D), BF),
            pltpu.VMEM((n_dp, 2, 3, 16, 4 * width), BF),
            pltpu.VMEM((32, 1, D), F32),
            pltpu.VMEM((2, width, D), F32),
            pltpu.SemaphoreType.DMA((count,)),
            pltpu.SemaphoreType.DMA((count,)),
            pltpu.SemaphoreType.DMA((3, n_dp // 2)),
            pltpu.SemaphoreType.REGULAR,
            pltpu.SemaphoreType.DMA((2,)),
            pltpu.SemaphoreType.DMA((4,)),
        ]
    else:
        outs += [((3,) + BLOCKS, BF)] + blocks
        out_specs = [ANY, ANY, VM, ANY, VM, VM]
    return pl.pallas_call(
        functools.partial(layer_kernel, fused),
        out_shape=[jax.ShapeDtypeStruct(*s) for s in outs],
        in_specs=[ANY, ANY, SM, VM, VM, VM, VM, VM, ANY, ANY],
        out_specs=out_specs,
        scratch_shapes=vmem + extra,
        compiler_params=pltpu.CompilerParams(
            vmem_limit_bytes=63 * 2**20, collective_id=0 if fused else 1, has_side_effects=True
        ),
    )(*args)


def place_kernel(red, cols, wide, grads):
    width = red.shape[1]
    me = lax.axis_index("dp") * lax.axis_size("section") + lax.axis_index("section")
    last = jnp.where(me * width >= 3 * D, wide[3].astype(F32), wide[2].astype(F32)).astype(BF)
    for i, k in enumerate((0, 2, 3)):
        grads[k] = red[i].astype(F32)

    def put(k, value):
        grads[k] = value

    cls_grads([wide[0], wide[1], last], cols, put, lambda v: v)


def place(red, cols, wide):
    return pl.pallas_call(
        place_kernel,
        out_shape=jax.ShapeDtypeStruct((6,) + red.shape[1:], F32),
        in_specs=[VM] * 3,
        out_specs=VM,
        compiler_params=pltpu.CompilerParams(vmem_limit_bytes=56 * 2**20),
    )(red, cols, wide)


def finish_kernel(grads, small, enc, dx, enc_o, dx_o, ga, gm, ab, an, mb, ms, embed, grads_v, enc_v, dx_v, sems):
    loads, stores = Copies(sems.at[0]), Copies(sems.at[1])
    pieces = [(grads.at[i], grads_v.at[i], ga.at[i] if i < 2 else gm.at[i - 2]) for i in range(6)]
    for i in range(4):
        rows = pl.ds(i * (ROWS // 4), ROWS // 4)
        pieces += [(a.at[rows], b.at[rows], c.at[rows]) for a, b, c in ((enc, enc_v, enc_o), (dx, dx_v, dx_o))]
    for src, dst, _ in pieces:
        loads.start(src, dst)
    for k in range(2):
        at = 12 * k
        for i in range(3):
            ab[i, k : k + 1, :] = small[at + i]
            ms[i, k : k + 1, :] = small[at + 9 + i]
        for i in range(2):
            an[k, i : i + 1, :] = small[at + 3 + i]
        for j in range(4):
            mb[k : k + 1, j * D : (j + 1) * D] = small[at + 5 + j]
    for i in range(8):
        embed[i : i + 1, :] = small[24 + i]
    for copy, (_, src, dst) in zip(loads.all, pieces):
        copy.wait()
        stores.start(src, dst)
    for copy in stores.all:
        copy.wait()


def finish(grads, small, enc, dx):
    enc = enc.reshape(ROWS, D)
    width = grads.shape[1]
    shapes = [(2, width, D), (4, width, D), (3, 2, D), (2, 2, D), (2, FF), (3, 2, D), (8, D)]
    outs = [jax.ShapeDtypeStruct((ROWS, D), BF)] * 2 + [jax.ShapeDtypeStruct(s, F32) for s in shapes]
    return pl.pallas_call(
        finish_kernel,
        out_shape=outs,
        in_specs=[ANY, VM, ANY, ANY],
        out_specs=[ANY] * 4 + [VM] * 5,
        scratch_shapes=[
            pltpu.VMEM(grads.shape, F32),
            pltpu.VMEM((ROWS, D), BF),
            pltpu.VMEM((ROWS, D), BF),
            pltpu.SemaphoreType.DMA((2, 14)),
        ],
    )(grads, small, enc, dx)


def on_device(tokens, counts, aw, ab, an, mw, mb, ms, embed, cot):
    n_dp, n_section = lax.axis_size("dp"), lax.axis_size("section")
    ab, ms = ab.swapaxes(0, 1), ms.swapaxes(0, 1)
    aw, mw = aw.reshape((2,) + BLOCKS[1:5] + (4 * D,)), mw.reshape((2, 2) + BLOCKS[1:5] + (FF,))
    fused = (n_dp // 2, 2, 2, 2, FF // (n_dp * n_section), D) == BLOCKS and n_section == 4
    result = layer(fused, n_dp, tokens, cot, counts, ab, ms, an, mb, embed, aw, mw)
    if fused:
        encoded, dx, small, grads = result
    else:
        encoded, dx, small, dw, cols, wide = result
        own = jnp.arange(16) // 8 == lax.axis_index("section") % 2
        cols = jnp.where(own[None, :, None], cols, jnp.zeros_like(cols))
        cols = lax.all_to_all(cols, BOTH, split_axis=2, concat_axis=1, tiled=True)
        wide = lax.all_gather(wide, BOTH, axis=1, tiled=True)
        red = lax.psum_scatter(dw.reshape(3, FF, D), BOTH, scatter_dimension=1, tiled=True)
        small = lax.psum(small, BOTH)
        grads = place(red, cols, wide)
    encoded, dx, ga, gm, g_ab, g_an, g_mb, g_ms, g_embed = finish(grads, small, encoded, dx)
    gm = gm.reshape((2, 2) + gm.shape[1:])
    return (
        encoded,
        dx,
        ga.swapaxes(1, 2),
        g_ab.swapaxes(0, 1),
        g_an,
        gm.swapaxes(2, 3),
        g_mb,
        g_ms.swapaxes(0, 1),
        g_embed,
    )


def solution(mesh):
    return jax.shard_map(
        on_device,
        mesh=mesh,
        in_specs=(P(BOTH, None), P("dp", None)) + (P(),) * 7 + (P(BOTH, None),),
        out_specs=(
            P(BOTH, None),
            P(BOTH, None),
            P(None, None, BOTH),
            P(),
            P(),
            P(None, None, None, BOTH),
            P(),
            P(),
            P(),
        ),
        check_vma=False,
    )
```

```python
import functools
import itertools

import jax
import jax.numpy as jnp
from jax import lax
from jax.experimental import pallas as pl
from jax.experimental.pallas import tpu as pltpu
from jax.sharding import PartitionSpec as P

F32 = jnp.float32
BF = jnp.bfloat16
D = 768
FF = 3072
SEG = 128
HEAD = 64
HEADS = 12
PAIRS = 6
MICRO = 2
SEGS = 12
OWN = 6
ROWS = OWN * SEG
BLOCKS = (4, 2, 2, 2, 96, D)
BOTH = ("dp", "section")
MASKED = -1e30
VM = pl.BlockSpec(memory_space=pltpu.VMEM)
SM = pl.BlockSpec(memory_space=pltpu.SMEM)
ANY = pl.BlockSpec(memory_space=pl.ANY)
MESH = pl.DeviceIdType.MESH


def dot(a, b):
    return jnp.dot(a, b, preferred_element_type=F32)


def dot_nt(a, b):
    return lax.dot_general(a, b, (((1,), (1,)), ((), ())), preferred_element_type=F32)


def dot_tn(a, b):
    return lax.dot_general(a, b, (((0,), (0,)), ((), ())), preferred_element_type=F32)


def gelu_parts(h):
    phi = 0.5 + 0.5 * lax.erf(h * 0.7071067811865476)
    return h * phi, phi + h * (0.3989422804014327 * jnp.exp2((h * h) * -0.7213475204444817))


def norm_rows(r):
    center = r - jnp.mean(r, axis=-1, keepdims=True)
    rstd = lax.rsqrt(jnp.mean(center * center, axis=-1, keepdims=True) + 1e-5)
    return center * rstd, rstd


def norm_back(dy, n, rstd, gain):
    dyg = dy * gain
    return (
        dyg
        - jnp.mean(dyg, axis=-1, keepdims=True)
        - n * jnp.mean(dyg * n, axis=-1, keepdims=True)
    ) * rstd


def halves(v):
    lane = lax.broadcasted_iota(jnp.int32, v.shape, 1)
    zero = jnp.zeros_like(v)
    return jnp.concatenate([jnp.where(lane < HEAD, v, zero), jnp.where(lane < HEAD, zero, v)], 0)


def unhalve(v):
    top, bottom = v[:SEG], v[SEG:]
    lane = lax.broadcasted_iota(jnp.int32, top.shape, 1)
    return jnp.where(lane < HEAD, top, bottom)


def fold8(v):
    return jnp.sum(v.reshape(v.shape[0] // 8, 8, v.shape[1]), axis=0)


def pair_rows(g, h):
    start = (g * PAIRS + h) * 2 * SEG
    return slice(start, start + 2 * SEG)


def block(ref, j):
    return ref[j].reshape(D, D)


def row(ref, *idx):
    if isinstance(ref, tuple):
        return row(ref[idx[0] // 6], idx[0] % 3, idx[0] // 3 % 2)
    i = idx[-1]
    return ref[idx[:-1] + (slice(i, i + 1), slice(None))].astype(F32)


class Copies:
    def __init__(self, sems):
        self.sems, self.all = sems, []

    def start(self, src, dst):
        copy = pltpu.make_async_copy(src, dst, self.sems.at[len(self.all)])
        copy.start()
        self.all.append(copy)
        return copy


def cls_chain(
    own, other, counts, wq, w1, w2, par, an, mb, embed, cols_o, wide_o, small_o
):
    section = lax.axis_index("section")
    per_micro = lax.axis_size("section") // MICRO
    half = lax.rem(section, per_micro)
    micro = section // per_micro
    ends = [counts[micro, 0], counts[micro, 0] + counts[micro, 1]]

    def layout(shape, axis):
        r = lax.broadcasted_iota(jnp.int32, shape, axis)
        seg = jnp.where(r < 8, r, r - 2)
        valid = (r < 6) | ((r >= 8) & (r < 14))
        doc = jnp.where(seg >= ends[0], 1, 0) + jnp.where(seg >= ends[1], 1, 0)
        start = jnp.where(doc == 0, 0, jnp.where(doc == 1, ends[0], ends[1]))
        pos = jnp.where(valid, seg - start, -1)
        return jnp.where(valid, doc, jnp.where(r < 16, 100 + r, -1)), pos, valid

    def order(a, b):
        first = half == 0
        return jnp.concatenate([jnp.where(first, a, b), jnp.where(first, b, a)], axis=0)

    def mine(v):
        return jnp.where(half == 0, v[:8], v[8:])

    doc_q, pos, valid = layout((16, 128), 0)
    doc_k, _, _ = layout((16, 128), 1)
    allowed = jnp.concatenate([doc_q == doc_k] * HEADS, axis=0)
    lanes8 = lax.broadcasted_iota(jnp.int32, (16, 8), 1)
    onehot = (pos[:, :8] == lanes8).astype(BF)
    leaders = order(own[0], other[0]) + dot(onehot, embed[...])
    low = leaders.astype(BF)
    lane = lax.broadcasted_iota(jnp.int32, (16, D), 1) // HEAD

    def stack(v):
        return jnp.concatenate([jnp.where(lane == h, v, jnp.zeros_like(v)) for h in range(HEADS)], 0)

    def unstack(v):
        total = jnp.where(lane == 0, v[:16], 0.0)
        for h in range(1, HEADS):
            total = total + jnp.where(lane == h, v[h * 16 : (h + 1) * 16], 0.0)
        return total

    def deep(v):
        return jnp.concatenate([v, jnp.zeros((112, D), BF)], axis=0)

    q = (dot(low, block(wq, 0)) + row(par, 3)).astype(BF)
    k = dot(low, block(wq, 1)).astype(BF)
    v = (dot(low, block(wq, 2)) + row(par, 4)).astype(BF)
    qs, kd, vd = stack(q), deep(k), deep(v)
    scores = jnp.where(allowed, dot_nt(qs, kd) * 0.125, MASKED)
    e = jnp.exp(scores - jnp.max(scores, axis=-1, keepdims=True))
    probs = e / jnp.sum(e, axis=-1, keepdims=True)
    probs_low = probs.astype(BF)
    ctx = unstack(dot(probs_low, vd)).astype(BF)
    n1, rs1 = norm_rows(leaders + dot(ctx, block(wq, 3)) + row(par, 5))
    third = (n1 * row(an, 1, 0) + row(an, 1, 1)).astype(BF)
    act, gp, v = [], [], third.astype(F32) + row(par, 9)
    for j in range(4):
        a, g = gelu_parts(dot(third, block(w1, j)) + mb[1:2, j * D : (j + 1) * D].astype(F32))
        act.append(a.astype(BF))
        gp.append(g)
        v = v + dot_nt(act[j], block(w2, j))
    n2, rs2 = norm_rows(v)
    fourth = mine(n2 * row(par, 10) + row(par, 11))

    dy = order(own[1], other[1])
    small_o[22] = jnp.sum(mine(dy * n2), axis=0, keepdims=True)
    small_o[23] = jnp.sum(mine(dy), axis=0, keepdims=True)
    dr = norm_back(dy, n2, rs2, row(par, 10))
    dbf = dr.astype(BF)
    small_o[21] = jnp.sum(mine(dbf.astype(F32)), axis=0, keepdims=True)
    dthird = dr
    for j in range(4):
        dh = (dot(dbf, block(w2, j)) * gp[j]).astype(BF)
        dh_mine = mine(dh.astype(F32))
        small_o[17 + j] = jnp.sum(dh_mine, axis=0, keepdims=True)
        cols_o[0, :, j * D : (j + 1) * D] = dh
        cols_o[1, :, j * D : (j + 1) * D] = act[j]
        dthird = dthird + dot_nt(dh, block(w1, j))
    dthird = dthird.astype(BF).astype(F32)
    small_o[15] = jnp.sum(mine(dthird * n1), axis=0, keepdims=True)
    small_o[16] = jnp.sum(mine(dthird), axis=0, keepdims=True)
    dr = norm_back(dthird, n1, rs1, row(an, 1, 0))
    dba = dr.astype(BF)
    small_o[14] = jnp.sum(mine(dba.astype(F32)), axis=0, keepdims=True)
    dctx = stack(dot_nt(dba, block(wq, 3)).astype(BF))
    dp = dot_nt(dctx, vd)
    dv = dot_tn(probs_low, dctx)[:16].astype(BF)
    ds = (probs * (dp - jnp.sum(dp * probs, axis=-1, keepdims=True))).astype(BF)
    dq = (unstack(dot(ds, kd)) * 0.125).astype(BF)
    dk = (dot_tn(ds, qs)[:16] * 0.125).astype(BF)
    small_o[12] = jnp.sum(mine(dq.astype(F32)), axis=0, keepdims=True)
    small_o[13] = jnp.sum(mine(dv.astype(F32)), axis=0, keepdims=True)
    dlead = dr
    for j, piece in enumerate((dq, dk, dv)):
        dlead = dlead + dot_nt(piece, block(wq, j))
    dlead_mine = mine(dlead)
    pos_mine = jnp.where(half == 0, pos[:8], pos[8:])
    for i in range(8):
        hit = jnp.where(pos_mine[:, 0:1] == i, dlead_mine, 0.0)
        small_o[24 + i] = jnp.sum(hit, axis=0, keepdims=True)
    for j, piece in enumerate((dq, dk, dv, dba)):
        cols_o[2, :, j * D : (j + 1) * D] = piece
    for j, piece in enumerate((third, dbf, low, ctx)):
        wide_o[j] = piece
    return fourth, dlead_mine


class Place:
    def __init__(self):
        self.dp, self.section = lax.axis_index("dp"), lax.axis_index("section")
        self.n_dp, self.n_section = lax.axis_size("dp"), lax.axis_size("section")
        self.nz = self.n_dp // 2
        self.z, self.x = self.dp // 2, lax.rem(self.dp, 2)
        self.y, self.c = self.section // 2, lax.rem(self.section, 2)

    def at(self, dz=0, x=None, y=None, c=None):
        x = self.x if x is None else x
        y = self.y if y is None else y
        c = self.c if c is None else c
        return ((self.z + dz) * 2 + x, y * 2 + c)

    def to_x(self):
        return self.at(x=1 - self.x)

    def to_y(self):
        return self.at(y=1 - self.y)

    def to_c(self):
        return self.at(c=1 - self.c)

    def device(self, index):
        return (index // self.n_section, lax.rem(index, self.n_section))


class Links:
    def __init__(self, sends, recvs):
        self.sends, self.recvs, self.used = sends, recvs, 0

    def copy(self, src, dst, peer, recv=None):
        i = self.used
        self.used += 1
        return pltpu.make_async_remote_copy(
            src_ref=src, dst_ref=dst, send_sem=self.sends.at[i], recv_sem=self.recvs.at[i] if recv is None else recv,
            device_id=peer, device_id_type=MESH,
        )


HALF, THIRD = D // 2, D // 3


class Scatter:
    def __init__(self, me, links, held, core, xa, yb, ya, xb, zb, zc, z_recv, c_recv, j):
        self.me, self.held, self.j, self.paired = me, held, j, zc is not None
        self.core, self.xa, self.yb, self.ya, self.xb = core, xa, yb, ya, xb
        x, y, c = me.x, me.y, me.c
        wide = THIRD if self.paired else HALF

        def span(start, size):
            return pl.ds(start, size), slice(start, start + size)

        (a, self.a), (b, self.b) = span(0, wide), span(wide, wide)
        w, self.w = span(0, wide)
        self.core_copy = links.copy(held.at[j, :, :, 1 - c], core.at[j], me.to_c())
        self.xa_copy = links.copy(held.at[j, 1 - x, :, c, :, a], xa.at[j, :, :, w], me.to_x())
        self.yb_copy = links.copy(held.at[j, :, 1 - y, c, :, b], yb.at[j, :, :, w], me.to_y())
        self.ya_copy = links.copy(held.at[j, x, 1 - y, c, :, a], ya.at[j, :, w], me.to_y())
        self.xb_copy = links.copy(held.at[j, 1 - x, y, c, :, b], xb.at[j, :, w], me.to_x())
        target = (j * 2 + x, me.section)
        ab = pl.ds(0, 2 * wide)
        self.z_copy = links.copy(held.at[j, x, y, c, :, ab], zb.at[me.z, :, ab], target, z_recv.at[me.z])
        if not self.paired:
            return
        self.holds = lax.rem(me.z, 2) == j % 2
        self.zc = zc.at[j // 2]
        cc, self.cc = span(2 * THIRD, THIRD)
        (p, self.p), (q, self.q) = span(2 * THIRD, THIRD // 2), span(2 * THIRD + THIRD // 2, THIRD // 2)
        v, self.v = span(THIRD, THIRD // 2)
        self.zc_copy = links.copy(held.at[j, :, :, c, :, cc], self.zc, me.at(dz=1 - 2 * lax.rem(me.z, 2)))
        self.xp_copy = links.copy(held.at[j, 1 - x, :, c, :, p], xa.at[j, :, :, v], me.to_x())
        self.yq_copy = links.copy(held.at[j, :, 1 - y, c, :, q], yb.at[j, :, :, v], me.to_y())
        self.yp_copy = links.copy(held.at[j, x, 1 - y, c, :, p], ya.at[j, :, v], me.to_y())
        self.xq_copy = links.copy(held.at[j, 1 - x, y, c, :, q], xb.at[j, :, v], me.to_x())
        self.zz_copy = links.copy(held.at[j, x, y, c, :, cc], zb.at[me.z, :, cc], target, c_recv)

    def add(self, x, y, cols, value):
        j, c = self.j, self.me.c
        self.held[j, x, y, c, :, cols] = self.held[j, x, y, c, :, cols] + value

    def start(self):
        self.core_copy.start()

    def first(self):
        j, x, y, core = self.j, self.me.x, self.me.y, self.core
        self.core_copy.wait_recv()
        for i in range(2):
            self.add(1 - x, i, self.a, core[j, 1 - x, i, :, self.a])
        self.xa_copy.start()
        for i in range(2):
            self.add(i, 1 - y, self.b, core[j, i, 1 - y, :, self.b])
        self.yb_copy.start()
        if self.paired:
            for i in range(4):
                self.add(i // 2, i % 2, self.cc, core[j, i // 2, i % 2, :, self.cc])

            @pl.when(jnp.logical_not(self.holds))
            def _():
                self.zc_copy.start()

        for i in range(2):
            self.add(x, i, self.a, core[j, x, i, :, self.a])
            self.add(i, y, self.b, core[j, i, y, :, self.b])

    def second(self):
        j, x, y = self.j, self.me.x, self.me.y
        self.xa_copy.wait_recv()
        self.add(x, 1 - y, self.a, self.xa[j, 1 - y, :, self.w])
        self.ya_copy.start()
        self.yb_copy.wait_recv()
        self.add(1 - x, y, self.b, self.yb[j, 1 - x, :, self.w])
        self.xb_copy.start()
        self.add(x, y, self.a, self.xa[j, y, :, self.w])
        self.add(x, y, self.b, self.yb[j, x, :, self.w])

    def third(self):
        j, x, y = self.j, self.me.x, self.me.y
        self.ya_copy.wait_recv()
        self.xb_copy.wait_recv()
        self.add(x, y, self.a, self.ya[j, :, self.w])
        self.add(x, y, self.b, self.xb[j, :, self.w])

        @pl.when(self.me.z != j)
        def _():
            self.z_copy.start()

    def pair_first(self):
        x, y = self.me.x, self.me.y

        @pl.when(self.holds)
        def _():
            self.zc_copy.wait_recv()
            for i in range(2):
                self.add(1 - x, i, self.p, self.zc[1 - x, i, :, 0 : THIRD // 2])
            self.xp_copy.start()
            for i in range(2):
                self.add(i, 1 - y, self.q, self.zc[i, 1 - y, :, THIRD // 2 :])
            self.yq_copy.start()
            for i in range(2):
                self.add(x, i, self.p, self.zc[x, i, :, 0 : THIRD // 2])
                self.add(i, y, self.q, self.zc[i, y, :, THIRD // 2 :])

    def pair_second(self):
        j, x, y = self.j, self.me.x, self.me.y

        @pl.when(self.holds)
        def _():
            self.xp_copy.wait_recv()
            self.add(x, 1 - y, self.p, self.xa[j, 1 - y, :, self.v])
            self.yp_copy.start()
            self.yq_copy.wait_recv()
            self.add(1 - x, y, self.q, self.yb[j, 1 - x, :, self.v])
            self.xq_copy.start()
            self.add(x, y, self.p, self.xa[j, y, :, self.v])
            self.add(x, y, self.q, self.yb[j, x, :, self.v])

    def pair_third(self):
        j, x, y = self.j, self.me.x, self.me.y

        @pl.when(self.holds)
        def _():
            self.yp_copy.wait_recv()
            self.xq_copy.wait_recv()
            self.add(x, y, self.p, self.ya[j, :, self.v])
            self.add(x, y, self.q, self.xb[j, :, self.v])

            @pl.when(self.me.z != j)
            def _():
                self.zz_copy.start()

    def drain(self):
        for copy in (self.core_copy, self.xa_copy, self.yb_copy, self.ya_copy, self.xb_copy):
            copy.wait_send()

        @pl.when(self.me.z != self.j)
        def _():
            self.z_copy.wait_send()

        if self.paired:

            @pl.when(jnp.logical_not(self.holds))
            def _():
                self.zc_copy.wait_send()

            @pl.when(self.holds)
            def _():
                for copy in (self.xp_copy, self.yq_copy, self.yp_copy, self.xq_copy):
                    copy.wait_send()

                @pl.when(self.me.z != self.j)
                def _():
                    self.zz_copy.wait_send()


class Matrix:
    def __init__(self, me, links, z_recv, c_recv, held, core, xa, yb, ya, xb, zb, zc):
        self.me, self.held, self.zb, self.paired = me, held, zb, zc is not None
        buffers = (core, xa, yb, ya, xb, zb, zc)
        self.units = [Scatter(me, links, held, *buffers, z_recv, c_recv, j) for j in range(me.nz)]
        self.z_recv, self.c_recv = z_recv, c_recv

    def arrival(self, i, cols, sem):
        part = self.zb.at[i, :, cols]
        return pltpu.make_async_remote_copy(
            src_ref=part, dst_ref=part, send_sem=sem, recv_sem=sem,
            device_id=(self.me.dp, self.me.section), device_id_type=MESH,
        )

    def finish(self, total):
        me = self.me
        for unit in self.units:
            unit.drain()
        total[...] = self.held[me.z, me.x, me.y, me.c].astype(F32)
        cols = 2 * THIRD if self.paired else D
        for i in range(me.nz):

            @pl.when(me.z != i)
            def _():
                self.arrival(i, pl.ds(0, cols), self.z_recv.at[i]).wait_recv()
                total[:, 0:cols] += self.zb[i, :, 0:cols].astype(F32)

            if self.paired:

                @pl.when(lax.rem(me.z + 2, me.nz) == i)
                def _():
                    self.arrival(i, pl.ds(cols, THIRD), self.c_recv).wait_recv()
                    total[:, cols:] += self.zb[i, :, cols:].astype(F32)


def scatter_buffers(nz, width):
    shapes = [(nz, 2, 2, width, D)] + [(nz, 2, width, HALF)] * 2 + [(nz, width, HALF)] * 2
    return shapes + [(nz, width, D), (nz // 2, 2, 2, width, THIRD)]


class Gather:
    def __init__(self, me, links, wide, cols, all_wide, all_cols):
        self.me, self.all_wide, self.all_cols = me, all_wide, all_cols
        self.wide, self.cols = wide, cols
        self.span = cols.shape[-1] // me.n_dp
        self.copies = [[], [], []]
        for c in range(2):
            w, k = (pl.ds(0, 2), pl.ds(0, 1)) if c == 0 else (pl.ds(2, 1), pl.ds(1, 2))
            given = [wide.at[me.y, pl.ds(2 * c, 2)], cols.at[me.y, k]]
            self.copies[0].append([links.copy(a, a, me.to_y()) for a in given])
            spread = []
            for i in range(1, me.n_dp):
                peer = lax.rem(me.dp + i, me.n_dp)
                spread.append(links.copy(self.given(c, peer), all_wide.at[me.dp, :, w], (peer, me.section)))
                spread.append(links.copy(self.part(k, peer), all_cols.at[me.dp, :, k], (peer, me.section)))
            self.copies[1].append(spread)
            beside = [all_wide.at[:, :, w], all_cols.at[:, :, k]]
            self.copies[2].append([links.copy(a, a, me.to_c()) for a in beside])

    def given(self, c, peer):
        if c == 0:
            return self.wide.at[:, pl.ds(0, 2)]
        return self.wide.at[:, pl.ds(2 + peer * self.span // (3 * D), 1)]

    def part(self, k, peer):
        return self.cols.at[:, k, :, pl.ds(pl.multiple_of(peer * self.span, 128), self.span)]

    def each(self, do):
        for c in range(2):

            @pl.when(self.me.c == c)
            def _():
                do(c)

    def start(self):
        def go(c):
            for copy in self.copies[0][c]:
                copy.start()

        self.each(go)

    def second(self):
        me = self.me

        def go(c):
            for copy in self.copies[0][c]:
                copy.wait()
            for copy in self.copies[1][c]:
                copy.start()
            w, k = (slice(0, 2), slice(0, 1)) if c == 0 else (slice(2, 3), slice(1, 3))
            self.all_wide[me.dp, :, w] = self.given(c, me.dp)[...]
            self.all_cols[me.dp, :, k] = self.part(pl.ds(k.start, k.stop - k.start), me.dp)[...]

        self.each(go)

    def third(self):
        def go(c):
            for copy in self.copies[1][c]:
                copy.wait()
            for copy in self.copies[2][c]:
                copy.start()

        self.each(go)

    def finish(self):
        def go(c):
            for copy in self.copies[2][c]:
                copy.wait_send()
            for copy in self.copies[2][1 - c]:
                copy.wait_recv()

        self.each(go)


class Total:
    def __init__(self, me, acc, got, out, sems):
        self.me, self.acc, self.got, self.out, self.sems = me, acc, got, out, sems
        self.count = acc.shape[0]
        self.index = me.dp * me.n_section + me.section

    def send(self, phase):
        @pl.loop(1, self.count)
        def _(i):
            peer = lax.rem(self.index + i, self.count)
            src = self.acc.at[peer] if phase == 0 else self.out.at[self.index]
            dst = (self.got if phase == 0 else self.out).at[self.index]
            pltpu.make_async_remote_copy(
                src_ref=src, dst_ref=dst, send_sem=self.sems.at[2 * phase], recv_sem=self.sems.at[2 * phase + 1],
                device_id=self.me.device(peer), device_id_type=MESH,
            ).start()

    def wait(self, phase):
        rows = self.got.at[pl.ds(0, self.count - 1)]
        for i in range(2):
            pltpu.make_async_copy(rows, rows, self.sems.at[2 * phase + i]).wait()

    def step(self, i):
        if i == 0:
            self.got[self.index] = self.acc[self.index]
            self.send(0)
        elif i == 1:
            self.wait(0)
            self.out[self.index] = jnp.sum(self.got[...], axis=0)
            self.send(1)
        else:
            self.wait(1)


def pick_own(me, width):
    def pick(v):
        out = v[:, :width]
        for s in range(1, 4):
            out = jnp.where(me.section == s, v[:, s * width : (s + 1) * width], out)
        return out

    return pick


N_SET = 7
BLOCK_ORDER = (0, 2, 1, 3)
PAIRED = (False, True, True)
QKV_ORDER = (0, 2, 1)
PLAN = {
    "ffnout0": (
        ("g", 0, 0),
    ),
    "dwout0": (
        ("o", 0, 0),
    ),
    "dwout2": (
        ("o", 2, 0),
    ),
    "dwout1": (
        ("o", 1, 0),
        ("o", 0, 1),
    ),
    "dwout3": (
        ("o", 3, 0),
    ),
    "dh0": (
        ("o", 2, 1),
    ),
    "dh2": (
        ("o", 1, 1),
    ),
    "dwin0": (
        ("i", 0, 0),
        ("o", 3, 1),
        ("f", 0, 0),
    ),
    "dwin2": (
        ("i", 2, 0),
        ("o", 0, 2),
    ),
    "dwin1": (
        ("i", 1, 0),
        ("i", 0, 1),
    ),
    "dwin3": (
        ("i", 3, 0),
        ("o", 2, 2),
    ),
    "dfirst0": (
        ("o", 1, 2),
        ("i", 2, 1),
    ),
    "dfirst1": (
        ("o", 0, 4),
        ("o", 1, 4),
        ("g", 1, 0),
        ("o", 0, 3),
        ("o", 3, 2),
    ),
    "dwo": (
        ("f", 0, 1),
        ("a", 3, 0),
        ("i", 0, 2),
    ),
    "dctx": (
        ("g", 2, 0),
        ("o", 2, 4),
        ("o", 3, 4),
        ("o", 2, 3),
        ("o", 1, 3),
        ("i", 1, 1),
        ("i", 3, 1),
        ("i", 2, 2),
    ),
    "att0": (
        ("o", 0, 5),
        ("o", 1, 5),
        ("i", 0, 4),
        ("o", 3, 3),
    ),
    "att1": (
        ("i", 0, 3),
    ),
    "att2": (
        ("o", 2, 5),
        ("o", 3, 5),
        ("a", 3, 1),
    ),
    "att3": (
        ("i", 2, 4),
        ("i", 1, 2),
    ),
    "att5": (
        ("i", 3, 2),
    ),
    "dwqkv0": (
        ("a", 0, 0),
        ("o", 0, 6),
        ("o", 1, 6),
        ("o", 2, 6),
        ("o", 3, 6),
        ("i", 0, 5),
        ("i", 1, 4),
        ("i", 2, 3),
    ),
    "dwqkv2": (
        ("a", 2, 0),
        ("a", 0, 1),
    ),
    "dwqkv1": (
        ("a", 1, 0),
    ),
    "sums": (
        ("s", 0, 0),
        ("i", 2, 5),
        ("i", 3, 4),
        ("i", 1, 3),
        ("i", 3, 3),
        ("i", 0, 6),
        ("a", 3, 2),
    ),
    "dx0": (
        ("i", 1, 5),
        ("a", 2, 1),
    ),
    "dx1": (
        ("a", 0, 2),
    ),
    "tail": (
        ("p", 3, 0),
        ("i", 2, 6),
        ("i", 3, 5),
        ("a", 1, 1),
        ("a", 3, 3),
        ("i", 1, 6),
        ("s", 1, 0),
        ("a", 2, 2),
        ("a", 0, 3),
        ("i", 3, 6),
        ("a", 1, 2),
        ("a", 2, 3),
        ("a", 1, 3),
        ("s", 2, 0),
        ("p", 2, 0),
        ("p", 0, 0),
    ),
}


def cls_grads(wide, cols, put, pick):
    for i, k in enumerate((4, 5, 1)):
        put(k, dot_tn(pick(cols[i]), wide[i]))


class Net:
    def __init__(self, mats, acc, out, wide, cols, grads, scratch):
        sets = [scratch[i * N_SET : (i + 1) * N_SET] for i in range(3)]
        sets[0] = sets[2][:1] + sets[0][1:]
        sets = [part if PAIRED[m] else part[:-1] + (None,) for m, part in enumerate(sets)]
        all_wide, all_cols, got, self.stage, sends, recvs, z_recvs, c_recvs, self.free, self.out_sems, sum_sems = scratch[3 * N_SET :]
        self.outs = []
        self.me, self.grads = Place(), grads
        links = Links(sends, recvs)
        self.attn, self.win, self.wout = [
            Matrix(self.me, links, z_recvs.at[m], c_recvs.at[m], mats[m], *sets[m]) for m in range(3)
        ]
        self.gather = Gather(self.me, links, wide, cols, all_wide, all_cols)
        self.summed = Total(self.me, acc, got, out, sum_sems)

    def slot(self):
        i = len(self.outs)
        if i >= 2:
            self.outs[i - 2].wait()
        return self.stage.at[i % 2]

    def put(self, k):
        i = len(self.outs)
        copy = pltpu.make_async_copy(self.stage.at[i % 2], self.grads.at[k], self.out_sems.at[i % 2])
        copy.start()
        self.outs.append(copy)

    def cls(self):
        self.gather.finish()
        width = self.stage.shape[1]
        rows = 16 * 2 * self.me.n_dp
        wide = [self.gather.all_wide[:, :, i].reshape(rows, D) for i in range(3)]
        cols = [self.gather.all_cols[:, :, i].reshape(rows, 4 * width) for i in range(3)]

        def put(k, value):
            self.slot()[...] = value
            self.put(k)

        cls_grads(wide, cols, put, pick_own(self.me, width))

    def place(self, which, k):
        which.finish(self.slot())
        self.put(k)

    def after(self, name):
        kinds = {"a": self.attn.units, "i": self.win.units, "o": self.wout.units}
        for step in PLAN.get(name, ()):
            kind, number, phase = step
            if kind == "g":
                (self.gather.second, self.gather.third, self.cls)[number]()
            elif kind == "s":
                self.summed.step(number)
            elif kind == "p":
                self.place((self.attn, None, self.win, self.wout)[number], number)
            elif kind == "f":
                if phase == 0:
                    pl.semaphore_signal(self.free, inc=1, device_id=self.me.to_c(), device_id_type=MESH)
                else:
                    pl.semaphore_wait(self.free, 1)
            else:
                unit = kinds[kind][number]
                parts = (unit.start, unit.first, unit.second, unit.third)
                (parts + (unit.pair_first, unit.pair_second, unit.pair_third))[phase]()


def layer_kernel(fused, x_i, cot, counts, ab, ms, an, mb, embed, aw, mw, enc_o, dx_o, small_o, *refs):
    par = (ab, ms)
    if fused:
        grads_o, refs = refs[0], refs[1:]
    else:
        dw_o, refs = refs[0], refs[1:]
    cols, wide, a0, win0, wout0, a1, v1, v2, first, n1, db, x, rs1, qkv, p, ctx = refs[:16]
    heads, rows16, mine, theirs, sums, wsem, osem, ssem, rsem = refs[16:25]
    act, gp, dwout = v1, v2, a1
    mats = (gp, act, dwout)
    loads = Copies(wsem)

    def load(src, dst):
        return [loads.start(src.at[:, :, :, :, j * D : (j + 1) * D], dst.at[j]) for j in range(4)]

    x_in = loads.start(x_i, x)
    a0_in = load(aw.at[0], a0)
    heads_in = [loads.start(cot.at[pl.ds(g * SEG, 16)], heads.at[g]) for g in range(OWN)]
    win0_in, wout0_in = load(mw.at[0, 0], win0), load(mw.at[0, 1], wout0)
    cls_in = load(aw.at[1], a1) + load(mw.at[1, 0], v1) + load(mw.at[1, 1], v2)
    cot_in = loads.start(cot, db)

    section = lax.axis_index("section")
    partner = (lax.axis_index("dp"), section + 1 - 2 * lax.rem(section, 2))
    barrier = pltpu.get_barrier_semaphore()
    if fused:
        small, refs = refs[25], refs[:25] + refs[26:]
        net = Net(mats, small, small_o, wide, cols, grads_o, refs[25:])
        expected = net.me.n_dp * net.me.n_section - 1

        @pl.loop(1, expected + 1)
        def _(i):
            peer = net.me.device(lax.rem(net.summed.index + i, expected + 1))
            pl.semaphore_signal(barrier, inc=1, device_id=peer, device_id_type=MESH)
    else:
        small, expected = small_o, 1
        pl.semaphore_signal(barrier, inc=1, device_id=partner, device_id_type=MESH)

    def after(name):
        if fused:
            net.after(name)

    swaps = [
        pltpu.make_async_remote_copy(
            src_ref=mine.at[i], dst_ref=theirs.at[i], send_sem=ssem.at[i], recv_sem=rsem.at[i],
            device_id=partner, device_id_type=MESH,
        )
        for i in range(2)
    ]

    x_in.wait()
    for j in range(3):
        a0_in[j].wait()
        v = dot(x[...], block(a0, j))
        if j != 1:
            v = v + row(par, j // 2)
        qkv[:, j * D : (j + 1) * D] = v.astype(BF)
    for g, h in itertools.product(range(OWN), range(PAIRS)):
        rows, c = slice(g * SEG, (g + 1) * SEG), slice(h * 128, (h + 1) * 128)
        q = qkv[rows, c] * jnp.asarray(0.125, BF)
        kc = halves(qkv[rows, D + h * 128 : D + (h + 1) * 128])
        vc = halves(qkv[rows, 2 * D + h * 128 : 2 * D + (h + 1) * 128])
        scores = dot_nt(kc, q)
        ps = []
        for i in range(2):
            si = scores[i * SEG : (i + 1) * SEG]
            e = jnp.exp(si - jnp.max(si, axis=0, keepdims=True))
            ps.append((e / jnp.sum(e, axis=0, keepdims=True)).astype(BF))
        pt = jnp.concatenate(ps, axis=0)
        p[pair_rows(g, h), :] = pt
        ctx[rows, c] = dot_tn(pt, vc).astype(BF)

    mine[...] = jnp.zeros_like(mine)
    rows16[...] = jnp.zeros_like(rows16)
    for copy in heads_in:
        copy.wait()
    for g in range(OWN):
        mine[1, g : g + 1, :] = heads[g, 0:1, :].astype(F32)
        rows16[0, g : g + 1, :] = x[g * SEG : g * SEG + 1, :].astype(F32)
        rows16[1, g : g + 1, :] = ctx[g * SEG : g * SEG + 1, :].astype(F32)
    pl.semaphore_wait(barrier, expected)
    swaps[1].start()
    a0_in[3].wait()
    n, _ = norm_rows(rows16[0] + dot(rows16[1].astype(BF), block(a0, 3)) + row(par, 2))
    low = (n * row(an, 0, 0) + row(an, 0, 1)).astype(BF)
    v = low.astype(F32) + row(par, 6)
    for j in range(4):
        win0_in[j].wait()
        wout0_in[j].wait()
        a, _ = gelu_parts(dot(low, block(win0, j)) + mb[0:1, j * D : (j + 1) * D].astype(F32))
        v = v + dot_nt(a.astype(BF), block(wout0, j))
    n, _ = norm_rows(v)
    value = (n * row(par, 7) + row(par, 8)).astype(BF).astype(F32)
    mine[0] = jnp.where(lax.broadcasted_iota(jnp.int32, (8, D), 0) < OWN, value[:8], 0.0)
    swaps[0].start()

    for half in range(2):
        rows = slice(half * 384, half * 384 + 384)
        v = dot(ctx[rows, :], block(a0, 3)) + x[rows, :].astype(F32) + row(par, 2)
        n, rs = norm_rows(v)
        n1[rows, :] = n.astype(BF)
        rs1[rows, :] = rs
        first[rows, :] = (n * row(an, 0, 0) + row(an, 0, 1)).astype(BF)
    for copy in cls_in:
        copy.wait()
    for swap in swaps:
        swap.wait()
    if fused:
        cols_o, wide_o = cols.at[net.me.y], wide.at[net.me.y]
    else:
        cols_o, wide_o = cols, wide
    fourth, dlead = cls_chain(mine, theirs, counts, a1, v1, v2, par, an, mb, embed, cols_o, wide_o, small)
    lead = dlead.astype(BF).astype(F32)

    for j in range(4):
        a, g = gelu_parts(dot(first[...], block(win0, j)) + mb[0:1, j * D : (j + 1) * D].astype(F32))
        act[j] = a.astype(BF).reshape(BLOCKS[1:])
        gp[j] = g.astype(BF).reshape(BLOCKS[1:])
        if fused and j == 0:
            net.gather.start()
        after(f"ffnin{j}")

    def norm_step(rows, dy, n, rs, gain, at):
        low = norm_back(dy, n, rs, gain).astype(BF)
        db[rows, :] = low
        for i, v in enumerate((low.astype(F32), dy * n, dy)):
            sums[at + i] = fold8(v) if rows.start == 0 else sums[at + i] + fold8(v)

    def put(ref, j, value):
        ref[j] = value.astype(BF).reshape(BLOCKS[1:])

    cot_in.wait()
    at = lax.broadcasted_iota(jnp.int32, (384, D), 0)
    for half in range(2):
        rows = slice(half * 384, half * 384 + 384)
        v = first[rows, :].astype(F32) + row(par, 6)
        for j in range(4):
            v = v + dot_nt(act[j, half].reshape(384, D), block(wout0, j))
        n, rs = norm_rows(v)
        value, dy = n * row(par, 7) + row(par, 8), db[rows, :].astype(F32)
        for g in range(3):
            value = jnp.where(at == g * SEG, fourth[3 * half + g : 3 * half + g + 1], value)
            dy = jnp.where(at == g * SEG, lead[3 * half + g : 3 * half + g + 1], dy)
        dwout[2, half] = value.astype(BF).reshape(BLOCKS[2:])
        norm_step(rows, dy, n, rs, row(par, 7), 0)
        after(f"ffnout{half}")
    enc_out = pltpu.make_async_copy(dwout.at[2], enc_o, osem.at[0])
    enc_out.start()

    for j in BLOCK_ORDER:
        if j == 2:
            enc_out.wait()
        put(dwout, j, dot_tn(block(act, j), db[...]))
        after(f"dwout{j}")
    for j in range(4):
        low = (dot(db[...], block(wout0, j)) * block(gp, j).astype(F32)).astype(BF)
        put(gp, j, low)
        sums[6 + j] = fold8(low.astype(F32))
        after(f"dh{j}")
    for j in BLOCK_ORDER:
        put(act, j, dot_tn(block(gp, j), first[...]))
        after(f"dwin{j}")
    for half in range(2):
        rows = slice(half * 384, half * 384 + 384)
        v = db[rows, :].astype(F32)
        for j in range(4):
            v = v + dot_nt(gp[j, half].reshape(384, D), block(win0, j))
        norm_step(rows, v.astype(BF).astype(F32), n1[rows, :].astype(F32), rs1[rows, :], row(an, 0, 0), 3)
        after(f"dfirst{half}")

    put(gp, 3, dot_tn(db[...], ctx[...]))
    after("dwo")
    dctx = first
    dctx[...] = dot_nt(db[...], block(a0, 3)).astype(BF)
    after("dctx")

    def attention(g):
        rows = slice(g * SEG, (g + 1) * SEG)
        for h in range(PAIRS):
            cq = slice(h * 128, (h + 1) * 128)
            ck = slice(D + h * 128, D + (h + 1) * 128)
            cv = slice(2 * D + h * 128, 2 * D + (h + 1) * 128)
            q, dc, pt = qkv[rows, cq], dctx[rows, cq], p[pair_rows(g, h), :]
            kc, vc = halves(qkv[rows, ck]), halves(qkv[rows, cv])
            dp, pf = dot_nt(vc, dc), pt.astype(F32)
            ds = []
            for i in range(2):
                pi, di = pf[i * SEG : (i + 1) * SEG], dp[i * SEG : (i + 1) * SEG]
                ds.append((pi * (di - jnp.sum(pi * di, axis=0, keepdims=True))).astype(BF))
            ds = jnp.concatenate(ds, axis=0)
            qkv[rows, cq] = (dot_tn(ds, kc) * 0.125).astype(BF)
            qkv[rows, ck] = (unhalve(dot(ds, q)) * 0.125).astype(BF)
            qkv[rows, cv] = unhalve(dot(pt, dc)).astype(BF)

    for g in range(OWN):
        attention(g)
        after(f"att{g}")
    for j in QKV_ORDER:
        s = slice(j * D, (j + 1) * D)
        put(gp, j, dot_tn(qkv[:, s], x[...]))
        if j != 1:
            sums[10 + j // 2] = fold8(qkv[:, s].astype(F32))
        after(f"dwqkv{j}")
    for i, k in enumerate((10, 11, 3, 4, 5, 6, 7, 8, 9, 0, 1, 2)):
        small[i] = jnp.sum(sums[k], axis=0, keepdims=True)
    after("sums")
    if not fused:
        outs = [pltpu.make_async_copy(mats[i], dw_o.at[i], osem.at[1 + i]) for i in range(3)]
        for copy in outs:
            copy.start()
    for half in range(2):
        rows = slice(half * 384, half * 384 + 384)
        v = db[rows, :].astype(F32)
        for j in range(3):
            v = v + dot_nt(qkv[rows, j * D : (j + 1) * D], block(a0, j))
        db[rows, :] = v.astype(BF)
        after(f"dx{half}")
    dx_out = pltpu.make_async_copy(db, dx_o, osem.at[0])
    dx_out.start()
    if not fused:
        for copy in outs + [dx_out]:
            copy.wait()
        return
    after("tail")
    dx_out.wait()
    for copy in net.outs[-2:]:
        copy.wait()


def layer(fused, n_dp, *args):
    width = FF // (4 * n_dp)
    outs = [(BLOCKS[1:], BF), ((ROWS, D), BF), ((32, 1, D), F32)]
    blocks = [((3, 16, FF), BF), ((4, 16, D), BF)]
    buffers = [(BLOCKS, BF)] * 6 + [((ROWS, D), BF)] * 4
    buffers += [((ROWS, 1), F32), ((ROWS, 3 * D), BF), ((OWN * PAIRS * 2 * SEG, SEG), BF), ((ROWS, D), BF)]
    buffers += [((OWN, 16, D), BF), ((2, 16, D), F32), ((2, 8, D), F32), ((2, 8, D), F32), ((12, 8, D), F32)]
    sems = [32, 4, 2, 2]
    vmem, extra = [pltpu.VMEM(*b) for b in buffers], []
    vmem += [pltpu.SemaphoreType.DMA((n,)) for n in sems]
    if fused:
        outs += [((6, width, D), F32)]
        out_specs = [ANY, ANY, VM, ANY]
        vmem = [pltpu.VMEM((2,) + shape, dt) for shape, dt in blocks] + vmem
        count = (6 * 3 + 6 * 2) * (n_dp // 2) + 4 * (n_dp - 1) + 8
        parts = [pltpu.VMEM(s, BF) for s in scatter_buffers(n_dp // 2, width)]
        extra = [pltpu.VMEM((32, 1, D), F32), pltpu.VMEM((16, 128), BF)] + parts[1:-1]
        extra += [pltpu.VMEM((16, 128), BF)] + parts * 2
        extra += [
            pltpu.VMEM((n_dp, 2, 3, 16, D), BF),
            pltpu.VMEM((n_dp, 2, 3, 16, 4 * width), BF),
            pltpu.VMEM((32, 1, D), F32),
            pltpu.VMEM((2, width, D), F32),
            pltpu.SemaphoreType.DMA((count,)),
            pltpu.SemaphoreType.DMA((count,)),
            pltpu.SemaphoreType.DMA((3, n_dp // 2)),
            pltpu.SemaphoreType.DMA((3,)),
            pltpu.SemaphoreType.REGULAR,
            pltpu.SemaphoreType.DMA((2,)),
            pltpu.SemaphoreType.DMA((4,)),
        ]
    else:
        outs += [((3,) + BLOCKS, BF)] + blocks
        out_specs = [ANY, ANY, VM, ANY, VM, VM]
    return pl.pallas_call(
        functools.partial(layer_kernel, fused),
        out_shape=[jax.ShapeDtypeStruct(*s) for s in outs],
        in_specs=[ANY, ANY, SM, VM, VM, VM, VM, VM, ANY, ANY],
        out_specs=out_specs,
        scratch_shapes=vmem + extra,
        compiler_params=pltpu.CompilerParams(
            vmem_limit_bytes=63 * 2**20, collective_id=0 if fused else 1, has_side_effects=True
        ),
    )(*args)


def place_kernel(red, cols, wide, grads):
    width = red.shape[1]
    me = lax.axis_index("dp") * lax.axis_size("section") + lax.axis_index("section")
    last = jnp.where(me * width >= 3 * D, wide[3].astype(F32), wide[2].astype(F32)).astype(BF)
    for i, k in enumerate((0, 2, 3)):
        grads[k] = red[i].astype(F32)

    def put(k, value):
        grads[k] = value

    cls_grads([wide[0], wide[1], last], cols, put, lambda v: v)


def place(red, cols, wide):
    return pl.pallas_call(
        place_kernel,
        out_shape=jax.ShapeDtypeStruct((6,) + red.shape[1:], F32),
        in_specs=[VM] * 3,
        out_specs=VM,
        compiler_params=pltpu.CompilerParams(vmem_limit_bytes=56 * 2**20),
    )(red, cols, wide)


def finish_kernel(grads, small, enc, dx, enc_o, dx_o, ga, gm, ab, an, mb, ms, embed, grads_v, enc_v, dx_v, sems):
    loads, stores = Copies(sems.at[0]), Copies(sems.at[1])
    pieces = [(grads.at[i], grads_v.at[i], ga.at[i] if i < 2 else gm.at[i - 2]) for i in range(6)]
    for i in range(4):
        rows = pl.ds(i * (ROWS // 4), ROWS // 4)
        pieces += [(a.at[rows], b.at[rows], c.at[rows]) for a, b, c in ((enc, enc_v, enc_o), (dx, dx_v, dx_o))]
    for src, dst, _ in pieces:
        loads.start(src, dst)
    for k in range(2):
        at = 12 * k
        for i in range(3):
            ab[i, k : k + 1, :] = small[at + i]
            ms[i, k : k + 1, :] = small[at + 9 + i]
        for i in range(2):
            an[k, i : i + 1, :] = small[at + 3 + i]
        for j in range(4):
            mb[k : k + 1, j * D : (j + 1) * D] = small[at + 5 + j]
    for i in range(8):
        embed[i : i + 1, :] = small[24 + i]
    for copy, (_, src, dst) in zip(loads.all, pieces):
        copy.wait()
        stores.start(src, dst)
    for copy in stores.all:
        copy.wait()


def finish(grads, small, enc, dx):
    enc = enc.reshape(ROWS, D)
    width = grads.shape[1]
    shapes = [(2, width, D), (4, width, D), (3, 2, D), (2, 2, D), (2, FF), (3, 2, D), (8, D)]
    outs = [jax.ShapeDtypeStruct((ROWS, D), BF)] * 2 + [jax.ShapeDtypeStruct(s, F32) for s in shapes]
    return pl.pallas_call(
        finish_kernel,
        out_shape=outs,
        in_specs=[ANY, VM, ANY, ANY],
        out_specs=[ANY] * 4 + [VM] * 5,
        scratch_shapes=[
            pltpu.VMEM(grads.shape, F32),
            pltpu.VMEM((ROWS, D), BF),
            pltpu.VMEM((ROWS, D), BF),
            pltpu.SemaphoreType.DMA((2, 14)),
        ],
    )(grads, small, enc, dx)


def on_device(tokens, counts, aw, ab, an, mw, mb, ms, embed, cot):
    n_dp, n_section = lax.axis_size("dp"), lax.axis_size("section")
    ab, ms = ab.swapaxes(0, 1), ms.swapaxes(0, 1)
    aw, mw = aw.reshape((2,) + BLOCKS[1:5] + (4 * D,)), mw.reshape((2, 2) + BLOCKS[1:5] + (FF,))
    fused = (n_dp // 2, 2, 2, 2, FF // (n_dp * n_section), D) == BLOCKS and n_section == 4
    result = layer(fused, n_dp, tokens, cot, counts, ab, ms, an, mb, embed, aw, mw)
    if fused:
        encoded, dx, small, grads = result
    else:
        encoded, dx, small, dw, cols, wide = result
        own = jnp.arange(16) // 8 == lax.axis_index("section") % 2
        cols = jnp.where(own[None, :, None], cols, jnp.zeros_like(cols))
        cols = lax.all_to_all(cols, BOTH, split_axis=2, concat_axis=1, tiled=True)
        wide = lax.all_gather(wide, BOTH, axis=1, tiled=True)
        red = lax.psum_scatter(dw.reshape(3, FF, D), BOTH, scatter_dimension=1, tiled=True)
        small = lax.psum(small, BOTH)
        grads = place(red, cols, wide)
    encoded, dx, ga, gm, g_ab, g_an, g_mb, g_ms, g_embed = finish(grads, small, encoded, dx)
    gm = gm.reshape((2, 2) + gm.shape[1:])
    return (
        encoded,
        dx,
        ga.swapaxes(1, 2),
        g_ab.swapaxes(0, 1),
        g_an,
        gm.swapaxes(2, 3),
        g_mb,
        g_ms.swapaxes(0, 1),
        g_embed,
    )


def solution(mesh):
    return jax.shard_map(
        on_device,
        mesh=mesh,
        in_specs=(P(BOTH, None), P("dp", None)) + (P(),) * 7 + (P(BOTH, None),),
        out_specs=(
            P(BOTH, None),
            P(BOTH, None),
            P(None, None, BOTH),
            P(),
            P(),
            P(None, None, None, BOTH),
            P(),
            P(),
            P(),
        ),
        check_vma=False,
    )
```

```python
import functools
import itertools

import jax
import jax.numpy as jnp
from jax import lax
from jax.experimental import pallas as pl
from jax.experimental.pallas import tpu as pltpu
from jax.sharding import PartitionSpec as P

F32 = jnp.float32
BF = jnp.bfloat16
D = 768
FF = 3072
SEG = 128
HEAD = 64
HEADS = 12
PAIRS = 6
MICRO = 2
SEGS = 12
OWN = 6
ROWS = OWN * SEG
BLOCKS = (4, 2, 2, 2, 96, D)
BOTH = ("dp", "section")
MASKED = -1e30
VM = pl.BlockSpec(memory_space=pltpu.VMEM)
SM = pl.BlockSpec(memory_space=pltpu.SMEM)
ANY = pl.BlockSpec(memory_space=pl.ANY)
MESH = pl.DeviceIdType.MESH


def dot(a, b):
    return jnp.dot(a, b, preferred_element_type=F32)


def dot_nt(a, b):
    return lax.dot_general(a, b, (((1,), (1,)), ((), ())), preferred_element_type=F32)


def dot_tn(a, b):
    return lax.dot_general(a, b, (((0,), (0,)), ((), ())), preferred_element_type=F32)


def gelu_parts(h):
    phi = 0.5 + 0.5 * lax.erf(h * 0.7071067811865476)
    return h * phi, phi + h * (0.3989422804014327 * jnp.exp2((h * h) * -0.7213475204444817))


def norm_rows(r):
    center = r - jnp.mean(r, axis=-1, keepdims=True)
    rstd = lax.rsqrt(jnp.mean(center * center, axis=-1, keepdims=True) + 1e-5)
    return center * rstd, rstd


def norm_back(dy, n, rstd, gain):
    dyg = dy * gain
    return (
        dyg
        - jnp.mean(dyg, axis=-1, keepdims=True)
        - n * jnp.mean(dyg * n, axis=-1, keepdims=True)
    ) * rstd


def halves(v):
    lane = lax.broadcasted_iota(jnp.int32, v.shape, 1)
    zero = jnp.zeros_like(v)
    return jnp.concatenate([jnp.where(lane < HEAD, v, zero), jnp.where(lane < HEAD, zero, v)], 0)


def unhalve(v):
    top, bottom = v[:SEG], v[SEG:]
    lane = lax.broadcasted_iota(jnp.int32, top.shape, 1)
    return jnp.where(lane < HEAD, top, bottom)


def fold8(v):
    return jnp.sum(v.reshape(v.shape[0] // 8, 8, v.shape[1]), axis=0)


def pair_rows(g, h):
    start = (g * PAIRS + h) * 2 * SEG
    return slice(start, start + 2 * SEG)


def block(ref, j):
    return ref[j].reshape(D, D)


def row(ref, *idx):
    if isinstance(ref, tuple):
        return row(ref[idx[0] // 6], idx[0] % 3, idx[0] // 3 % 2)
    i = idx[-1]
    return ref[idx[:-1] + (slice(i, i + 1), slice(None))].astype(F32)


class Copies:
    def __init__(self, sems):
        self.sems, self.all = sems, []

    def start(self, src, dst):
        copy = pltpu.make_async_copy(src, dst, self.sems.at[len(self.all)])
        copy.start()
        self.all.append(copy)
        return copy


def cls_chain(
    own, other, counts, wq, w1, w2, par, an, mb, embed, cols_o, wide_o, small_o
):
    section = lax.axis_index("section")
    per_micro = lax.axis_size("section") // MICRO
    half = lax.rem(section, per_micro)
    micro = section // per_micro
    ends = [counts[micro, 0], counts[micro, 0] + counts[micro, 1]]

    def layout(shape, axis):
        r = lax.broadcasted_iota(jnp.int32, shape, axis)
        seg = jnp.where(r < 8, r, r - 2)
        valid = (r < 6) | ((r >= 8) & (r < 14))
        doc = jnp.where(seg >= ends[0], 1, 0) + jnp.where(seg >= ends[1], 1, 0)
        start = jnp.where(doc == 0, 0, jnp.where(doc == 1, ends[0], ends[1]))
        pos = jnp.where(valid, seg - start, -1)
        return jnp.where(valid, doc, jnp.where(r < 16, 100 + r, -1)), pos, valid

    def order(a, b):
        first = half == 0
        return jnp.concatenate([jnp.where(first, a, b), jnp.where(first, b, a)], axis=0)

    def mine(v):
        return jnp.where(half == 0, v[:8], v[8:])

    doc_q, pos, valid = layout((16, 128), 0)
    doc_k, _, _ = layout((16, 128), 1)
    allowed = jnp.concatenate([doc_q == doc_k] * HEADS, axis=0)
    lanes8 = lax.broadcasted_iota(jnp.int32, (16, 8), 1)
    onehot = (pos[:, :8] == lanes8).astype(BF)
    leaders = order(own[0], other[0]) + dot(onehot, embed[...])
    low = leaders.astype(BF)
    lane = lax.broadcasted_iota(jnp.int32, (16, D), 1) // HEAD

    def stack(v):
        return jnp.concatenate([jnp.where(lane == h, v, jnp.zeros_like(v)) for h in range(HEADS)], 0)

    def unstack(v):
        total = jnp.where(lane == 0, v[:16], 0.0)
        for h in range(1, HEADS):
            total = total + jnp.where(lane == h, v[h * 16 : (h + 1) * 16], 0.0)
        return total

    def deep(v):
        return jnp.concatenate([v, jnp.zeros((112, D), BF)], axis=0)

    q = (dot(low, block(wq, 0)) + row(par, 3)).astype(BF)
    k = dot(low, block(wq, 1)).astype(BF)
    v = (dot(low, block(wq, 2)) + row(par, 4)).astype(BF)
    qs, kd, vd = stack(q), deep(k), deep(v)
    scores = jnp.where(allowed, dot_nt(qs, kd) * 0.125, MASKED)
    e = jnp.exp(scores - jnp.max(scores, axis=-1, keepdims=True))
    probs = e / jnp.sum(e, axis=-1, keepdims=True)
    probs_low = probs.astype(BF)
    ctx = unstack(dot(probs_low, vd)).astype(BF)
    n1, rs1 = norm_rows(leaders + dot(ctx, block(wq, 3)) + row(par, 5))
    third = (n1 * row(an, 1, 0) + row(an, 1, 1)).astype(BF)
    act, gp, v = [], [], third.astype(F32) + row(par, 9)
    for j in range(4):
        a, g = gelu_parts(dot(third, block(w1, j)) + mb[1:2, j * D : (j + 1) * D].astype(F32))
        act.append(a.astype(BF))
        gp.append(g)
        v = v + dot_nt(act[j], block(w2, j))
    n2, rs2 = norm_rows(v)
    fourth = mine(n2 * row(par, 10) + row(par, 11))

    dy = order(own[1], other[1])
    small_o[22] = jnp.sum(mine(dy * n2), axis=0, keepdims=True)
    small_o[23] = jnp.sum(mine(dy), axis=0, keepdims=True)
    dr = norm_back(dy, n2, rs2, row(par, 10))
    dbf = dr.astype(BF)
    small_o[21] = jnp.sum(mine(dbf.astype(F32)), axis=0, keepdims=True)
    dthird = dr
    for j in range(4):
        dh = (dot(dbf, block(w2, j)) * gp[j]).astype(BF)
        dh_mine = mine(dh.astype(F32))
        small_o[17 + j] = jnp.sum(dh_mine, axis=0, keepdims=True)
        cols_o[0, :, j * D : (j + 1) * D] = dh
        cols_o[1, :, j * D : (j + 1) * D] = act[j]
        dthird = dthird + dot_nt(dh, block(w1, j))
    dthird = dthird.astype(BF).astype(F32)
    small_o[15] = jnp.sum(mine(dthird * n1), axis=0, keepdims=True)
    small_o[16] = jnp.sum(mine(dthird), axis=0, keepdims=True)
    dr = norm_back(dthird, n1, rs1, row(an, 1, 0))
    dba = dr.astype(BF)
    small_o[14] = jnp.sum(mine(dba.astype(F32)), axis=0, keepdims=True)
    dctx = stack(dot_nt(dba, block(wq, 3)).astype(BF))
    dp = dot_nt(dctx, vd)
    dv = dot_tn(probs_low, dctx)[:16].astype(BF)
    ds = (probs * (dp - jnp.sum(dp * probs, axis=-1, keepdims=True))).astype(BF)
    dq = (unstack(dot(ds, kd)) * 0.125).astype(BF)
    dk = (dot_tn(ds, qs)[:16] * 0.125).astype(BF)
    small_o[12] = jnp.sum(mine(dq.astype(F32)), axis=0, keepdims=True)
    small_o[13] = jnp.sum(mine(dv.astype(F32)), axis=0, keepdims=True)
    dlead = dr
    for j, piece in enumerate((dq, dk, dv)):
        dlead = dlead + dot_nt(piece, block(wq, j))
    dlead_mine = mine(dlead)
    pos_mine = jnp.where(half == 0, pos[:8], pos[8:])
    for i in range(8):
        hit = jnp.where(pos_mine[:, 0:1] == i, dlead_mine, 0.0)
        small_o[24 + i] = jnp.sum(hit, axis=0, keepdims=True)
    for j, piece in enumerate((dq, dk, dv, dba)):
        cols_o[2, :, j * D : (j + 1) * D] = piece
    for j, piece in enumerate((third, dbf, low, ctx)):
        wide_o[j] = piece
    return fourth, dlead_mine


class Place:
    def __init__(self):
        self.dp, self.section = lax.axis_index("dp"), lax.axis_index("section")
        self.n_dp, self.n_section = lax.axis_size("dp"), lax.axis_size("section")
        self.nz = self.n_dp // 2
        self.z, self.x = self.dp // 2, lax.rem(self.dp, 2)
        self.y, self.c = self.section // 2, lax.rem(self.section, 2)

    def at(self, dz=0, x=None, y=None, c=None):
        x = self.x if x is None else x
        y = self.y if y is None else y
        c = self.c if c is None else c
        return ((self.z + dz) * 2 + x, y * 2 + c)

    def to_x(self):
        return self.at(x=1 - self.x)

    def to_y(self):
        return self.at(y=1 - self.y)

    def to_c(self):
        return self.at(c=1 - self.c)

    def device(self, index):
        return (index // self.n_section, lax.rem(index, self.n_section))


class Links:
    def __init__(self, sends, recvs):
        self.sends, self.recvs, self.used = sends, recvs, 0

    def copy(self, src, dst, peer, recv=None):
        i = self.used
        self.used += 1
        return pltpu.make_async_remote_copy(
            src_ref=src, dst_ref=dst, send_sem=self.sends.at[i], recv_sem=self.recvs.at[i] if recv is None else recv,
            device_id=peer, device_id_type=MESH,
        )


HALF, THIRD = D // 2, D // 3


class Scatter:
    def __init__(self, me, links, held, core, xa, yb, ya, xb, zb, zc, z_recv, c_recv, j):
        self.me, self.held, self.j, self.paired = me, held, j, zc is not None
        self.core, self.xa, self.yb, self.ya, self.xb = core, xa, yb, ya, xb
        x, y, c = me.x, me.y, me.c
        wide = THIRD if self.paired else HALF

        def span(start, size):
            return pl.ds(start, size), slice(start, start + size)

        (a, self.a), (b, self.b) = span(0, wide), span(wide, wide)
        w, self.w = span(0, wide)
        self.core_copy = links.copy(held.at[j, :, :, 1 - c], core.at[j], me.to_c())
        self.xa_copy = links.copy(held.at[j, 1 - x, :, c, :, a], xa.at[j, :, :, w], me.to_x())
        self.yb_copy = links.copy(held.at[j, :, 1 - y, c, :, b], yb.at[j, :, :, w], me.to_y())
        self.ya_copy = links.copy(held.at[j, x, 1 - y, c, :, a], ya.at[j, :, w], me.to_y())
        self.xb_copy = links.copy(held.at[j, 1 - x, y, c, :, b], xb.at[j, :, w], me.to_x())
        target = (j * 2 + x, me.section)
        ab = pl.ds(0, 2 * wide)
        self.z_copy = links.copy(held.at[j, x, y, c, :, ab], zb.at[me.z, :, ab], target, z_recv.at[me.z])
        if not self.paired:
            return
        self.holds = lax.rem(me.z, 2) == j % 2
        self.zc = zc.at[j // 2]
        cc, self.cc = span(2 * THIRD, THIRD)
        (p, self.p), (q, self.q) = span(2 * THIRD, THIRD // 2), span(2 * THIRD + THIRD // 2, THIRD // 2)
        v, self.v = span(THIRD, THIRD // 2)
        self.zc_copy = links.copy(held.at[j, :, :, c, :, cc], self.zc, me.at(dz=1 - 2 * lax.rem(me.z, 2)))
        self.xp_copy = links.copy(held.at[j, 1 - x, :, c, :, p], xa.at[j, :, :, v], me.to_x())
        self.yq_copy = links.copy(held.at[j, :, 1 - y, c, :, q], yb.at[j, :, :, v], me.to_y())
        self.yp_copy = links.copy(held.at[j, x, 1 - y, c, :, p], ya.at[j, :, v], me.to_y())
        self.xq_copy = links.copy(held.at[j, 1 - x, y, c, :, q], xb.at[j, :, v], me.to_x())
        self.zz_copy = links.copy(held.at[j, x, y, c, :, cc], zb.at[me.z, :, cc], target, c_recv)

    def add(self, x, y, cols, value):
        j, c = self.j, self.me.c
        self.held[j, x, y, c, :, cols] = self.held[j, x, y, c, :, cols] + value

    def start(self):
        self.core_copy.start()

    def first(self):
        j, x, y, core = self.j, self.me.x, self.me.y, self.core
        self.core_copy.wait_recv()
        for i in range(2):
            self.add(1 - x, i, self.a, core[j, 1 - x, i, :, self.a])
        self.xa_copy.start()
        for i in range(2):
            self.add(i, 1 - y, self.b, core[j, i, 1 - y, :, self.b])
        self.yb_copy.start()
        if self.paired:
            for i in range(4):
                self.add(i // 2, i % 2, self.cc, core[j, i // 2, i % 2, :, self.cc])

            @pl.when(jnp.logical_not(self.holds))
            def _():
                self.zc_copy.start()

        for i in range(2):
            self.add(x, i, self.a, core[j, x, i, :, self.a])
            self.add(i, y, self.b, core[j, i, y, :, self.b])

    def second(self):
        j, x, y = self.j, self.me.x, self.me.y
        self.xa_copy.wait_recv()
        self.add(x, 1 - y, self.a, self.xa[j, 1 - y, :, self.w])
        self.ya_copy.start()
        self.yb_copy.wait_recv()
        self.add(1 - x, y, self.b, self.yb[j, 1 - x, :, self.w])
        self.xb_copy.start()
        self.add(x, y, self.a, self.xa[j, y, :, self.w])
        self.add(x, y, self.b, self.yb[j, x, :, self.w])

    def third(self):
        j, x, y = self.j, self.me.x, self.me.y
        self.ya_copy.wait_recv()
        self.xb_copy.wait_recv()
        self.add(x, y, self.a, self.ya[j, :, self.w])
        self.add(x, y, self.b, self.xb[j, :, self.w])

        @pl.when(self.me.z != j)
        def _():
            self.z_copy.start()

    def pair_first(self):
        x, y = self.me.x, self.me.y

        @pl.when(self.holds)
        def _():
            self.zc_copy.wait_recv()
            for i in range(2):
                self.add(1 - x, i, self.p, self.zc[1 - x, i, :, 0 : THIRD // 2])
            self.xp_copy.start()
            for i in range(2):
                self.add(i, 1 - y, self.q, self.zc[i, 1 - y, :, THIRD // 2 :])
            self.yq_copy.start()
            for i in range(2):
                self.add(x, i, self.p, self.zc[x, i, :, 0 : THIRD // 2])
                self.add(i, y, self.q, self.zc[i, y, :, THIRD // 2 :])

    def pair_second(self):
        j, x, y = self.j, self.me.x, self.me.y

        @pl.when(self.holds)
        def _():
            self.xp_copy.wait_recv()
            self.add(x, 1 - y, self.p, self.xa[j, 1 - y, :, self.v])
            self.yp_copy.start()
            self.yq_copy.wait_recv()
            self.add(1 - x, y, self.q, self.yb[j, 1 - x, :, self.v])
            self.xq_copy.start()
            self.add(x, y, self.p, self.xa[j, y, :, self.v])
            self.add(x, y, self.q, self.yb[j, x, :, self.v])

    def pair_third(self):
        j, x, y = self.j, self.me.x, self.me.y

        @pl.when(self.holds)
        def _():
            self.yp_copy.wait_recv()
            self.xq_copy.wait_recv()
            self.add(x, y, self.p, self.ya[j, :, self.v])
            self.add(x, y, self.q, self.xb[j, :, self.v])

            @pl.when(self.me.z != j)
            def _():
                self.zz_copy.start()

    def drain(self):
        for copy in (self.core_copy, self.xa_copy, self.yb_copy, self.ya_copy, self.xb_copy):
            copy.wait_send()

        @pl.when(self.me.z != self.j)
        def _():
            self.z_copy.wait_send()

        if self.paired:

            @pl.when(jnp.logical_not(self.holds))
            def _():
                self.zc_copy.wait_send()

            @pl.when(self.holds)
            def _():
                for copy in (self.xp_copy, self.yq_copy, self.yp_copy, self.xq_copy):
                    copy.wait_send()

                @pl.when(self.me.z != self.j)
                def _():
                    self.zz_copy.wait_send()


class Matrix:
    def __init__(self, me, links, z_recv, c_recv, held, core, xa, yb, ya, xb, zb, zc):
        self.me, self.held, self.zb, self.paired = me, held, zb, zc is not None
        buffers = (core, xa, yb, ya, xb, zb, zc)
        self.units = [Scatter(me, links, held, *buffers, z_recv, c_recv, j) for j in range(me.nz)]
        self.z_recv, self.c_recv = z_recv, c_recv

    def arrival(self, i, cols, sem):
        part = self.zb.at[i, :, cols]
        return pltpu.make_async_remote_copy(
            src_ref=part, dst_ref=part, send_sem=sem, recv_sem=sem,
            device_id=(self.me.dp, self.me.section), device_id_type=MESH,
        )

    def finish(self, total):
        me = self.me
        for unit in self.units:
            unit.drain()
        total[...] = self.held[me.z, me.x, me.y, me.c].astype(F32)
        cols = 2 * THIRD if self.paired else D
        for i in range(me.nz):

            @pl.when(me.z != i)
            def _():
                self.arrival(i, pl.ds(0, cols), self.z_recv.at[i]).wait_recv()
                total[:, 0:cols] += self.zb[i, :, 0:cols].astype(F32)

            if self.paired:

                @pl.when(lax.rem(me.z + 2, me.nz) == i)
                def _():
                    self.arrival(i, pl.ds(cols, THIRD), self.c_recv).wait_recv()
                    total[:, cols:] += self.zb[i, :, cols:].astype(F32)


def scatter_buffers(nz, width):
    shapes = [(nz, 2, 2, width, D)] + [(nz, 2, width, HALF)] * 2 + [(nz, width, HALF)] * 2
    return shapes + [(nz, width, D), (nz // 2, 2, 2, width, THIRD)]


class Gather:
    def __init__(self, me, links, wide, cols, all_wide, all_cols):
        self.me, self.all_wide, self.all_cols = me, all_wide, all_cols
        self.wide, self.cols = wide, cols
        self.span = cols.shape[-1] // me.n_dp
        self.copies = [[], [], []]
        for c in range(2):
            w, k = (pl.ds(0, 2), pl.ds(0, 1)) if c == 0 else (pl.ds(2, 1), pl.ds(1, 2))
            given = [wide.at[me.y, pl.ds(2 * c, 2)], cols.at[me.y, k]]
            self.copies[0].append([links.copy(a, a, me.to_y()) for a in given])
            spread = []
            for i in range(1, me.n_dp):
                peer = lax.rem(me.dp + i, me.n_dp)
                spread.append(links.copy(self.given(c, peer), all_wide.at[me.dp, :, w], (peer, me.section)))
                spread.append(links.copy(self.part(k, peer), all_cols.at[me.dp, :, k], (peer, me.section)))
            self.copies[1].append(spread)
            beside = [all_wide.at[:, :, w], all_cols.at[:, :, k]]
            self.copies[2].append([links.copy(a, a, me.to_c()) for a in beside])

    def given(self, c, peer):
        if c == 0:
            return self.wide.at[:, pl.ds(0, 2)]
        return self.wide.at[:, pl.ds(2 + peer * self.span // (3 * D), 1)]

    def part(self, k, peer):
        return self.cols.at[:, k, :, pl.ds(pl.multiple_of(peer * self.span, 128), self.span)]

    def each(self, do):
        for c in range(2):

            @pl.when(self.me.c == c)
            def _():
                do(c)

    def start(self):
        def go(c):
            for copy in self.copies[0][c]:
                copy.start()

        self.each(go)

    def second(self):
        me = self.me

        def go(c):
            for copy in self.copies[0][c]:
                copy.wait()
            for copy in self.copies[1][c]:
                copy.start()
            w, k = (slice(0, 2), slice(0, 1)) if c == 0 else (slice(2, 3), slice(1, 3))
            self.all_wide[me.dp, :, w] = self.given(c, me.dp)[...]
            self.all_cols[me.dp, :, k] = self.part(pl.ds(k.start, k.stop - k.start), me.dp)[...]

        self.each(go)

    def third(self):
        def go(c):
            for copy in self.copies[1][c]:
                copy.wait()
            for copy in self.copies[2][c]:
                copy.start()

        self.each(go)

    def finish(self):
        def go(c):
            for copy in self.copies[2][c]:
                copy.wait_send()
            for copy in self.copies[2][1 - c]:
                copy.wait_recv()

        self.each(go)


class Total:
    def __init__(self, me, acc, got, out, sems):
        self.me, self.acc, self.got, self.out, self.sems = me, acc, got, out, sems
        self.count = acc.shape[0]
        self.index = me.dp * me.n_section + me.section

    def send(self, phase):
        @pl.loop(1, self.count)
        def _(i):
            peer = lax.rem(self.index + i, self.count)
            src = self.acc.at[peer] if phase == 0 else self.out.at[self.index]
            dst = (self.got if phase == 0 else self.out).at[self.index]
            pltpu.make_async_remote_copy(
                src_ref=src, dst_ref=dst, send_sem=self.sems.at[2 * phase], recv_sem=self.sems.at[2 * phase + 1],
                device_id=self.me.device(peer), device_id_type=MESH,
            ).start()

    def wait(self, phase):
        rows = self.got.at[pl.ds(0, self.count - 1)]
        for i in range(2):
            pltpu.make_async_copy(rows, rows, self.sems.at[2 * phase + i]).wait()

    def step(self, i):
        if i == 0:
            self.got[self.index] = self.acc[self.index]
            self.send(0)
        elif i == 1:
            self.wait(0)
            self.out[self.index] = jnp.sum(self.got[...], axis=0)
            self.send(1)
        else:
            self.wait(1)


def pick_own(me, width):
    def pick(v):
        out = v[:, :width]
        for s in range(1, 4):
            out = jnp.where(me.section == s, v[:, s * width : (s + 1) * width], out)
        return out

    return pick


N_SET = 7
BLOCK_ORDER = (0, 2, 1, 3)
PAIRED = (False, True, True)
QKV_ORDER = (0, 2, 1)
PLAN = {
    "ffnout0": (
        ("g", 0, 0),
    ),
    "dwout0": (
        ("o", 0, 0),
    ),
    "dwout2": (
        ("o", 2, 0),
    ),
    "dwout1": (
        ("o", 1, 0),
        ("o", 0, 1),
    ),
    "dwout3": (
        ("o", 3, 0),
    ),
    "dh0": (
        ("o", 2, 1),
    ),
    "dh2": (
        ("o", 1, 1),
    ),
    "dwin0": (
        ("i", 0, 0),
        ("o", 3, 1),
        ("f", 0, 0),
    ),
    "dwin2": (
        ("i", 2, 0),
        ("o", 0, 2),
    ),
    "dwin1": (
        ("i", 1, 0),
        ("i", 0, 1),
    ),
    "dwin3": (
        ("i", 3, 0),
        ("o", 2, 2),
    ),
    "dfirst0": (
        ("o", 1, 2),
        ("i", 2, 1),
    ),
    "dfirst1": (
        ("o", 0, 4),
        ("o", 1, 4),
        ("g", 1, 0),
        ("o", 0, 3),
        ("o", 3, 2),
    ),
    "dwo": (
        ("f", 0, 1),
        ("a", 3, 0),
        ("i", 0, 2),
    ),
    "dctx": (
        ("g", 2, 0),
        ("o", 2, 4),
        ("o", 3, 4),
        ("o", 2, 3),
        ("o", 1, 3),
        ("i", 1, 1),
        ("i", 3, 1),
        ("i", 2, 2),
    ),
    "att0": (
        ("o", 0, 5),
        ("o", 1, 5),
        ("i", 0, 4),
        ("o", 3, 3),
    ),
    "att1": (
        ("i", 0, 3),
    ),
    "att2": (
        ("o", 2, 5),
        ("o", 3, 5),
        ("a", 3, 1),
    ),
    "att3": (
        ("i", 2, 4),
        ("i", 1, 2),
    ),
    "att5": (
        ("i", 3, 2),
    ),
    "dwqkv0": (
        ("a", 0, 0),
        ("o", 0, 6),
        ("o", 1, 6),
        ("o", 2, 6),
        ("o", 3, 6),
        ("i", 0, 5),
        ("i", 1, 4),
        ("i", 2, 3),
    ),
    "dwqkv2": (
        ("a", 2, 0),
        ("a", 0, 1),
    ),
    "dwqkv1": (
        ("a", 1, 0),
    ),
    "sums": (
        ("s", 0, 0),
        ("i", 2, 5),
        ("i", 3, 4),
        ("i", 1, 3),
        ("i", 3, 3),
        ("i", 0, 6),
        ("a", 3, 2),
    ),
    "dx0": (
        ("i", 1, 5),
        ("a", 2, 1),
    ),
    "dx1": (
        ("a", 0, 2),
    ),
    "tail": (
        ("p", 3, 0),
        ("i", 2, 6),
        ("i", 3, 5),
        ("a", 1, 1),
        ("a", 3, 3),
        ("i", 1, 6),
        ("s", 1, 0),
        ("a", 2, 2),
        ("a", 0, 3),
        ("i", 3, 6),
        ("a", 1, 2),
        ("a", 2, 3),
        ("a", 1, 3),
        ("s", 2, 0),
        ("p", 2, 0),
        ("p", 0, 0),
    ),
}


def cls_grads(wide, cols, put, pick):
    for i, k in enumerate((4, 5, 1)):
        put(k, dot_tn(pick(cols[i]), wide[i]))


class Net:
    def __init__(self, mats, acc, out, wide, cols, grads, scratch):
        sets = [scratch[i * N_SET : (i + 1) * N_SET] for i in range(3)]
        sets[0] = sets[2][:1] + sets[0][1:]
        sets = [part if PAIRED[m] else part[:-1] + (None,) for m, part in enumerate(sets)]
        all_wide, all_cols, got, self.stage, sends, recvs, z_recvs, c_recvs, self.free, self.out_sems, sum_sems = scratch[3 * N_SET :]
        self.outs = []
        self.me, self.grads = Place(), grads
        links = Links(sends, recvs)
        self.attn, self.win, self.wout = [
            Matrix(self.me, links, z_recvs.at[m], c_recvs.at[m], mats[m], *sets[m]) for m in range(3)
        ]
        self.gather = Gather(self.me, links, wide, cols, all_wide, all_cols)
        self.summed = Total(self.me, acc, got, out, sum_sems)

    def slot(self):
        i = len(self.outs)
        if i >= 2:
            self.outs[i - 2].wait()
        return self.stage.at[i % 2]

    def put(self, k):
        i = len(self.outs)
        copy = pltpu.make_async_copy(self.stage.at[i % 2], self.grads.at[k], self.out_sems.at[i % 2])
        copy.start()
        self.outs.append(copy)

    def cls(self):
        self.gather.finish()
        width = self.stage.shape[1]
        rows = 16 * 2 * self.me.n_dp
        wide = [self.gather.all_wide[:, :, i].reshape(rows, D) for i in range(3)]
        cols = [self.gather.all_cols[:, :, i].reshape(rows, 4 * width) for i in range(3)]

        def put(k, value):
            self.slot()[...] = value
            self.put(k)

        cls_grads(wide, cols, put, pick_own(self.me, width))

    def place(self, which, k):
        which.finish(self.slot())
        self.put(k)

    def after(self, name):
        kinds = {"a": self.attn.units, "i": self.win.units, "o": self.wout.units}
        for step in PLAN.get(name, ()):
            kind, number, phase = step
            if kind == "g":
                (self.gather.second, self.gather.third, self.cls)[number]()
            elif kind == "s":
                self.summed.step(number)
            elif kind == "p":
                self.place((self.attn, None, self.win, self.wout)[number], number)
            elif kind == "f":
                if phase == 0:
                    pl.semaphore_signal(self.free, inc=1, device_id=self.me.to_c(), device_id_type=MESH)
                else:
                    pl.semaphore_wait(self.free, 1)
            else:
                unit = kinds[kind][number]
                parts = (unit.start, unit.first, unit.second, unit.third)
                (parts + (unit.pair_first, unit.pair_second, unit.pair_third))[phase]()


def layer_kernel(fused, x_i, cot, counts, ab, ms, an, mb, embed, aw, mw, enc_o, dx_o, small_o, *refs):
    par = (ab, ms)
    if fused:
        grads_o, refs = refs[0], refs[1:]
    else:
        dw_o, refs = refs[0], refs[1:]
    cols, wide, a0, win0, wout0, a1, v1, v2, first, n1, db, x, rs1, qkv, p, ctx = refs[:16]
    heads, rows16, mine, theirs, sums, wsem, osem, ssem, rsem = refs[16:25]
    act, gp, dwout = v1, v2, a1
    mats = (gp, act, dwout)
    loads = Copies(wsem)

    def load(src, dst):
        return [loads.start(src.at[:, :, :, :, j * D : (j + 1) * D], dst.at[j]) for j in range(4)]

    x_in = loads.start(x_i, x)
    a0_in = load(aw.at[0], a0)
    heads_in = [loads.start(cot.at[pl.ds(g * SEG, 16)], heads.at[g]) for g in range(OWN)]
    win0_in, wout0_in = load(mw.at[0, 0], win0), load(mw.at[0, 1], wout0)
    cls_in = load(aw.at[1], a1) + load(mw.at[1, 0], v1) + load(mw.at[1, 1], v2)
    cot_in = loads.start(cot, db)

    section = lax.axis_index("section")
    partner = (lax.axis_index("dp"), section + 1 - 2 * lax.rem(section, 2))
    barrier = pltpu.get_barrier_semaphore()
    if fused:
        small, refs = refs[25], refs[:25] + refs[26:]
        net = Net(mats, small, small_o, wide, cols, grads_o, refs[25:])
        expected = net.me.n_dp * net.me.n_section - 1

        @pl.loop(1, expected + 1)
        def _(i):
            peer = net.me.device(lax.rem(net.summed.index + i, expected + 1))
            pl.semaphore_signal(barrier, inc=1, device_id=peer, device_id_type=MESH)
    else:
        small, expected = small_o, 1
        pl.semaphore_signal(barrier, inc=1, device_id=partner, device_id_type=MESH)

    def after(name):
        if fused:
            net.after(name)

    swaps = [
        pltpu.make_async_remote_copy(
            src_ref=mine.at[i], dst_ref=theirs.at[i], send_sem=ssem.at[i], recv_sem=rsem.at[i],
            device_id=partner, device_id_type=MESH,
        )
        for i in range(2)
    ]

    x_in.wait()
    for j in range(3):
        a0_in[j].wait()
        v = dot(x[...], block(a0, j))
        if j != 1:
            v = v + row(par, j // 2)
        qkv[:, j * D : (j + 1) * D] = v.astype(BF)
    for g, h in itertools.product(range(OWN), range(PAIRS)):
        rows, c = slice(g * SEG, (g + 1) * SEG), slice(h * 128, (h + 1) * 128)
        q = qkv[rows, c] * jnp.asarray(0.125, BF)
        kc = halves(qkv[rows, D + h * 128 : D + (h + 1) * 128])
        vc = halves(qkv[rows, 2 * D + h * 128 : 2 * D + (h + 1) * 128])
        scores = dot_nt(kc, q)
        ps = []
        for i in range(2):
            si = scores[i * SEG : (i + 1) * SEG]
            e = jnp.exp(si - jnp.max(si, axis=0, keepdims=True))
            ps.append((e / jnp.sum(e, axis=0, keepdims=True)).astype(BF))
        pt = jnp.concatenate(ps, axis=0)
        p[pair_rows(g, h), :] = pt
        ctx[rows, c] = dot_tn(pt, vc).astype(BF)

    mine[...] = jnp.zeros_like(mine)
    rows16[...] = jnp.zeros_like(rows16)
    for copy in heads_in:
        copy.wait()
    for g in range(OWN):
        mine[1, g : g + 1, :] = heads[g, 0:1, :].astype(F32)
        rows16[0, g : g + 1, :] = x[g * SEG : g * SEG + 1, :].astype(F32)
        rows16[1, g : g + 1, :] = ctx[g * SEG : g * SEG + 1, :].astype(F32)
    pl.semaphore_wait(barrier, expected)
    swaps[1].start()
    a0_in[3].wait()
    n, _ = norm_rows(rows16[0] + dot(rows16[1].astype(BF), block(a0, 3)) + row(par, 2))
    low = (n * row(an, 0, 0) + row(an, 0, 1)).astype(BF)
    v = low.astype(F32) + row(par, 6)
    for j in range(4):
        win0_in[j].wait()
        wout0_in[j].wait()
        a, _ = gelu_parts(dot(low, block(win0, j)) + mb[0:1, j * D : (j + 1) * D].astype(F32))
        v = v + dot_nt(a.astype(BF), block(wout0, j))
    n, _ = norm_rows(v)
    value = (n * row(par, 7) + row(par, 8)).astype(BF).astype(F32)
    mine[0] = jnp.where(lax.broadcasted_iota(jnp.int32, (8, D), 0) < OWN, value[:8], 0.0)
    swaps[0].start()

    for half in range(2):
        rows = slice(half * 384, half * 384 + 384)
        v = dot(ctx[rows, :], block(a0, 3)) + x[rows, :].astype(F32) + row(par, 2)
        n, rs = norm_rows(v)
        n1[rows, :] = n.astype(BF)
        rs1[rows, :] = rs
        first[rows, :] = (n * row(an, 0, 0) + row(an, 0, 1)).astype(BF)
    for copy in cls_in:
        copy.wait()
    for swap in swaps:
        swap.wait()
    if fused:
        cols_o, wide_o = cols.at[net.me.y], wide.at[net.me.y]
    else:
        cols_o, wide_o = cols, wide
    fourth, dlead = cls_chain(mine, theirs, counts, a1, v1, v2, par, an, mb, embed, cols_o, wide_o, small)
    lead = dlead.astype(BF).astype(F32)

    for j in range(4):
        a, g = gelu_parts(dot(first[...], block(win0, j)) + mb[0:1, j * D : (j + 1) * D].astype(F32))
        act[j] = a.astype(BF).reshape(BLOCKS[1:])
        gp[j] = g.astype(BF).reshape(BLOCKS[1:])
        if fused and j == 0:
            net.gather.start()
        after(f"ffnin{j}")

    def norm_step(rows, dy, n, rs, gain, at):
        low = norm_back(dy, n, rs, gain).astype(BF)
        db[rows, :] = low
        for i, v in enumerate((low.astype(F32), dy * n, dy)):
            sums[at + i] = fold8(v) if rows.start == 0 else sums[at + i] + fold8(v)

    def put(ref, j, value):
        ref[j] = value.astype(BF).reshape(BLOCKS[1:])

    cot_in.wait()
    at = lax.broadcasted_iota(jnp.int32, (384, D), 0)
    for half in range(2):
        rows = slice(half * 384, half * 384 + 384)
        v = first[rows, :].astype(F32) + row(par, 6)
        for j in range(4):
            v = v + dot_nt(act[j, half].reshape(384, D), block(wout0, j))
        n, rs = norm_rows(v)
        value, dy = n * row(par, 7) + row(par, 8), db[rows, :].astype(F32)
        for g in range(3):
            value = jnp.where(at == g * SEG, fourth[3 * half + g : 3 * half + g + 1], value)
            dy = jnp.where(at == g * SEG, lead[3 * half + g : 3 * half + g + 1], dy)
        dwout[2, half] = value.astype(BF).reshape(BLOCKS[2:])
        norm_step(rows, dy, n, rs, row(par, 7), 0)
        after(f"ffnout{half}")
    enc_out = pltpu.make_async_copy(dwout.at[2], enc_o, osem.at[0])
    enc_out.start()

    for j in BLOCK_ORDER:
        if j == 2:
            enc_out.wait()
        put(dwout, j, dot_tn(block(act, j), db[...]))
        after(f"dwout{j}")
    for j in range(4):
        low = (dot(db[...], block(wout0, j)) * block(gp, j).astype(F32)).astype(BF)
        put(gp, j, low)
        sums[6 + j] = fold8(low.astype(F32))
        after(f"dh{j}")
    for j in BLOCK_ORDER:
        put(act, j, dot_tn(block(gp, j), first[...]))
        after(f"dwin{j}")
    for half in range(2):
        rows = slice(half * 384, half * 384 + 384)
        v = db[rows, :].astype(F32)
        for j in range(4):
            v = v + dot_nt(gp[j, half].reshape(384, D), block(win0, j))
        norm_step(rows, v.astype(BF).astype(F32), n1[rows, :].astype(F32), rs1[rows, :], row(an, 0, 0), 3)
        after(f"dfirst{half}")

    put(gp, 3, dot_tn(db[...], ctx[...]))
    after("dwo")
    dctx = first
    dctx[...] = dot_nt(db[...], block(a0, 3)).astype(BF)
    after("dctx")

    def attention(g):
        rows = slice(g * SEG, (g + 1) * SEG)
        for h in range(PAIRS):
            cq = slice(h * 128, (h + 1) * 128)
            ck = slice(D + h * 128, D + (h + 1) * 128)
            cv = slice(2 * D + h * 128, 2 * D + (h + 1) * 128)
            q, dc, pt = qkv[rows, cq], dctx[rows, cq], p[pair_rows(g, h), :]
            kc, vc = halves(qkv[rows, ck]), halves(qkv[rows, cv])
            dp, pf = dot_nt(vc, dc), pt.astype(F32)
            ds = []
            for i in range(2):
                pi, di = pf[i * SEG : (i + 1) * SEG], dp[i * SEG : (i + 1) * SEG]
                ds.append((pi * (di - jnp.sum(pi * di, axis=0, keepdims=True))).astype(BF))
            ds = jnp.concatenate(ds, axis=0)
            qkv[rows, cq] = (dot_tn(ds, kc) * 0.125).astype(BF)
            qkv[rows, ck] = (unhalve(dot(ds, q)) * 0.125).astype(BF)
            qkv[rows, cv] = unhalve(dot(pt, dc)).astype(BF)

    for g in range(OWN):
        attention(g)
        after(f"att{g}")
    for j in QKV_ORDER:
        s = slice(j * D, (j + 1) * D)
        put(gp, j, dot_tn(qkv[:, s], x[...]))
        if j != 1:
            sums[10 + j // 2] = fold8(qkv[:, s].astype(F32))
        after(f"dwqkv{j}")
    for i, k in enumerate((10, 11, 3, 4, 5, 6, 7, 8, 9, 0, 1, 2)):
        small[i] = jnp.sum(sums[k], axis=0, keepdims=True)
    after("sums")
    if not fused:
        outs = [pltpu.make_async_copy(mats[i], dw_o.at[i], osem.at[1 + i]) for i in range(3)]
        for copy in outs:
            copy.start()
    for half in range(2):
        rows = slice(half * 384, half * 384 + 384)
        v = db[rows, :].astype(F32)
        for j in range(3):
            v = v + dot_nt(qkv[rows, j * D : (j + 1) * D], block(a0, j))
        db[rows, :] = v.astype(BF)
        after(f"dx{half}")
    dx_out = pltpu.make_async_copy(db, dx_o, osem.at[0])
    dx_out.start()
    if not fused:
        for copy in outs + [dx_out]:
            copy.wait()
        return
    after("tail")
    dx_out.wait()
    for copy in net.outs[-2:]:
        copy.wait()


def layer(fused, n_dp, *args):
    width = FF // (4 * n_dp)
    outs = [(BLOCKS[1:], BF), ((ROWS, D), BF), ((32, 1, D), F32)]
    blocks = [((3, 16, FF), BF), ((4, 16, D), BF)]
    buffers = [(BLOCKS, BF)] * 6 + [((ROWS, D), BF)] * 4
    buffers += [((ROWS, 1), F32), ((ROWS, 3 * D), BF), ((OWN * PAIRS * 2 * SEG, SEG), BF), ((ROWS, D), BF)]
    buffers += [((OWN, 16, D), BF), ((2, 16, D), F32), ((2, 8, D), F32), ((2, 8, D), F32), ((12, 8, D), F32)]
    sems = [32, 4, 2, 2]
    vmem, extra = [pltpu.VMEM(*b) for b in buffers], []
    vmem += [pltpu.SemaphoreType.DMA((n,)) for n in sems]
    if fused:
        outs += [((6, width, D), F32)]
        out_specs = [ANY, ANY, VM, ANY]
        vmem = [pltpu.VMEM((2,) + shape, dt) for shape, dt in blocks] + vmem
        count = (6 * 3 + 6 * 2) * (n_dp // 2) + 4 * (n_dp - 1) + 8
        parts = [pltpu.VMEM(s, BF) for s in scatter_buffers(n_dp // 2, width)]
        extra = [pltpu.VMEM((32, 1, D), F32), pltpu.VMEM((16, 128), BF)] + parts[1:-1]
        extra += [pltpu.VMEM((16, 128), BF)] + parts * 2
        extra += [
            pltpu.VMEM((n_dp, 2, 3, 16, D), BF),
            pltpu.VMEM((n_dp, 2, 3, 16, 4 * width), BF),
            pltpu.VMEM((32, 1, D), F32),
            pltpu.VMEM((2, width, D), F32),
            pltpu.SemaphoreType.DMA((count,)),
            pltpu.SemaphoreType.DMA((count,)),
            pltpu.SemaphoreType.DMA((3, n_dp // 2)),
            pltpu.SemaphoreType.DMA((3,)),
            pltpu.SemaphoreType.REGULAR,
            pltpu.SemaphoreType.DMA((2,)),
            pltpu.SemaphoreType.DMA((4,)),
        ]
    else:
        outs += [((3,) + BLOCKS, BF)] + blocks
        out_specs = [ANY, ANY, VM, ANY, VM, VM]
    return pl.pallas_call(
        functools.partial(layer_kernel, fused),
        out_shape=[jax.ShapeDtypeStruct(*s) for s in outs],
        in_specs=[ANY, ANY, SM, VM, VM, VM, VM, VM, ANY, ANY],
        out_specs=out_specs,
        scratch_shapes=vmem + extra,
        compiler_params=pltpu.CompilerParams(
            vmem_limit_bytes=63 * 2**20, collective_id=0 if fused else 1, has_side_effects=True
        ),
    )(*args)


def place_kernel(red, cols, wide, grads):
    width = red.shape[1]
    me = lax.axis_index("dp") * lax.axis_size("section") + lax.axis_index("section")
    last = jnp.where(me * width >= 3 * D, wide[3].astype(F32), wide[2].astype(F32)).astype(BF)
    for i, k in enumerate((0, 2, 3)):
        grads[k] = red[i].astype(F32)

    def put(k, value):
        grads[k] = value

    cls_grads([wide[0], wide[1], last], cols, put, lambda v: v)


def place(red, cols, wide):
    return pl.pallas_call(
        place_kernel,
        out_shape=jax.ShapeDtypeStruct((6,) + red.shape[1:], F32),
        in_specs=[VM] * 3,
        out_specs=VM,
        compiler_params=pltpu.CompilerParams(vmem_limit_bytes=56 * 2**20),
    )(red, cols, wide)


def finish_kernel(grads, small, ga, gm, ab, an, mb, ms, embed, grads_v, sems):
    loads, stores = Copies(sems.at[0]), Copies(sems.at[1])
    pieces = [(grads.at[i], grads_v.at[i], ga.at[i] if i < 2 else gm.at[i - 2]) for i in range(6)]
    for src, dst, _ in pieces:
        loads.start(src, dst)
    for k in range(2):
        at = 12 * k
        for i in range(3):
            ab[i, k : k + 1, :] = small[at + i]
            ms[i, k : k + 1, :] = small[at + 9 + i]
        for i in range(2):
            an[k, i : i + 1, :] = small[at + 3 + i]
        for j in range(4):
            mb[k : k + 1, j * D : (j + 1) * D] = small[at + 5 + j]
    for i in range(8):
        embed[i : i + 1, :] = small[24 + i]
    for copy, (_, src, dst) in zip(loads.all, pieces):
        copy.wait()
        stores.start(src, dst)
    for copy in stores.all:
        copy.wait()


def finish(grads, small):
    width = grads.shape[1]
    shapes = [(2, width, D), (4, width, D), (3, 2, D), (2, 2, D), (2, FF), (3, 2, D), (8, D)]
    outs = [jax.ShapeDtypeStruct(s, F32) for s in shapes]
    return pl.pallas_call(
        finish_kernel,
        out_shape=outs,
        in_specs=[ANY, VM],
        out_specs=[ANY] * 2 + [VM] * 5,
        scratch_shapes=[
            pltpu.VMEM(grads.shape, F32),
            pltpu.SemaphoreType.DMA((2, 6)),
        ],
    )(grads, small)


def on_device(tokens, counts, aw, ab, an, mw, mb, ms, embed, cot):
    n_dp, n_section = lax.axis_size("dp"), lax.axis_size("section")
    ab, ms = ab.swapaxes(0, 1), ms.swapaxes(0, 1)
    aw, mw = aw.reshape((2,) + BLOCKS[1:5] + (4 * D,)), mw.reshape((2, 2) + BLOCKS[1:5] + (FF,))
    fused = (n_dp // 2, 2, 2, 2, FF // (n_dp * n_section), D) == BLOCKS and n_section == 4
    result = layer(fused, n_dp, tokens, cot, counts, ab, ms, an, mb, embed, aw, mw)
    if fused:
        encoded, dx, small, grads = result
    else:
        encoded, dx, small, dw, cols, wide = result
        own = jnp.arange(16) // 8 == lax.axis_index("section") % 2
        cols = jnp.where(own[None, :, None], cols, jnp.zeros_like(cols))
        cols = lax.all_to_all(cols, BOTH, split_axis=2, concat_axis=1, tiled=True)
        wide = lax.all_gather(wide, BOTH, axis=1, tiled=True)
        red = lax.psum_scatter(dw.reshape(3, FF, D), BOTH, scatter_dimension=1, tiled=True)
        small = lax.psum(small, BOTH)
        grads = place(red, cols, wide)
    ga, gm, g_ab, g_an, g_mb, g_ms, g_embed = finish(grads, small)
    gm = gm.reshape((2, 2) + gm.shape[1:])
    return (
        encoded.reshape(ROWS, D),
        dx,
        ga.swapaxes(1, 2),
        g_ab.swapaxes(0, 1),
        g_an,
        gm.swapaxes(2, 3),
        g_mb,
        g_ms.swapaxes(0, 1),
        g_embed,
    )


def solution(mesh):
    return jax.shard_map(
        on_device,
        mesh=mesh,
        in_specs=(P(BOTH, None), P("dp", None)) + (P(),) * 7 + (P(BOTH, None),),
        out_specs=(
            P(BOTH, None),
            P(BOTH, None),
            P(None, None, BOTH),
            P(),
            P(),
            P(None, None, None, BOTH),
            P(),
            P(),
            P(),
        ),
        check_vma=False,
    )
```
